32 devices in a mesh: dp: 16 (over z, y, x), mp: 2 (over core).
Axes of the slice: x: 2, y: 2, z: 4, core: 2. Of those that a mesh axis runs over, the one named last changes fastest.
Arguments:
- inputs: bfloat16 [4, 2048, 2048], P(None, 'dp'), may hold values from -6 to 6
- doc_spans: int32 [4, 2], replicated, may hold values from 32 to 2016, as said below
- doc_lengths: int32 [4, 2], replicated, may hold values from 1 to 2016, as said below
- state_in: float32 [4, 2, 2560], P(None, None, 'mp'), may hold values from -6 to 6
- conv_in: bfloat16 [4, 2, 3, 2560], P(None, None, None, 'mp'), may hold values from -6 to 6
- norm_gains: bfloat16 [2, 2048], P(None, 'dp'), may hold values from 0.5 to 1.5
- w_x: bfloat16 [2048, 2560], P('dp', 'mp'), may hold values from -0.125 to 0.125
- w_g: bfloat16 [2048, 2560], P('dp', 'mp'), may hold values from -0.125 to 0.125
- rec_params: bfloat16 [2, 1280, 8], P('mp', 'dp')
- gate_weights: bfloat16 [2, 1280, 320], P('mp', 'dp'), may hold values from -0.5 to 0.5
- w_o: bfloat16 [2560, 2048], P('mp', 'dp'), may hold values from -0.125 to 0.125
- w_gate: bfloat16 [2048, 6144], P('dp', 'mp'), may hold values from -0.125 to 0.125
- w_up: bfloat16 [2048, 6144], P('dp', 'mp'), may hold values from -0.125 to 0.125
- w_down: bfloat16 [6144, 2048], P('mp', 'dp'), may hold values from -0.078125 to 0.078125
- cotangent: bfloat16 [4, 2048, 2048], P(None, 'dp'), may hold values from -6 to 6
Outputs:
- output: bfloat16 [4, 2048, 2048], P(None, 'dp')
- input_grad: bfloat16 [4, 2048, 2048], P(None, 'dp')
- final_state: float32 [4, 2, 2, 1280], P(None, None, 'mp', 'dp')
- final_conv: bfloat16 [4, 2, 3, 2, 1280], P(None, None, None, 'mp', 'dp')
- grad_gains: float32 [2, 2048], P(None, 'dp')
- grad_w_x: float32 [2048, 2560], P('dp', 'mp')
- grad_w_g: float32 [2048, 2560], P('dp', 'mp')
- grad_rec_params: float32 [2, 1280, 8], P('mp', 'dp')
- grad_gate_weights: float32 [2, 1280, 320], P('mp', 'dp')
- grad_w_o: float32 [2560, 2048], P('mp', 'dp')
- grad_w_gate: float32 [2048, 6144], P('dp', 'mp')
- grad_w_up: float32 [2048, 6144], P('dp', 'mp')
- grad_w_down: float32 [6144, 2048], P('mp', 'dp')
The draws below stay inside these ranges and needn't reach their ends.
Inputs may be any that keep to these rules, and one draw needn't show every extreme that they name: Each stream is cut into two documents: the first takes doc_spans[s, 0] positions from the start, the second the remaining doc_spans[s, 1]; the two sum to 2048. Document d of stream s has doc_lengths[s, d] real tokens at the start of its positions, then padding; doc_lengths[s, d] <= doc_spans[s, d].
All inputs are finite; a program needn't handle non-finite values.
Results may differ from the reference program's by a relative error of at most 0.013.
Values may be sent and summed in bfloat16 or wider, within the bound.
A program may use at most 320 MiB of HBM per device.

```python
import jax
import jax.numpy as jnp
from jax import lax

D = 2048
RWIDTH = 2560
HEADS = 16
FF = 6144
CONV = 4
DOCS = 2
ROWS = 128
STREAMS = 4
HEAD_DIM = 160
LEN = 2048
N_MP = 2


def doc_tables(key):
    key = jax.random.fold_in(key, 5)
    subkeys = jax.random.split(key, 4)
    quarter_rows = max(ROWS // 4, 1)
    first_span = jax.random.randint(subkeys[0], (STREAMS,), LEN // 4, 3 * LEN // 4 + 1)
    chosen = jax.random.randint(subkeys[1], (), 0, STREAMS)
    longest = LEN - quarter_rows
    is_chosen = jnp.arange(STREAMS) == chosen
    first_span = jnp.where(is_chosen, longest, first_span)
    spans_all = jnp.stack([first_span, LEN - first_span], axis=1)
    half_limit = jnp.maximum(spans_all // 2, 1)
    padding = jax.random.randint(subkeys[3], (STREAMS, DOCS), 0, half_limit)
    chosen_pad = jnp.array([0, quarter_rows - 1], dtype=jnp.int32)
    padding = jnp.where(is_chosen[:, None], chosen_pad[None, :], padding)
    return (spans_all.astype(jnp.int32), (spans_all - padding).astype(jnp.int32))


def draw_doc_spans(key, part):
    return doc_tables(key)[0]


def draw_doc_lengths(key, part):
    return doc_tables(key)[1]


def draw_rec_params(key, part):
    key = jax.random.fold_in(key, 11)
    subkeys = jax.random.split(key, 5)
    lead_shape = (N_MP, RWIDTH // N_MP)
    conv_taps = 0.5 * jax.random.normal(subkeys[0], lead_shape + (4,), jnp.float32)
    conv_bias = 0.5 * jax.random.normal(subkeys[1], lead_shape + (1,), jnp.float32)
    gate_bias = jax.random.normal(subkeys[2], lead_shape + (2,), jnp.float32)
    slow_share = 0.5
    slow_mask = jax.random.uniform(subkeys[3], lead_shape + (1,), jnp.float32) < slow_share
    pick_value = jax.random.uniform(subkeys[4], lead_shape + (1,), jnp.float32)
    slow_rate = jnp.exp(jnp.log(0.2 / LEN) + pick_value * jnp.log(10.0))
    fast_rate = jnp.exp(jnp.log(1.0 / 50.0) + pick_value * jnp.log(6.0))
    rate_step = jnp.where(slow_mask, slow_rate, fast_rate)
    lam_value = jnp.log(jnp.expm1(rate_step / 4.0))
    return jnp.concatenate([conv_taps, conv_bias, gate_bias, lam_value], axis=-1).astype(jnp.bfloat16)


def shard_levels(key, shape, pieces, smallest, high):
    loudness, own = 1.0, jax.random.fold_in(key, 6)
    for dim, blocks in pieces:
        heights = jnp.exp(jax.random.uniform(jax.random.fold_in(own, dim), (blocks,), jnp.float32, smallest / len(pieces), high / len(pieces)))
        loudness = loudness * jnp.repeat(heights, shape[dim] // blocks).reshape([-1 if axis == dim else 1 for axis in range(len(shape))])
    return loudness


def bell_draw(rng, shape, width, limit, shards=(), kind=jnp.bfloat16):
    factor_of = shard_levels(rng, shape, shards, -0.22, 0.18) if shards else 1.0
    result = jax.random.normal(rng, shape, jnp.float32) * width * factor_of
    return jnp.minimum(jnp.maximum(result, -limit), limit).astype(kind)


def setup_inputs(seed: int = 0) -> dict:
    arg_keys = jax.random.split(jax.random.key(seed), 16)
    return {
        "inputs": bell_draw(arg_keys[0], (STREAMS, LEN, D), 1.0, 6.0, ((1, 16),)),
        "doc_spans": draw_doc_spans(jax.random.fold_in(arg_keys[15], 71), 0),
        "doc_lengths": draw_doc_lengths(jax.random.fold_in(arg_keys[15], 71), 0),
        "state_in": bell_draw(arg_keys[3], (STREAMS, DOCS, RWIDTH), 1.0, 6.0, ((2, 2),), jnp.float32),
        "conv_in": bell_draw(arg_keys[4], (STREAMS, DOCS, CONV - 1, RWIDTH), 1.0, 6.0, ((3, 2),)),
        "norm_gains": jnp.clip(1.0 + 0.1 * jax.random.normal(arg_keys[5], (2, D), jnp.float32), 0.5, 1.5).astype(jnp.bfloat16),
        "w_x": bell_draw(arg_keys[6], (D, RWIDTH), D ** -0.5, 0.125, ((0, 16), (1, 2))),
        "w_g": bell_draw(arg_keys[7], (D, RWIDTH), D ** -0.5, 0.125, ((0, 16), (1, 2))),
        "rec_params": draw_rec_params(jax.random.fold_in(arg_keys[15], 71), 0),
        "gate_weights": bell_draw(arg_keys[9], (N_MP, RWIDTH // N_MP, 2 * HEAD_DIM), HEAD_DIM ** -0.5, 0.5, ((0, 2), (1, 16))),
        "w_o": bell_draw(arg_keys[10], (RWIDTH, D), RWIDTH ** -0.5, 0.125, ((0, 2), (1, 16))),
        "w_gate": bell_draw(arg_keys[11], (D, FF), D ** -0.5, 0.125, ((0, 16), (1, 2))),
        "w_up": bell_draw(arg_keys[12], (D, FF), D ** -0.5, 0.125, ((0, 16), (1, 2))),
        "w_down": bell_draw(arg_keys[13], (FF, D), FF ** -0.5, 0.078125, ((0, 2), (1, 16))),
        "cotangent": bell_draw(arg_keys[14], (STREAMS, LEN, D), 1.0, 6.0, ((1, 16),)),
    }


@jax.custom_vjp
def low(v):
    return lax.optimization_barrier(v.astype(jnp.bfloat16)).astype(jnp.float32)

@jax.custom_vjp
def low_back(v):
    return v

def low_keep(v):
    return (low(v), None)

def low_pass(kept, grad):
    return (grad,)

def back_keep(v):
    return (v, None)

def back_low(kept, grad):
    return (low(grad),)
low.defvjp(low_keep, low_pass)
low_back.defvjp(back_keep, back_low)
EPSILON = 1e-06

def matmul_high(left, right):
    return jnp.dot(left, right, precision=lax.Precision.HIGHEST, preferred_element_type=jnp.float32)

def rms_norm(values, norm_gain):
    factor = lax.rsqrt(lax.optimization_barrier(jnp.mean(values * values, axis=-1, keepdims=True)) + EPSILON)
    return values * factor * norm_gain

def gate_math(pre_rate, pre_entry, lam_param, conv_value):
    rate_gate = jax.nn.sigmoid(pre_rate)
    entry_gate = jax.nn.sigmoid(pre_entry)
    log_decay = -8.0 * rate_gate * jax.nn.softplus(lam_param)
    retain = jnp.exp(log_decay)
    factor = jnp.sqrt(-jnp.expm1(2.0 * log_decay))
    return (retain, factor * entry_gate * conv_value)

def chain(earlier, latter):
    return (earlier[0] * latter[0], latter[0] * earlier[1] + latter[1])

def stream_forward(inputs, params, doc_spans, doc_lengths, state_in, conv_in):
    norm_gains, w_x, w_g, rec_params, gate_weights, w_o, w_gate, w_up, w_down = params
    total_len = inputs.shape[0]
    rec_width = w_x.shape[1]
    position = jnp.arange(total_len, dtype=jnp.int32)
    second_start = doc_spans[0]
    doc_id = (position >= second_start).astype(jnp.int32)
    doc_start = doc_id * second_start
    doc_stop = doc_start + jnp.where(doc_id == 1, doc_lengths[1], doc_lengths[0])
    live_rows = (position < doc_stop).astype(jnp.float32)[:, None]
    normed_one = low(rms_norm(inputs, norm_gains[0]))
    conv_source = low_back(low(matmul_high(normed_one, w_x)))
    branch_pre = low_back(matmul_high(normed_one, w_g))
    branch = jax.nn.gelu(branch_pre)
    conv_value = rec_params[:, 4] + rec_params[:, 0] * conv_source
    for offset in (1, 2, 3):
        earlier_rows = jnp.concatenate([jnp.zeros((offset, rec_width), jnp.float32), conv_source[:total_len - offset]], axis=0)
        earlier_pos = position - offset
        slot_index = jnp.clip(3 + earlier_pos - doc_start, 0, 2).astype(jnp.int32)
        kept_rows = conv_in[doc_id, slot_index]
        conv_value = conv_value + rec_params[:, offset] * jnp.where((earlier_pos >= doc_start)[:, None], earlier_rows, kept_rows)
    conv_low = low(conv_value)
    heads_all = gate_weights.shape[0]
    head_dim = gate_weights.shape[1]
    gate_mixed = jnp.einsum('nhk,hko->nho', conv_low.reshape(total_len, heads_all, head_dim), gate_weights, precision=lax.Precision.HIGHEST)
    pre_rate = low_back(gate_mixed[..., :head_dim].reshape(total_len, rec_width) + rec_params[:, 5])
    pre_entry = low_back(gate_mixed[..., head_dim:].reshape(total_len, rec_width) + rec_params[:, 6])
    retain, drive_term = gate_math(pre_rate, pre_entry, rec_params[:, 7], conv_value)
    reset_rows = (position == doc_start)[:, None]
    carried = state_in[doc_id]
    retain_eff = jnp.where(reset_rows, 0.0, retain)
    drive_eff = drive_term + jnp.where(reset_rows, retain * carried, 0.0)
    states = lax.associative_scan(chain, (retain_eff, drive_eff), axis=0)[1]
    mixed_rows = low(states * branch)
    rec_total = low_back(matmul_high(mixed_rows, w_o))
    hidden_one = inputs + live_rows * rec_total
    normed_two = low(rms_norm(hidden_one, norm_gains[1]))
    gate_value = low_back(matmul_high(normed_two, w_gate))
    up_value = low_back(matmul_high(normed_two, w_up))
    activated = low(jax.nn.gelu(gate_value) * up_value)
    down_total = low_back(matmul_high(activated, w_down))
    output = hidden_one + live_rows * down_total
    starts_doc = jnp.concatenate([jnp.zeros((1,), jnp.int32), doc_spans[:1]]).astype(jnp.int32)
    stops_doc = (starts_doc + doc_lengths).astype(jnp.int32)
    final_state = states[stops_doc - 1]
    slot_range = jnp.arange(3, dtype=jnp.int32)
    tail_pos = (stops_doc[:, None] - 3 + slot_range[None, :]).astype(jnp.int32)
    from_rows = conv_source[jnp.clip(tail_pos, 0, total_len - 1).astype(jnp.int32)]
    state_slot = jnp.clip(doc_lengths[:, None] + slot_range[None, :], 0, 2).astype(jnp.int32)
    from_state = conv_in[jnp.arange(2, dtype=jnp.int32)[:, None], state_slot]
    final_conv = jnp.where((tail_pos >= starts_doc[:, None])[..., None], from_rows, from_state)
    return (output, final_state, final_conv)

def reference(inputs, doc_spans, doc_lengths, state_in, conv_in, norm_gains, w_x, w_g, rec_params, gate_weights, w_o, w_gate, w_up, w_down, cotangent):
    params = (norm_gains.astype(jnp.float32), w_x.astype(jnp.float32), w_g.astype(jnp.float32), rec_params.astype(jnp.float32).reshape(RWIDTH, 8), gate_weights.astype(jnp.float32).reshape(HEADS, HEAD_DIM, 2 * HEAD_DIM), w_o.astype(jnp.float32), w_gate.astype(jnp.float32), w_up.astype(jnp.float32), w_down.astype(jnp.float32))

    def one_stream(totals, item):
        row_in, row_cot, row_spans, row_lengths, row_state, row_conv = item

        def forward(values, weights):
            return stream_forward(values, weights, row_spans, row_lengths, row_state, row_conv)
        (output, final_state, final_conv), pullback = jax.vjp(forward, row_in.astype(jnp.float32), params)
        input_grad, weight_grads = pullback((row_cot.astype(jnp.float32), jnp.zeros_like(final_state), jnp.zeros_like(final_conv)))
        totals = jax.tree.map(jnp.add, totals, weight_grads)
        return (totals, (output.astype(jnp.bfloat16), input_grad.astype(jnp.bfloat16), final_state, final_conv.astype(jnp.bfloat16)))
    zero_grads = jax.tree.map(jnp.zeros_like, params)
    totals, stacked = lax.scan(one_stream, zero_grads, (inputs, cotangent, doc_spans, doc_lengths, state_in, conv_in.astype(jnp.float32)))
    output, input_grad, final_state, final_conv = stacked
    g_gains, g_wx, g_wg, g_params, g_gates, g_wo, g_gate, g_up, g_down = totals
    final_state = final_state.reshape(STREAMS, DOCS, N_MP, RWIDTH // N_MP)
    final_conv = final_conv.reshape(STREAMS, DOCS, CONV - 1, N_MP, RWIDTH // N_MP)
    return (output, input_grad, final_state, final_conv, g_gains, g_wx, g_wg, g_params.reshape(N_MP, RWIDTH // N_MP, 8), g_gates.reshape(N_MP, RWIDTH // N_MP, 2 * HEAD_DIM), g_wo, g_gate, g_up, g_down)
```

```python
from functools import partial

import jax
import jax.numpy as jnp
from jax import lax
from jax.experimental import pallas as pl
from jax.experimental.pallas import tpu as pltpu
from jax.sharding import Mesh
from jax.sharding import PartitionSpec as P

HEAD_DIM = 160
PLANE = 4
SEGMENTS = 8
EPSILON = 1e-06
BF16 = jnp.bfloat16
F32 = jnp.float32


def dot(left, right, left_dim, right_dim):
    return lax.dot_general(
        left, right, (((left_dim,), (right_dim,)), ((), ())), preferred_element_type=F32
    )


def to_partner(block, bit):
    return lax.ppermute(block, "j", [(i, i ^ bit) for i in range(PLANE)])


def at(block, index, axis):
    return lax.dynamic_index_in_dim(block, index, axis, keepdims=False)


def put(whole, block, index, axis):
    return lax.dynamic_update_index_in_dim(whole, block, index, axis)


def plane_gather(own):
    mine = lax.axis_index("j")
    streams, rows, width = own.shape
    half = streams // 2
    from_x = to_partner(own, 1)
    from_y = to_partner(own, 2)
    first = to_partner(from_x[:half], 2)
    second = to_partner(from_y[half:], 1)
    whole = jnp.zeros((streams, PLANE, rows, width), own.dtype)
    whole = put(whole, own, mine, 1)
    whole = put(whole, from_x, mine ^ 1, 1)
    whole = put(whole, from_y, mine ^ 2, 1)
    whole = put(whole, jnp.concatenate([first, second], axis=0), mine ^ 3, 1)
    return whole.reshape(streams, PLANE * rows, width)


def plane_sum(part, streams):
    mine = lax.axis_index("j")
    width = part.shape[-1]
    part = part.astype(BF16).reshape(streams, PLANE, -1, width)
    half = streams // 2
    far = at(part, mine ^ 3, 1)
    via_x = to_partner(far[:half], 1).astype(F32)
    via_y = to_partner(far[half:], 2).astype(F32)
    for_x = at(part, mine ^ 1, 1)
    for_y = at(part, mine ^ 2, 1)
    for_x = jnp.concatenate([for_x[:half], (for_x[half:] + via_y).astype(BF16)], axis=0)
    for_y = jnp.concatenate([(for_y[:half] + via_x).astype(BF16), for_y[half:]], axis=0)
    from_x = to_partner(for_x, 1)
    from_y = to_partner(for_y, 2)
    own = at(part, mine, 1)
    return own.astype(F32) + from_x.astype(F32) + from_y.astype(F32)


def plane_swap(blocks):
    mine = lax.axis_index("j")
    swapped = blocks
    for bit in (1, 2, 3):
        swapped = put(swapped, to_partner(at(blocks, mine ^ bit, 0), bit), mine ^ bit, 0)
    return swapped


def spread(weight):
    rows, four, columns = weight.shape
    blocks = plane_swap(jnp.moveaxis(weight, 1, 0)).reshape(four * rows, columns)
    return lax.all_gather(blocks, ("c", "z"), axis=0, tiled=False).reshape(
        lax.axis_size("c"), -1, columns
    )


def collect(grads, rows):
    halves, all_rows, columns = grads.shape
    summed = lax.psum_scatter(
        grads.reshape(halves * all_rows, columns), ("c", "z"), scatter_dimension=0, tiled=True
    )
    return jnp.moveaxis(plane_swap(summed.reshape(PLANE, rows, columns)), 0, 1).astype(F32)


def with_other_core(array, dim):
    core = lax.axis_index("c")
    count = array.shape[0] // 2
    mine = lax.dynamic_slice_in_dim(array, core * count, count, 0)
    other = lax.dynamic_slice_in_dim(array, (1 - core) * count, count, 0)
    other = lax.ppermute(other, "c", [(0, 1), (1, 0)])
    return jnp.where(
        core == 0,
        jnp.concatenate([mine, other], axis=dim),
        jnp.concatenate([other, mine], axis=dim),
    )


def all_streams(own):
    core = lax.axis_index("c")
    other = lax.ppermute(own, "c", [(0, 1), (1, 0)])
    count = own.shape[0]
    whole = jnp.zeros((2 * count, *own.shape[1:]), own.dtype)
    whole = lax.dynamic_update_slice_in_dim(whole, own, core * count, 0)
    return lax.dynamic_update_slice_in_dim(whole, other, (1 - core) * count, 0)


def shifted(block, distance):
    size = lax.axis_size("z")
    return lax.ppermute(
        block, "z", [(i - distance, i) for i in range(size) if 0 <= i - distance < size]
    )


def entering(keep, state, backward):
    size, mine = lax.axis_size("z"), lax.axis_index("z")
    pair = jnp.stack([keep, state])
    result = jnp.zeros_like(state)
    for distance in range(size - 1, 0, -1):
        got = shifted(pair, -distance if backward else distance)
        there = mine + distance < size if backward else mine >= distance
        result = jnp.where(there, got[0] * result + got[1], result)
    return result


def scan_kernel(backward, keep_ref, add_ref, product_ref, state_ref):
    streams, rows, width = keep_ref.shape
    steps = rows // SEGMENTS
    for s in range(streams):

        def step(number, carry):
            product, state = carry
            place = steps - 1 - number if backward else number
            at_once = pl.ds(place, SEGMENTS, stride=steps)
            keep = keep_ref[s, at_once, :]
            state = keep * state + add_ref[s, at_once, :]
            product = keep * product
            product_ref[s, at_once, :] = product
            state_ref[s, at_once, :] = state
            return product, state

        product, state = lax.fori_loop(
            0,
            steps,
            step,
            (jnp.ones((SEGMENTS, width), F32), jnp.zeros((SEGMENTS, width), F32)),
            unroll=8,
        )
        product_in = jnp.ones((1, width), F32)
        state_in = jnp.zeros((1, width), F32)
        order = range(SEGMENTS - 1, -1, -1) if backward else range(SEGMENTS)
        for k in order:
            here = pl.ds(k * steps, steps)
            local = product_ref[s, here, :]
            state_ref[s, here, :] = state_ref[s, here, :] + local * state_in
            product_ref[s, here, :] = local * product_in
            state_in = product[k : k + 1] * state_in + state[k : k + 1]
            product_in = product[k : k + 1] * product_in


def local_scan(keep, add, backward):
    streams, rows, width = keep.shape
    block = pl.BlockSpec((streams, rows, 128), lambda i: (0, 0, i))
    return pl.pallas_call(
        partial(scan_kernel, backward),
        grid=(width // 128,),
        in_specs=[block, block],
        out_specs=[block, block],
        out_shape=[jax.ShapeDtypeStruct(keep.shape, F32)] * 2,
        compiler_params=pltpu.CompilerParams(vmem_limit_bytes=32 * 1024 * 1024),
        cost_estimate=pl.CostEstimate(
            flops=8 * streams * rows * width,
            bytes_accessed=16 * streams * rows * width,
            transcendentals=0,
        ),
    )(keep, add)


def rms_norm(values, norm_gain):
    factor = lax.rsqrt(jnp.mean(values * values, axis=-1, keepdims=True) + EPSILON)
    return values * factor * norm_gain


def gate_math(pre_rate, pre_entry, lam_param, conv_value):
    rate_gate = jax.nn.sigmoid(pre_rate)
    entry_gate = jax.nn.sigmoid(pre_entry)
    log_decay = -8.0 * rate_gate * jax.nn.softplus(lam_param)
    retain = jnp.exp(log_decay)
    factor = jnp.sqrt(-jnp.expm1(2.0 * log_decay))
    return (retain, factor * entry_gate * conv_value)


def mix_gelu(gate_value, up_value):
    return jax.nn.gelu(gate_value) * up_value


def convolve(extended, conv_taps, conv_bias, fill_values, insides):
    n_rows = extended.shape[1] - 3
    result = conv_bias + conv_taps[:, 0] * extended[:, 3:]
    for offset in (1, 2, 3):
        window = extended[:, 3 - offset : 3 - offset + n_rows]
        result = result + conv_taps[:, offset] * jnp.where(
            insides[offset - 1], window, fill_values[offset - 1]
        )
    return result


def halves_together(weight, parts):
    halves, rows, columns = weight.shape
    each = columns // parts
    return jnp.concatenate(
        [weight[h, :, p * each : (p + 1) * each] for p in range(parts) for h in range(halves)],
        axis=1,
    )


def halves_apart(grads, halves):
    each = grads[0].shape[1] // halves
    return jnp.stack(
        [
            jnp.concatenate([g[:, h * each : (h + 1) * each] for g in grads], axis=1)
            for h in range(halves)
        ]
    )


def shards(
    inputs,
    doc_spans,
    doc_lengths,
    state_in,
    conv_in,
    norm_gains,
    w_x,
    w_g,
    rec_params,
    gate_weights,
    w_o,
    w_gate,
    w_up,
    w_down,
    cotangent,
):
    all_streams_count, own_rows, model_width = inputs.shape
    halves = lax.axis_size("c")
    z_size = lax.axis_size("z")
    z_index, j_index, core = lax.axis_index("z"), lax.axis_index("j"), lax.axis_index("c")
    n_streams = all_streams_count // halves
    n_rows = own_rows * PLANE
    tokens = n_streams * n_rows
    own_tokens = n_streams * own_rows
    weight_rows = w_x.shape[0]
    half_width = w_x.shape[1]
    part_width = half_width // PLANE
    rec_width = part_width * halves
    heads_here = rec_width // HEAD_DIM
    ff_part = w_gate.shape[1] // PLANE

    first_stream = core * n_streams

    def own_streams(array):
        return lax.dynamic_slice_in_dim(array, first_stream, n_streams, 0)

    spans = own_streams(doc_spans)
    lengths = own_streams(doc_lengths)
    own_in = own_streams(inputs)
    own_cot = own_streams(cotangent)
    whole_in = plane_gather(own_in)
    gains_all = lax.all_gather(norm_gains, ("z", "j"), axis=1, tiled=True).astype(F32)
    small = lax.all_gather(
        jnp.concatenate([rec_params[0], gate_weights[0]], axis=1), ("c", "z", "j"), axis=0
    ).reshape(halves, half_width, -1)
    small = lax.dynamic_slice_in_dim(small, j_index * part_width, part_width, 1)
    small = small.reshape(rec_width, -1)
    params_all = small[:, :8].astype(F32)
    gates_all = small[:, 8:].reshape(heads_here, HEAD_DIM, 2 * HEAD_DIM)

    def by_chip(weight):
        return weight.reshape(weight_rows, PLANE, -1)

    w_rec = halves_together(spread(jnp.concatenate([by_chip(w_x), by_chip(w_g)], axis=2)), 2)
    w_back = halves_together(spread(by_chip(w_o.T)), 1)
    w_wide = spread(jnp.concatenate([by_chip(w_gate), by_chip(w_up)], axis=2))
    w_narrow = spread(by_chip(w_down.T))

    def live_at(position):
        second_start = spans[:, 0:1]
        doc_id = (position[None, :] >= second_start).astype(jnp.int32)
        doc_start = doc_id * second_start
        doc_stop = doc_start + jnp.where(doc_id == 1, lengths[:, 1:2], lengths[:, 0:1])
        live = (position[None, :] < doc_stop).astype(F32)
        return doc_id, doc_start, live

    own_first = (z_index * PLANE + j_index) * own_rows
    own_live = live_at(own_first + jnp.arange(own_rows, dtype=jnp.int32))[2]
    own_live = own_live.reshape(own_tokens, 1)
    position = z_index * n_rows + jnp.arange(n_rows, dtype=jnp.int32)
    doc_id, doc_start, _ = live_at(position)

    d_out = own_cot.reshape(own_tokens, model_width).astype(F32)
    own_down = (d_out * own_live).astype(BF16).reshape(n_streams, own_rows, model_width)
    d_down = plane_gather(own_down).reshape(tokens, model_width)

    flat_in = own_in.reshape(own_tokens, model_width).astype(F32)
    _, norm_one_back = jax.vjp(rms_norm, flat_in, gains_all[0])
    normed_low = rms_norm(
        whole_in.reshape(tokens, model_width).astype(F32), gains_all[0]
    ).astype(BF16)
    projected = dot(normed_low, w_rec, 1, 0)
    source_rows = projected[:, :rec_width].astype(BF16).reshape(n_streams, n_rows, rec_width)
    branch, branch_back = jax.vjp(jax.nn.gelu, projected[:, rec_width:])
    rim_rows = shifted(source_rows[:, n_rows - 3 :], 1)
    extended = jnp.concatenate([rim_rows, source_rows], axis=1).astype(F32)

    conv_here = with_other_core(
        lax.dynamic_slice_in_dim(conv_in, j_index * part_width, part_width, 3), 3
    )
    state_here = with_other_core(
        lax.dynamic_slice_in_dim(state_in, j_index * part_width, part_width, 2), 2
    )
    slot_range = jnp.arange(3, dtype=jnp.int32)
    doc_range = jnp.arange(2, dtype=jnp.int32)
    fill_values = []
    insides = []
    for offset in (1, 2, 3):
        earlier_pos = position[None, :] - offset
        insides.append((earlier_pos >= doc_start)[..., None])
        slot_pick = (doc_id[..., None, None] == doc_range[:, None]) & (
            (3 + earlier_pos - doc_start)[..., None, None] == slot_range
        )
        fill_values.append(
            jnp.einsum(
                "btds,bdsc->btc",
                slot_pick.astype(BF16),
                conv_here,
                preferred_element_type=F32,
            )
        )
    conv_value, conv_back = jax.vjp(
        partial(convolve, fill_values=fill_values, insides=insides),
        extended,
        params_all[:, 0:4],
        params_all[:, 4],
    )
    conv_flat = conv_value.reshape(tokens, rec_width)
    conv_low = conv_flat.astype(BF16).reshape(tokens, heads_here, HEAD_DIM)
    gate_mixed = jnp.einsum("nhk,hko->nho", conv_low, gates_all, preferred_element_type=F32)
    pre_rate = gate_mixed[..., :HEAD_DIM].reshape(tokens, rec_width) + params_all[:, 5]
    pre_entry = gate_mixed[..., HEAD_DIM:].reshape(tokens, rec_width) + params_all[:, 6]
    (retain, drive_term), gate_back = jax.vjp(
        gate_math, pre_rate, pre_entry, params_all[:, 7], conv_flat
    )
    reset_rows = (position[None, :] == doc_start)[..., None]
    carried = jnp.where((doc_id == 1)[..., None], state_here[:, None, 1], state_here[:, None, 0])
    retain_rows = retain.reshape(n_streams, n_rows, rec_width)
    retain_eff = jnp.where(reset_rows, 0.0, retain_rows)
    drive_eff = drive_term.reshape(n_streams, n_rows, rec_width) + jnp.where(
        reset_rows, retain_rows * carried, 0.0
    )
    local_keep, local_state = local_scan(retain_eff, drive_eff, False)
    state_before = entering(local_keep[:, -1], local_state[:, -1], False)
    states = local_state + local_keep * state_before[:, None]

    starts_doc = jnp.concatenate([jnp.zeros_like(spans[:, :1]), spans[:, :1]], axis=1)
    stops_doc = starts_doc + lengths
    is_last = position[None, :, None] == (stops_doc - 1)[:, None, :]
    final_part = jnp.sum(jnp.where(is_last[..., None], states[:, :, None, :], 0.0), axis=1)
    tail_pos = stops_doc[..., None] - 3 + slot_range
    from_rows = (position[None, :, None, None] == tail_pos[:, None]) & (
        tail_pos >= starts_doc[..., None]
    )[:, None]
    conv_part = jnp.einsum(
        "btdj,btc->bdjc", from_rows.astype(BF16), source_rows, preferred_element_type=F32
    )
    from_state = (
        (tail_pos < starts_doc[..., None])[..., None]
        & ((lengths[..., None] + slot_range)[..., None] == slot_range)
        & (z_index == 0)
    )
    conv_part = conv_part + jnp.einsum(
        "bdjs,bdsc->bdjc", from_state.astype(BF16), conv_here, preferred_element_type=F32
    )
    finals = jnp.concatenate([final_part[:, :, None], conv_part], axis=2)
    finals = lax.all_gather(finals, ("z", "j", "c"), axis=0)
    finals = finals.reshape(z_size, PLANE, halves * n_streams, 2, 4, halves, part_width)
    finals = jnp.sum(finals, axis=0)
    finals = at(finals, core, 4)
    finals = jnp.moveaxis(finals, 0, 3).reshape(all_streams_count, 2, 4, half_width)
    dp_index = z_index * PLANE + j_index
    out_width = half_width // (z_size * PLANE)
    finals = lax.dynamic_slice_in_dim(finals, dp_index * out_width, out_width, 3)
    state_block = finals[:, :, 0][:, :, None]
    conv_block = finals[:, :, 1:].astype(BF16)[:, :, :, None]

    states_flat = states.reshape(tokens, rec_width)
    mixed_rows = (states_flat * branch).astype(BF16)
    rec_part = dot(mixed_rows, w_back, 1, 1)
    rec_total = plane_sum(rec_part, n_streams).reshape(own_tokens, model_width)
    hidden_one = flat_in + own_live * rec_total
    normed_two, norm_two_back = jax.vjp(rms_norm, hidden_one, gains_all[1])
    own_second = normed_two.astype(BF16).reshape(n_streams, own_rows, model_width)
    second_low = plane_gather(own_second).reshape(tokens, model_width)

    down_part = second_part = 0.0
    g_narrow, g_wide = [], []
    for h in range(halves):
        both = dot(second_low, w_wide[h], 1, 0)
        activated, mix_back = jax.vjp(mix_gelu, both[:, :ff_part], both[:, ff_part:])
        act_low = activated.astype(BF16)
        down_part = down_part + dot(act_low, w_narrow[h], 1, 1)
        d_act = dot(d_down, w_narrow[h], 1, 0)
        d_both = jnp.concatenate([d.astype(BF16) for d in mix_back(d_act)], axis=1)
        second_part = second_part + dot(d_both, w_wide[h], 1, 1)
        g_narrow.append(dot(d_down, act_low, 0, 0).astype(BF16))
        g_wide.append(dot(second_low, d_both, 0, 0).astype(BF16))
    out_narrow = collect(jnp.stack(g_narrow), weight_rows)
    out_wide = collect(jnp.stack(g_wide), weight_rows)

    mlp_total = plane_sum(down_part, n_streams).reshape(own_tokens, model_width)
    out_flat = (hidden_one + own_live * mlp_total).astype(BF16)
    output = all_streams(out_flat.reshape(n_streams, own_rows, model_width))

    second_total = plane_sum(second_part, n_streams).reshape(own_tokens, model_width)
    d_hidden_norm, g_gain_two = norm_two_back(second_total)
    d_hidden = d_out + d_hidden_norm
    own_rec = (d_hidden * own_live).astype(BF16).reshape(n_streams, own_rows, model_width)
    d_rec = plane_gather(own_rec).reshape(tokens, model_width)
    d_mixed = dot(d_rec, w_back, 1, 0)
    g_back = dot(d_rec, mixed_rows, 0, 0).astype(BF16)
    out_back = collect(halves_apart([g_back], halves), weight_rows)

    grad_state = (d_mixed * branch).reshape(n_streams, n_rows, rec_width)
    branch_low = branch_back(d_mixed * states_flat)[0].astype(BF16)
    next_keep = jnp.concatenate([retain_eff[:, 1:], jnp.ones_like(retain_eff[:, :1])], axis=1)
    later_keep, later_sum = local_scan(next_keep, grad_state, True)
    carried_grad = entering(
        retain_eff[:, 0] * later_keep[:, 0], retain_eff[:, 0] * later_sum[:, 0], True
    )
    adjoint = later_sum + later_keep * carried_grad[:, None]
    state_prev = jnp.concatenate([state_before[:, None], states[:, :-1]], axis=1)
    state_prev = jnp.where(reset_rows, carried, state_prev)
    d_retain = (adjoint * state_prev).reshape(tokens, rec_width)
    d_rate, d_entry, g_lam, d_conv_direct = gate_back(
        (d_retain, adjoint.reshape(tokens, rec_width))
    )
    rate_low = d_rate.astype(BF16)
    entry_low = d_entry.astype(BF16)
    grad_gates = jnp.concatenate(
        [
            rate_low.reshape(tokens, heads_here, HEAD_DIM),
            entry_low.reshape(tokens, heads_here, HEAD_DIM),
        ],
        axis=2,
    )
    g_gates = jnp.einsum(
        "nhk,nho->hko", conv_low, grad_gates, preferred_element_type=F32
    ).reshape(rec_width, 2 * HEAD_DIM)
    d_conv_gates = jnp.einsum(
        "nho,hko->nhk", grad_gates, gates_all, preferred_element_type=F32
    ).reshape(tokens, rec_width)
    d_conv = (d_conv_direct + d_conv_gates).reshape(n_streams, n_rows, rec_width)
    d_extended, g_taps, g_conv_bias = conv_back(d_conv)
    rim_grad = shifted(d_extended[:, :3].astype(BF16), -1).astype(F32)
    d_source = jnp.concatenate([d_extended[:, 3:n_rows], d_extended[:, n_rows:] + rim_grad], axis=1)
    d_projected = jnp.concatenate(
        [d_source.reshape(tokens, rec_width).astype(BF16), branch_low], axis=1
    )
    first_part = dot(d_projected, w_rec, 1, 1)
    g_rec = dot(normed_low, d_projected, 0, 0).astype(BF16)
    out_rec = collect(
        halves_apart([g_rec[:, :rec_width], g_rec[:, rec_width:]], halves), weight_rows
    )
    g_small = jnp.concatenate(
        [
            g_taps,
            g_conv_bias[:, None],
            jnp.sum(rate_low.astype(F32), axis=0)[:, None],
            jnp.sum(entry_low.astype(F32), axis=0)[:, None],
            g_lam[:, None],
            g_gates,
        ],
        axis=1,
    ).astype(BF16)
    g_small = lax.psum_scatter(g_small, ("c", "z"), scatter_dimension=0, tiled=True)
    route = [(z * PLANE + j, j * z_size + z) for z in range(z_size) for j in range(PLANE)]
    g_small = lax.ppermute(g_small, ("z", "j"), route).astype(F32)[None]

    first_total = plane_sum(first_part, n_streams).reshape(own_tokens, model_width)
    d_input_norm, g_gain_one = norm_one_back(first_total)
    input_grad = all_streams(
        (d_hidden + d_input_norm).astype(BF16).reshape(n_streams, own_rows, model_width)
    )
    g_gains = lax.psum(jnp.stack([g_gain_one, g_gain_two]), ("z", "j", "c"))
    gain_width = norm_gains.shape[1]
    g_gains = lax.dynamic_slice_in_dim(g_gains, dp_index * gain_width, gain_width, 1)

    def flat(blocks):
        return blocks.reshape(weight_rows, -1)

    return (
        output,
        input_grad,
        state_block,
        conv_block,
        g_gains,
        flat(out_rec[..., :part_width]),
        flat(out_rec[..., part_width:]),
        g_small[..., :8],
        g_small[..., 8:],
        flat(out_back).T,
        flat(out_wide[..., :ff_part]),
        flat(out_wide[..., ff_part:]),
        flat(out_narrow).T,
    )


def solution(mesh):
    devices = mesh.devices.reshape(-1, PLANE, mesh.shape["mp"])
    planes = Mesh(devices, ("z", "j", "c"))
    dp, mp = ("z", "j"), "c"
    return jax.shard_map(
        shards,
        mesh=planes,
        in_specs=(
            P(None, dp, None),
            P(),
            P(),
            P(None, None, mp),
            P(None, None, None, mp),
            P(None, dp),
            P(dp, mp),
            P(dp, mp),
            P(mp, dp, None),
            P(mp, dp, None),
            P(mp, dp),
            P(dp, mp),
            P(dp, mp),
            P(mp, dp),
            P(None, dp, None),
        ),
        out_specs=(
            P(None, dp, None),
            P(None, dp, None),
            P(None, None, mp, dp),
            P(None, None, None, mp, dp),
            P(None, dp),
            P(dp, mp),
            P(dp, mp),
            P(mp, dp, None),
            P(mp, dp, None),
            P(mp, dp),
            P(dp, mp),
            P(dp, mp),
            P(mp, dp),
        ),
        check_vma=False,
    )
```

```python
from functools import partial

import jax
import jax.numpy as jnp
from jax import lax
from jax.experimental import pallas as pl
from jax.experimental.pallas import tpu as pltpu
from jax.sharding import Mesh
from jax.sharding import PartitionSpec as P

HEAD_DIM = 160
PLANE = 4
SEGMENTS = 8
EPSILON = 1e-06
BF16 = jnp.bfloat16
F32 = jnp.float32


def dot(left, right, left_dim, right_dim):
    return lax.dot_general(
        left, right, (((left_dim,), (right_dim,)), ((), ())), preferred_element_type=F32
    )


def to_partner(block, bit):
    return lax.ppermute(block, "j", [(i, i ^ bit) for i in range(PLANE)])


def at(block, index, axis):
    return lax.dynamic_index_in_dim(block, index, axis, keepdims=False)


def put(whole, block, index, axis):
    return lax.dynamic_update_index_in_dim(whole, block, index, axis)


def in_order(found, index):
    low, high = index % 2 == 1, index // 2 == 1
    found = [jnp.where(low, found[k ^ 1], found[k]) for k in range(PLANE)]
    return [jnp.where(high, found[k ^ 2], found[k]) for k in range(PLANE)]


def plane_gather(own):
    mine = lax.axis_index("j")
    streams, rows, width = own.shape
    half = streams // 2
    from_x = to_partner(own, 1)
    from_y = to_partner(own, 2)
    first = to_partner(from_x[:half], 2)
    second = to_partner(from_y[half:], 1)
    whole = jnp.zeros((streams, PLANE, rows, width), own.dtype)
    whole = put(whole, own, mine, 1)
    whole = put(whole, from_x, mine ^ 1, 1)
    whole = put(whole, from_y, mine ^ 2, 1)
    whole = put(whole, jnp.concatenate([first, second], axis=0), mine ^ 3, 1)
    return whole.reshape(streams, PLANE * rows, width)


def plane_sum(part, streams):
    mine = lax.axis_index("j")
    width = part.shape[-1]
    part = part.astype(BF16).reshape(streams, PLANE, -1, width)
    half = streams // 2
    far = at(part, mine ^ 3, 1)
    via_x = to_partner(far[:half], 1).astype(F32)
    via_y = to_partner(far[half:], 2).astype(F32)
    for_x = at(part, mine ^ 1, 1)
    for_y = at(part, mine ^ 2, 1)
    for_x = jnp.concatenate([for_x[:half], (for_x[half:] + via_y).astype(BF16)], axis=0)
    for_y = jnp.concatenate([(for_y[:half] + via_x).astype(BF16), for_y[half:]], axis=0)
    from_x = to_partner(for_x, 1)
    from_y = to_partner(for_y, 2)
    own = at(part, mine, 1)
    return own.astype(F32) + from_x.astype(F32) + from_y.astype(F32)


def plane_swap(blocks):
    mine = lax.axis_index("j")
    found = [at(blocks, mine, 0)]
    found += [to_partner(at(blocks, mine ^ bit, 0), bit) for bit in (1, 2, 3)]
    return in_order(found, mine)


def to_chips(weight):
    rows, columns = weight.shape
    blocks = weight.reshape(rows, PLANE, columns // PLANE)
    return jnp.moveaxis(blocks, 1, 0)


def to_core(block):
    return lax.ppermute(block, "c", [(0, 1), (1, 0)])


def along_z(block):
    own = lax.all_gather(block, "z", axis=0, tiled=True)
    return own, to_core(own)


def collect(own, other):
    total = (own.astype(F32) + to_core(other).astype(F32)).astype(BF16)
    summed = lax.psum_scatter(total, "z", scatter_dimension=0, tiled=True)
    return plane_swap(summed.reshape(PLANE, -1, summed.shape[1]))


def z_gather(block):
    size, mine = lax.axis_size("z"), lax.axis_index("z")
    whole = jnp.zeros((size, *block.shape), block.dtype)
    whole = put(whole, block, mine, 0)
    for step in range(1, size):
        got = lax.ppermute(block, "z", [(i, (i + step) % size) for i in range(size)])
        whole = put(whole, got, (mine - step) % size, 0)
    return whole


def sum_of_all(array):
    for axis, pairs in (
        ("c", [(0, 1), (1, 0)]),
        ("j", [(i, i ^ 1) for i in range(PLANE)]),
        ("j", [(i, i ^ 2) for i in range(PLANE)]),
    ):
        array = array + lax.ppermute(array, axis, pairs)
    return jnp.sum(z_gather(array), axis=0)


def with_other_core(array, dim):
    core = lax.axis_index("c")
    count = array.shape[0] // 2
    mine = lax.dynamic_slice_in_dim(array, core * count, count, 0)
    other = lax.dynamic_slice_in_dim(array, (1 - core) * count, count, 0)
    return jnp.concatenate([mine, to_core(other)], axis=dim)


def all_streams(own):
    core = lax.axis_index("c")
    other = to_core(own)
    count = own.shape[0]
    whole = jnp.zeros((2 * count, *own.shape[1:]), own.dtype)
    whole = lax.dynamic_update_slice_in_dim(whole, own, core * count, 0)
    return lax.dynamic_update_slice_in_dim(whole, other, (1 - core) * count, 0)


def shifted(block, distance):
    size = lax.axis_size("z")
    return lax.ppermute(
        block, "z", [(i - distance, i) for i in range(size) if 0 <= i - distance < size]
    )


def entering(keep, state, backward):
    size, mine = lax.axis_size("z"), lax.axis_index("z")
    pair = jnp.stack([keep, state])
    result = jnp.zeros_like(state)
    for distance in range(size - 1, 0, -1):
        got = shifted(pair, -distance if backward else distance)
        there = mine + distance < size if backward else mine >= distance
        result = jnp.where(there, got[0] * result + got[1], result)
    return result


def scan_kernel(backward, keep_ref, add_ref, product_ref, state_ref):
    streams, rows, width = keep_ref.shape
    steps = rows // SEGMENTS
    for s in range(streams):

        def step(number, carry):
            product, state = carry
            place = steps - 1 - number if backward else number
            at_once = pl.ds(place, SEGMENTS, stride=steps)
            keep = keep_ref[s, at_once, :]
            state = keep * state + add_ref[s, at_once, :]
            product = keep * product
            product_ref[s, at_once, :] = product
            state_ref[s, at_once, :] = state
            return product, state

        product, state = lax.fori_loop(
            0,
            steps,
            step,
            (jnp.ones((SEGMENTS, width), F32), jnp.zeros((SEGMENTS, width), F32)),
            unroll=8,
        )
        product_in = jnp.ones((1, width), F32)
        state_in = jnp.zeros((1, width), F32)
        order = range(SEGMENTS - 1, -1, -1) if backward else range(SEGMENTS)
        for k in order:
            here = pl.ds(k * steps, steps)
            local = product_ref[s, here, :]
            state_ref[s, here, :] = state_ref[s, here, :] + local * state_in
            product_ref[s, here, :] = local * product_in
            state_in = product[k : k + 1] * state_in + state[k : k + 1]
            product_in = product[k : k + 1] * product_in


def local_scan(keep, add, backward):
    streams, rows, width = keep.shape
    block = pl.BlockSpec((streams, rows, 128), lambda i: (0, 0, i))
    return pl.pallas_call(
        partial(scan_kernel, backward),
        grid=(width // 128,),
        in_specs=[block, block],
        out_specs=[block, block],
        out_shape=[jax.ShapeDtypeStruct(keep.shape, F32)] * 2,
        compiler_params=pltpu.CompilerParams(vmem_limit_bytes=32 * 1024 * 1024),
        cost_estimate=pl.CostEstimate(
            flops=8 * streams * rows * width,
            bytes_accessed=16 * streams * rows * width,
            transcendentals=0,
        ),
    )(keep, add)


def rms_norm(values, norm_gain):
    factor = lax.rsqrt(jnp.mean(values * values, axis=-1, keepdims=True) + EPSILON)
    return values * factor * norm_gain


def gate_math(pre_rate, pre_entry, lam_param, conv_value):
    rate_gate = jax.nn.sigmoid(pre_rate)
    entry_gate = jax.nn.sigmoid(pre_entry)
    log_decay = -8.0 * rate_gate * jax.nn.softplus(lam_param)
    retain = jnp.exp(log_decay)
    factor = jnp.sqrt(-jnp.expm1(2.0 * log_decay))
    return (retain, factor * entry_gate * conv_value)


def mix_gelu(gate_value, up_value):
    return jax.nn.gelu(gate_value) * up_value


def convolve(extended, conv_taps, conv_bias, fill_values, insides):
    n_rows = extended.shape[1] - 3
    result = conv_bias + conv_taps[:, 0] * extended[:, 3:]
    for offset in (1, 2, 3):
        window = extended[:, 3 - offset : 3 - offset + n_rows]
        result = result + conv_taps[:, offset] * jnp.where(
            insides[offset - 1], window, fill_values[offset - 1]
        )
    return result


def shards(
    inputs,
    doc_spans,
    doc_lengths,
    state_in,
    conv_in,
    norm_gains,
    w_x,
    w_g,
    rec_params,
    gate_weights,
    w_o,
    w_gate,
    w_up,
    w_down,
    cotangent,
):
    all_streams_count, own_rows, model_width = inputs.shape
    halves = lax.axis_size("c")
    z_size = lax.axis_size("z")
    z_index, j_index, core = lax.axis_index("z"), lax.axis_index("j"), lax.axis_index("c")
    n_streams = all_streams_count // halves
    n_rows = own_rows * PLANE
    tokens = n_streams * n_rows
    own_tokens = n_streams * own_rows
    weight_rows = w_x.shape[0]
    half_width = w_x.shape[1]
    part_width = half_width // PLANE
    rec_width = part_width * halves
    heads_here = rec_width // HEAD_DIM
    ff_part = w_gate.shape[1] // PLANE

    first_stream = core * n_streams

    def own_streams(array):
        return lax.dynamic_slice_in_dim(array, first_stream, n_streams, 0)

    spans = own_streams(doc_spans)
    lengths = own_streams(doc_lengths)
    own_in = own_streams(inputs)
    own_cot = own_streams(cotangent)
    small_rows = rec_params.shape[1]
    small = jnp.concatenate([rec_params[0], gate_weights[0]], axis=1)
    small_width = small.shape[1]
    gain_width = norm_gains.shape[1]
    tails = jnp.pad(norm_gains, ((0, 0), (0, small_width - gain_width)))
    small = jnp.concatenate([small, tails], axis=0)

    first_blocks = jnp.concatenate([to_chips(w_x), to_chips(w_g), to_chips(w_o.T)], axis=2)
    first_rows = jnp.concatenate(plane_swap(first_blocks), axis=0)
    whole_in = plane_gather(own_in)
    found = [small] + [to_partner(small, bit) for bit in (1, 2, 3)]
    small = z_gather(jnp.stack(in_order(found, j_index)))
    gains_all = jnp.moveaxis(small[:, :, small_rows:, :gain_width], 2, 0)
    gains_all = gains_all.reshape(2, model_width).astype(F32)
    small = small[:, :, :small_rows].reshape(half_width, small_width)
    small = lax.dynamic_slice_in_dim(small, j_index * part_width, part_width, 0)
    small = jnp.concatenate([small, to_core(small)], axis=0)
    params_all = small[:, :8].astype(F32)
    gates_all = small[:, 8:].reshape(heads_here, HEAD_DIM, 2 * HEAD_DIM)

    w_first = along_z(first_rows)
    w_rec = jnp.concatenate(
        [w[:, p * part_width : (p + 1) * part_width] for p in (0, 1) for w in w_first], axis=1
    )
    w_back = jnp.concatenate([w[:, 2 * part_width :] for w in w_first], axis=1)
    later = (w_gate, w_up, w_down)
    later, whole_in = lax.optimization_barrier((later, whole_in))
    wide_blocks = jnp.concatenate([to_chips(later[0]), to_chips(later[1])], axis=2)
    wide_rows = jnp.concatenate(plane_swap(wide_blocks), axis=0)
    narrow_rows = jnp.concatenate(plane_swap(to_chips(later[2].T)), axis=0)
    own_cot, narrow_rows = lax.optimization_barrier((own_cot, narrow_rows))
    w_wide = along_z(wide_rows)
    narrow_rows, w_wide = lax.optimization_barrier((narrow_rows, w_wide))
    w_narrow = along_z(narrow_rows)

    def live_at(position):
        second_start = spans[:, 0:1]
        doc_id = (position[None, :] >= second_start).astype(jnp.int32)
        doc_start = doc_id * second_start
        doc_stop = doc_start + jnp.where(doc_id == 1, lengths[:, 1:2], lengths[:, 0:1])
        live = (position[None, :] < doc_stop).astype(F32)
        return doc_id, doc_start, live

    own_first = (z_index * PLANE + j_index) * own_rows
    own_live = live_at(own_first + jnp.arange(own_rows, dtype=jnp.int32))[2]
    own_live = own_live.reshape(own_tokens, 1)
    position = z_index * n_rows + jnp.arange(n_rows, dtype=jnp.int32)
    doc_id, doc_start, _ = live_at(position)

    d_out = own_cot.reshape(own_tokens, model_width).astype(F32)
    own_down = (d_out * own_live).astype(BF16).reshape(n_streams, own_rows, model_width)
    d_down = plane_gather(own_down).reshape(tokens, model_width)

    flat_in = own_in.reshape(own_tokens, model_width).astype(F32)
    _, norm_one_back = jax.vjp(rms_norm, flat_in, gains_all[0])
    normed_low = rms_norm(
        whole_in.reshape(tokens, model_width).astype(F32), gains_all[0]
    ).astype(BF16)
    projected = dot(normed_low, w_rec, 1, 0)
    source_rows = projected[:, :rec_width].astype(BF16).reshape(n_streams, n_rows, rec_width)
    branch, branch_back = jax.vjp(jax.nn.gelu, projected[:, rec_width:])
    rim_rows = shifted(source_rows[:, n_rows - 3 :], 1)
    extended = jnp.concatenate([rim_rows, source_rows], axis=1).astype(F32)

    conv_here = with_other_core(
        lax.dynamic_slice_in_dim(conv_in, j_index * part_width, part_width, 3), 3
    )
    state_here = with_other_core(
        lax.dynamic_slice_in_dim(state_in, j_index * part_width, part_width, 2), 2
    )
    slot_range = jnp.arange(3, dtype=jnp.int32)
    doc_range = jnp.arange(2, dtype=jnp.int32)
    fill_values = []
    insides = []
    for offset in (1, 2, 3):
        earlier_pos = position[None, :] - offset
        insides.append((earlier_pos >= doc_start)[..., None])
        slot_pick = (doc_id[..., None, None] == doc_range[:, None]) & (
            (3 + earlier_pos - doc_start)[..., None, None] == slot_range
        )
        fill_values.append(
            jnp.einsum(
                "btds,bdsc->btc",
                slot_pick.astype(BF16),
                conv_here,
                preferred_element_type=F32,
            )
        )
    conv_value, conv_back = jax.vjp(
        partial(convolve, fill_values=fill_values, insides=insides),
        extended,
        params_all[:, 0:4],
        params_all[:, 4],
    )
    conv_flat = conv_value.reshape(tokens, rec_width)
    conv_low = conv_flat.astype(BF16).reshape(tokens, heads_here, HEAD_DIM)
    gate_mixed = jnp.einsum("nhk,hko->nho", conv_low, gates_all, preferred_element_type=F32)
    pre_rate = gate_mixed[..., :HEAD_DIM].reshape(tokens, rec_width) + params_all[:, 5]
    pre_entry = gate_mixed[..., HEAD_DIM:].reshape(tokens, rec_width) + params_all[:, 6]
    (retain, drive_term), gate_back = jax.vjp(
        gate_math, pre_rate, pre_entry, params_all[:, 7], conv_flat
    )
    reset_rows = (position[None, :] == doc_start)[..., None]
    carried = jnp.where((doc_id == 1)[..., None], state_here[:, None, 1], state_here[:, None, 0])
    retain_rows = retain.reshape(n_streams, n_rows, rec_width)
    retain_eff = jnp.where(reset_rows, 0.0, retain_rows)
    drive_eff = drive_term.reshape(n_streams, n_rows, rec_width) + jnp.where(
        reset_rows, retain_rows * carried, 0.0
    )
    local_keep, local_state = local_scan(retain_eff, drive_eff, False)
    state_before = entering(local_keep[:, -1], local_state[:, -1], False)
    states = local_state + local_keep * state_before[:, None]

    starts_doc = jnp.concatenate([jnp.zeros_like(spans[:, :1]), spans[:, :1]], axis=1)
    stops_doc = starts_doc + lengths
    is_last = position[None, :, None] == (stops_doc - 1)[:, None, :]
    final_part = jnp.sum(jnp.where(is_last[..., None], states[:, :, None, :], 0.0), axis=1)
    tail_pos = stops_doc[..., None] - 3 + slot_range
    from_rows = (position[None, :, None, None] == tail_pos[:, None]) & (
        tail_pos >= starts_doc[..., None]
    )[:, None]
    conv_part = jnp.einsum(
        "btdj,btc->bdjc", from_rows.astype(BF16), source_rows, preferred_element_type=F32
    )
    from_state = (
        (tail_pos < starts_doc[..., None])[..., None]
        & ((lengths[..., None] + slot_range)[..., None] == slot_range)
        & (z_index == 0)
    )
    conv_part = conv_part + jnp.einsum(
        "bdjs,bdsc->bdjc", from_state.astype(BF16), conv_here, preferred_element_type=F32
    )
    finals = jnp.concatenate([final_part[:, :, None], conv_part], axis=2)
    finals = jnp.concatenate(
        [finals[..., :part_width], to_core(finals[..., part_width:])], axis=0
    )
    finals = jnp.where(core == 0, finals, jnp.roll(finals, n_streams, 0))
    finals = lax.all_gather(finals, ("z", "j"), axis=0)
    finals = finals.reshape(z_size, PLANE, all_streams_count, 2, 4, part_width)
    finals = jnp.moveaxis(jnp.sum(finals, axis=0), 0, 3)
    finals = finals.reshape(all_streams_count, 2, 4, half_width)
    dp_index = z_index * PLANE + j_index
    out_width = half_width // (z_size * PLANE)
    finals = lax.dynamic_slice_in_dim(finals, dp_index * out_width, out_width, 3)
    state_block = finals[:, :, 0][:, :, None]
    conv_block = finals[:, :, 1:].astype(BF16)[:, :, :, None]

    states_flat = states.reshape(tokens, rec_width)
    mixed_rows = (states_flat * branch).astype(BF16)
    rec_part = dot(mixed_rows, w_back, 1, 1)
    rec_total = plane_sum(rec_part, n_streams).reshape(own_tokens, model_width)
    hidden_one = flat_in + own_live * rec_total
    normed_two, norm_two_back = jax.vjp(rms_norm, hidden_one, gains_all[1])
    own_second = normed_two.astype(BF16).reshape(n_streams, own_rows, model_width)
    second_low = plane_gather(own_second).reshape(tokens, model_width)

    down_part = second_part = 0.0
    g_narrow, g_wide = [], []
    for h in range(halves):
        both = dot(second_low, w_wide[h], 1, 0)
        activated, mix_back = jax.vjp(mix_gelu, both[:, :ff_part], both[:, ff_part:])
        act_low = activated.astype(BF16)
        down_part = down_part + dot(act_low, w_narrow[h], 1, 1)
        d_act = dot(d_down, w_narrow[h], 1, 0)
        d_both = jnp.concatenate([d.astype(BF16) for d in mix_back(d_act)], axis=1)
        second_part = second_part + dot(d_both, w_wide[h], 1, 1)
        g_narrow.append(dot(d_down, act_low, 0, 0).astype(BF16))
        g_wide.append(dot(second_low, d_both, 0, 0).astype(BF16))

    mlp_total = plane_sum(down_part, n_streams).reshape(own_tokens, model_width)
    out_flat = (hidden_one + own_live * mlp_total).astype(BF16)
    output = all_streams(out_flat.reshape(n_streams, own_rows, model_width))

    second_total = plane_sum(second_part, n_streams).reshape(own_tokens, model_width)
    d_hidden_norm, g_gain_two = norm_two_back(second_total)
    d_hidden = d_out + d_hidden_norm
    own_rec = (d_hidden * own_live).astype(BF16).reshape(n_streams, own_rows, model_width)
    d_rec = plane_gather(own_rec).reshape(tokens, model_width)
    d_rec, g_narrow, g_wide = lax.optimization_barrier((d_rec, g_narrow, g_wide))
    out_wide = collect(*g_wide)
    out_narrow = collect(*g_narrow)
    d_mixed = dot(d_rec, w_back, 1, 0)
    g_back = dot(d_rec, mixed_rows, 0, 0).astype(BF16)

    grad_state = (d_mixed * branch).reshape(n_streams, n_rows, rec_width)
    branch_low = branch_back(d_mixed * states_flat)[0].astype(BF16)
    next_keep = jnp.concatenate([retain_eff[:, 1:], jnp.ones_like(retain_eff[:, :1])], axis=1)
    later_keep, later_sum = local_scan(next_keep, grad_state, True)
    carried_grad = entering(
        retain_eff[:, 0] * later_keep[:, 0], retain_eff[:, 0] * later_sum[:, 0], True
    )
    adjoint = later_sum + later_keep * carried_grad[:, None]
    state_prev = jnp.concatenate([state_before[:, None], states[:, :-1]], axis=1)
    state_prev = jnp.where(reset_rows, carried, state_prev)
    d_retain = (adjoint * state_prev).reshape(tokens, rec_width)
    d_rate, d_entry, g_lam, d_conv_direct = gate_back(
        (d_retain, adjoint.reshape(tokens, rec_width))
    )
    rate_low = d_rate.astype(BF16)
    entry_low = d_entry.astype(BF16)
    grad_gates = jnp.concatenate(
        [
            rate_low.reshape(tokens, heads_here, HEAD_DIM),
            entry_low.reshape(tokens, heads_here, HEAD_DIM),
        ],
        axis=2,
    )
    g_gates = jnp.einsum(
        "nhk,nho->hko", conv_low, grad_gates, preferred_element_type=F32
    ).reshape(rec_width, 2 * HEAD_DIM)
    d_conv_gates = jnp.einsum(
        "nho,hko->nhk", grad_gates, gates_all, preferred_element_type=F32
    ).reshape(tokens, rec_width)
    d_conv = (d_conv_direct + d_conv_gates).reshape(n_streams, n_rows, rec_width)
    d_extended, g_taps, g_conv_bias = conv_back(d_conv)
    rim_grad = shifted(d_extended[:, :3].astype(BF16), -1).astype(F32)
    d_source = jnp.concatenate([d_extended[:, 3:n_rows], d_extended[:, n_rows:] + rim_grad], axis=1)
    d_projected = jnp.concatenate(
        [d_source.reshape(tokens, rec_width).astype(BF16), branch_low], axis=1
    )
    first_part = dot(d_projected, w_rec, 1, 1)
    g_rec = dot(normed_low, d_projected, 0, 0).astype(BF16)
    out_first = collect(
        *(
            jnp.concatenate(
                [
                    g[:, start + h * part_width : start + (h + 1) * part_width]
                    for g, start in ((g_rec, 0), (g_rec, rec_width), (g_back, 0))
                ],
                axis=1,
            )
            for h in range(halves)
        )
    )
    g_small = jnp.concatenate(
        [
            g_taps,
            g_conv_bias[:, None],
            jnp.sum(rate_low.astype(F32), axis=0)[:, None],
            jnp.sum(entry_low.astype(F32), axis=0)[:, None],
            g_lam[:, None],
            g_gates,
        ],
        axis=1,
    ).astype(BF16)
    g_small = g_small[:part_width].astype(F32) + to_core(g_small[part_width:]).astype(F32)
    g_small = lax.psum_scatter(g_small.astype(BF16), "z", scatter_dimension=0, tiled=True)
    route = [(z * PLANE + j, j * z_size + z) for z in range(z_size) for j in range(PLANE)]
    g_small = lax.ppermute(g_small, ("z", "j"), route).astype(F32)[None]

    first_total = plane_sum(first_part, n_streams).reshape(own_tokens, model_width)
    d_input_norm, g_gain_one = norm_one_back(first_total)
    input_grad = all_streams(
        (d_hidden + d_input_norm).astype(BF16).reshape(n_streams, own_rows, model_width)
    )
    g_gains = sum_of_all(jnp.stack([g_gain_one, g_gain_two]))
    g_gains = lax.dynamic_slice_in_dim(g_gains, dp_index * gain_width, gain_width, 1)

    def flat(blocks, start, stop):
        return jnp.concatenate([b[:, start:stop] for b in blocks], axis=1).astype(F32)

    return (
        output,
        input_grad,
        state_block,
        conv_block,
        g_gains,
        flat(out_first, 0, part_width),
        flat(out_first, part_width, 2 * part_width),
        g_small[..., :8],
        g_small[..., 8:],
        flat(out_first, 2 * part_width, 3 * part_width).T,
        flat(out_wide, 0, ff_part),
        flat(out_wide, ff_part, 2 * ff_part),
        flat(out_narrow, 0, ff_part).T,
    )


def solution(mesh):
    devices = mesh.devices.reshape(-1, PLANE, mesh.shape["mp"])
    planes = Mesh(devices, ("z", "j", "c"))
    dp, mp = ("z", "j"), "c"
    return jax.shard_map(
        shards,
        mesh=planes,
        in_specs=(
            P(None, dp, None),
            P(),
            P(),
            P(None, None, mp),
            P(None, None, None, mp),
            P(None, dp),
            P(dp, mp),
            P(dp, mp),
            P(mp, dp, None),
            P(mp, dp, None),
            P(mp, dp),
            P(dp, mp),
            P(dp, mp),
            P(mp, dp),
            P(None, dp, None),
        ),
        out_specs=(
            P(None, dp, None),
            P(None, dp, None),
            P(None, None, mp, dp),
            P(None, None, None, mp, dp),
            P(None, dp),
            P(dp, mp),
            P(dp, mp),
            P(mp, dp, None),
            P(mp, dp, None),
            P(mp, dp),
            P(dp, mp),
            P(dp, mp),
            P(mp, dp),
        ),
        check_vma=False,
    )
```

```python
from functools import partial

import jax
import jax.numpy as jnp
from jax import lax
from jax.experimental import pallas as pl
from jax.experimental.pallas import tpu as pltpu
from jax.sharding import Mesh
from jax.sharding import PartitionSpec as P

HEAD_DIM = 160
PLANE = 4
SEGMENTS = 8
EPSILON = 1e-06
BF16 = jnp.bfloat16
F32 = jnp.float32


def dot(left, right, left_dim, right_dim):
    return lax.dot_general(
        left, right, (((left_dim,), (right_dim,)), ((), ())), preferred_element_type=F32
    )


def to_partner(block, bit):
    return lax.ppermute(block, "j", [(i, i ^ bit) for i in range(PLANE)])


def at(block, index, axis):
    return lax.dynamic_index_in_dim(block, index, axis, keepdims=False)


def put(whole, block, index, axis):
    return lax.dynamic_update_index_in_dim(whole, block, index, axis)


def in_order(found, index):
    low, high = index % 2 == 1, index // 2 == 1
    found = [jnp.where(low, found[k ^ 1], found[k]) for k in range(PLANE)]
    return [jnp.where(high, found[k ^ 2], found[k]) for k in range(PLANE)]


def plane_gather(own):
    mine = lax.axis_index("j")
    streams, rows, width = own.shape
    half = streams // 2
    from_x = to_partner(own, 1)
    from_y = to_partner(own, 2)
    first = to_partner(from_x[:half], 2)
    second = to_partner(from_y[half:], 1)
    whole = jnp.zeros((streams, PLANE, rows, width), own.dtype)
    whole = put(whole, own, mine, 1)
    whole = put(whole, from_x, mine ^ 1, 1)
    whole = put(whole, from_y, mine ^ 2, 1)
    whole = put(whole, jnp.concatenate([first, second], axis=0), mine ^ 3, 1)
    return whole.reshape(streams, PLANE * rows, width)


def plane_sum(part, streams):
    mine = lax.axis_index("j")
    width = part.shape[-1]
    part = part.astype(BF16).reshape(streams, PLANE, -1, width)
    half = streams // 2
    far = at(part, mine ^ 3, 1)
    via_x = to_partner(far[:half], 1).astype(F32)
    via_y = to_partner(far[half:], 2).astype(F32)
    for_x = at(part, mine ^ 1, 1)
    for_y = at(part, mine ^ 2, 1)
    for_x = jnp.concatenate([for_x[:half], (for_x[half:] + via_y).astype(BF16)], axis=0)
    for_y = jnp.concatenate([(for_y[:half] + via_x).astype(BF16), for_y[half:]], axis=0)
    from_x = to_partner(for_x, 1)
    from_y = to_partner(for_y, 2)
    own = at(part, mine, 1)
    return own.astype(F32) + from_x.astype(F32) + from_y.astype(F32)


def plane_swap(blocks):
    mine = lax.axis_index("j")
    found = [at(blocks, mine, 0)]
    found += [to_partner(at(blocks, mine ^ bit, 0), bit) for bit in (1, 2, 3)]
    return in_order(found, mine)


def to_chips(weight):
    rows, columns = weight.shape
    blocks = weight.reshape(rows, PLANE, columns // PLANE)
    return jnp.moveaxis(blocks, 1, 0)


def to_core(block):
    return lax.ppermute(block, "c", [(0, 1), (1, 0)])


def along_z(block):
    own = lax.all_gather(block, "z", axis=0, tiled=True)
    return own, to_core(own)


def both_cores(own, other):
    return (own.astype(F32) + to_core(other).astype(F32)).astype(BF16)


def sum_along_z(total):
    return lax.psum_scatter(total, "z", scatter_dimension=0, tiled=True)


def to_owners(summed):
    return plane_swap(summed.reshape(PLANE, -1, summed.shape[1]))


def z_gather(block):
    size, mine = lax.axis_size("z"), lax.axis_index("z")
    whole = jnp.zeros((size, *block.shape), block.dtype)
    whole = put(whole, block, mine, 0)
    for step in range(1, size):
        got = lax.ppermute(block, "z", [(i, (i + step) % size) for i in range(size)])
        whole = put(whole, got, (mine - step) % size, 0)
    return whole


def sum_of_all(array):
    for axis, pairs in (
        ("c", [(0, 1), (1, 0)]),
        ("j", [(i, i ^ 1) for i in range(PLANE)]),
        ("j", [(i, i ^ 2) for i in range(PLANE)]),
    ):
        array = array + lax.ppermute(array, axis, pairs)
    return jnp.sum(z_gather(array), axis=0)


def with_other_core(array, dim):
    core = lax.axis_index("c")
    count = array.shape[0] // 2
    mine = lax.dynamic_slice_in_dim(array, core * count, count, 0)
    other = lax.dynamic_slice_in_dim(array, (1 - core) * count, count, 0)
    return jnp.concatenate([mine, to_core(other)], axis=dim)


def all_streams(own):
    core = lax.axis_index("c")
    other = to_core(own)
    count = own.shape[0]
    whole = jnp.zeros((2 * count, *own.shape[1:]), own.dtype)
    whole = lax.dynamic_update_slice_in_dim(whole, own, core * count, 0)
    return lax.dynamic_update_slice_in_dim(whole, other, (1 - core) * count, 0)


def shifted(block, distance):
    size = lax.axis_size("z")
    return lax.ppermute(
        block, "z", [(i - distance, i) for i in range(size) if 0 <= i - distance < size]
    )


def entering(keep, state, backward):
    size, mine = lax.axis_size("z"), lax.axis_index("z")
    pair = jnp.stack([keep, state])
    result = jnp.zeros_like(state)
    for distance in range(size - 1, 0, -1):
        got = shifted(pair, -distance if backward else distance)
        there = mine + distance < size if backward else mine >= distance
        result = jnp.where(there, got[0] * result + got[1], result)
    return result


def scan_kernel(backward, keep_ref, add_ref, product_ref, state_ref):
    streams, rows, width = keep_ref.shape
    steps = rows // SEGMENTS
    for s in range(streams):

        def step(number, carry):
            product, state = carry
            place = steps - 1 - number if backward else number
            at_once = pl.ds(place, SEGMENTS, stride=steps)
            keep = keep_ref[s, at_once, :]
            state = keep * state + add_ref[s, at_once, :]
            product = keep * product
            product_ref[s, at_once, :] = product
            state_ref[s, at_once, :] = state
            return product, state

        product, state = lax.fori_loop(
            0,
            steps,
            step,
            (jnp.ones((SEGMENTS, width), F32), jnp.zeros((SEGMENTS, width), F32)),
            unroll=8,
        )
        product_in = jnp.ones((1, width), F32)
        state_in = jnp.zeros((1, width), F32)
        order = range(SEGMENTS - 1, -1, -1) if backward else range(SEGMENTS)
        for k in order:
            here = pl.ds(k * steps, steps)
            local = product_ref[s, here, :]
            state_ref[s, here, :] = state_ref[s, here, :] + local * state_in
            product_ref[s, here, :] = local * product_in
            state_in = product[k : k + 1] * state_in + state[k : k + 1]
            product_in = product[k : k + 1] * product_in


def local_scan(keep, add, backward):
    streams, rows, width = keep.shape
    block = pl.BlockSpec((streams, rows, 128), lambda i: (0, 0, i))
    return pl.pallas_call(
        partial(scan_kernel, backward),
        grid=(width // 128,),
        in_specs=[block, block],
        out_specs=[block, block],
        out_shape=[jax.ShapeDtypeStruct(keep.shape, F32)] * 2,
        compiler_params=pltpu.CompilerParams(vmem_limit_bytes=32 * 1024 * 1024),
        cost_estimate=pl.CostEstimate(
            flops=8 * streams * rows * width,
            bytes_accessed=16 * streams * rows * width,
            transcendentals=0,
        ),
    )(keep, add)


def rms_norm(values, norm_gain):
    factor = lax.rsqrt(jnp.mean(values * values, axis=-1, keepdims=True) + EPSILON)
    return values * factor * norm_gain


def gate_math(pre_rate, pre_entry, lam_param, conv_value):
    rate_gate = jax.nn.sigmoid(pre_rate)
    entry_gate = jax.nn.sigmoid(pre_entry)
    log_decay = -8.0 * rate_gate * jax.nn.softplus(lam_param)
    retain = jnp.exp(log_decay)
    factor = jnp.sqrt(-jnp.expm1(2.0 * log_decay))
    return (retain, factor * entry_gate * conv_value)


def mix_gelu(gate_value, up_value):
    return jax.nn.gelu(gate_value) * up_value


def convolve(extended, conv_taps, conv_bias, fill_values, insides):
    n_rows = extended.shape[1] - 3
    result = conv_bias + conv_taps[:, 0] * extended[:, 3:]
    for offset in (1, 2, 3):
        window = extended[:, 3 - offset : 3 - offset + n_rows]
        result = result + conv_taps[:, offset] * jnp.where(
            insides[offset - 1], window, fill_values[offset - 1]
        )
    return result


def shards(
    inputs,
    doc_spans,
    doc_lengths,
    state_in,
    conv_in,
    norm_gains,
    w_x,
    w_g,
    rec_params,
    gate_weights,
    w_o,
    w_gate,
    w_up,
    w_down,
    cotangent,
):
    all_streams_count, own_rows, model_width = inputs.shape
    halves = lax.axis_size("c")
    z_size = lax.axis_size("z")
    z_index, j_index, core = lax.axis_index("z"), lax.axis_index("j"), lax.axis_index("c")
    n_streams = all_streams_count // halves
    n_rows = own_rows * PLANE
    tokens = n_streams * n_rows
    own_tokens = n_streams * own_rows
    weight_rows = w_x.shape[0]
    half_width = w_x.shape[1]
    part_width = half_width // PLANE
    rec_width = part_width * halves
    heads_here = rec_width // HEAD_DIM
    ff_part = w_gate.shape[1] // PLANE

    first_stream = core * n_streams

    def own_streams(array):
        return lax.dynamic_slice_in_dim(array, first_stream, n_streams, 0)

    spans = own_streams(doc_spans)
    lengths = own_streams(doc_lengths)
    own_in = own_streams(inputs)
    own_cot = own_streams(cotangent)
    small_rows = rec_params.shape[1]
    small = jnp.concatenate([rec_params[0], gate_weights[0]], axis=1)
    small_width = small.shape[1]
    gain_width = norm_gains.shape[1]
    tails = jnp.pad(norm_gains, ((0, 0), (0, small_width - gain_width)))
    small = jnp.concatenate([small, tails], axis=0)

    first_blocks = jnp.concatenate([to_chips(w_x), to_chips(w_g), to_chips(w_o.T)], axis=2)
    first_rows = jnp.concatenate(plane_swap(first_blocks), axis=0)
    first_rows, own_in, small = lax.optimization_barrier((first_rows, own_in, small))
    whole_in = plane_gather(own_in)
    found = [small] + [to_partner(small, bit) for bit in (1, 2, 3)]
    small = z_gather(jnp.stack(in_order(found, j_index)))
    gains_all = jnp.moveaxis(small[:, :, small_rows:, :gain_width], 2, 0)
    gains_all = gains_all.reshape(2, model_width).astype(F32)
    small = small[:, :, :small_rows].reshape(half_width, small_width)
    small = lax.dynamic_slice_in_dim(small, j_index * part_width, part_width, 0)
    small = jnp.concatenate([small, to_core(small)], axis=0)
    params_all = small[:, :8].astype(F32)
    gates_all = small[:, 8:].reshape(heads_here, HEAD_DIM, 2 * HEAD_DIM)

    w_first = along_z(first_rows)
    w_rec = jnp.concatenate(
        [w[:, p * part_width : (p + 1) * part_width] for p in (0, 1) for w in w_first], axis=1
    )
    w_back = jnp.concatenate([w[:, 2 * part_width :] for w in w_first], axis=1)
    later = (w_gate, w_up, w_down)
    later, whole_in, small = lax.optimization_barrier((later, whole_in, small))
    wide_blocks = jnp.concatenate([to_chips(later[0]), to_chips(later[1])], axis=2)
    wide_rows = jnp.concatenate(plane_swap(wide_blocks), axis=0)
    narrow_rows = jnp.concatenate(plane_swap(to_chips(later[2].T)), axis=0)
    own_cot, narrow_rows = lax.optimization_barrier((own_cot, narrow_rows))
    w_wide = along_z(wide_rows)
    narrow_rows, w_wide = lax.optimization_barrier((narrow_rows, w_wide))
    w_narrow = along_z(narrow_rows)

    def live_at(position):
        second_start = spans[:, 0:1]
        doc_id = (position[None, :] >= second_start).astype(jnp.int32)
        doc_start = doc_id * second_start
        doc_stop = doc_start + jnp.where(doc_id == 1, lengths[:, 1:2], lengths[:, 0:1])
        live = (position[None, :] < doc_stop).astype(F32)
        return doc_id, doc_start, live

    own_first = (z_index * PLANE + j_index) * own_rows
    own_live = live_at(own_first + jnp.arange(own_rows, dtype=jnp.int32))[2]
    own_live = own_live.reshape(own_tokens, 1)
    position = z_index * n_rows + jnp.arange(n_rows, dtype=jnp.int32)
    doc_id, doc_start, _ = live_at(position)

    d_out = own_cot.reshape(own_tokens, model_width).astype(F32)
    own_down = (d_out * own_live).astype(BF16).reshape(n_streams, own_rows, model_width)
    d_down = plane_gather(own_down).reshape(tokens, model_width)

    flat_in = own_in.reshape(own_tokens, model_width).astype(F32)
    _, norm_one_back = jax.vjp(rms_norm, flat_in, gains_all[0])
    normed_low = rms_norm(
        whole_in.reshape(tokens, model_width).astype(F32), gains_all[0]
    ).astype(BF16)
    projected = dot(normed_low, w_rec, 1, 0)
    source_rows = projected[:, :rec_width].astype(BF16).reshape(n_streams, n_rows, rec_width)
    branch, branch_back = jax.vjp(jax.nn.gelu, projected[:, rec_width:])
    rim_rows = shifted(source_rows[:, n_rows - 3 :], 1)
    extended = jnp.concatenate([rim_rows, source_rows], axis=1).astype(F32)

    conv_here = with_other_core(
        lax.dynamic_slice_in_dim(conv_in, j_index * part_width, part_width, 3), 3
    )
    state_here = with_other_core(
        lax.dynamic_slice_in_dim(state_in, j_index * part_width, part_width, 2), 2
    )
    slot_range = jnp.arange(3, dtype=jnp.int32)
    doc_range = jnp.arange(2, dtype=jnp.int32)
    fill_values = []
    insides = []
    for offset in (1, 2, 3):
        earlier_pos = position[None, :] - offset
        insides.append((earlier_pos >= doc_start)[..., None])
        slot_pick = (doc_id[..., None, None] == doc_range[:, None]) & (
            (3 + earlier_pos - doc_start)[..., None, None] == slot_range
        )
        fill_values.append(
            jnp.einsum(
                "btds,bdsc->btc",
                slot_pick.astype(BF16),
                conv_here,
                preferred_element_type=F32,
            )
        )
    conv_value, conv_back = jax.vjp(
        partial(convolve, fill_values=fill_values, insides=insides),
        extended,
        params_all[:, 0:4],
        params_all[:, 4],
    )
    conv_flat = conv_value.reshape(tokens, rec_width)
    conv_low = conv_flat.astype(BF16).reshape(tokens, heads_here, HEAD_DIM)
    gate_mixed = jnp.einsum("nhk,hko->nho", conv_low, gates_all, preferred_element_type=F32)
    pre_rate = gate_mixed[..., :HEAD_DIM].reshape(tokens, rec_width) + params_all[:, 5]
    pre_entry = gate_mixed[..., HEAD_DIM:].reshape(tokens, rec_width) + params_all[:, 6]
    (retain, drive_term), gate_back = jax.vjp(
        gate_math, pre_rate, pre_entry, params_all[:, 7], conv_flat
    )
    reset_rows = (position[None, :] == doc_start)[..., None]
    carried = jnp.where((doc_id == 1)[..., None], state_here[:, None, 1], state_here[:, None, 0])
    retain_rows = retain.reshape(n_streams, n_rows, rec_width)
    retain_eff = jnp.where(reset_rows, 0.0, retain_rows)
    drive_eff = drive_term.reshape(n_streams, n_rows, rec_width) + jnp.where(
        reset_rows, retain_rows * carried, 0.0
    )
    local_keep, local_state = local_scan(retain_eff, drive_eff, False)
    state_before = entering(local_keep[:, -1], local_state[:, -1], False)
    states = local_state + local_keep * state_before[:, None]

    starts_doc = jnp.concatenate([jnp.zeros_like(spans[:, :1]), spans[:, :1]], axis=1)
    stops_doc = starts_doc + lengths
    is_last = position[None, :, None] == (stops_doc - 1)[:, None, :]
    final_part = jnp.sum(jnp.where(is_last[..., None], states[:, :, None, :], 0.0), axis=1)
    tail_pos = stops_doc[..., None] - 3 + slot_range
    from_rows = (position[None, :, None, None] == tail_pos[:, None]) & (
        tail_pos >= starts_doc[..., None]
    )[:, None]
    conv_part = jnp.einsum(
        "btdj,btc->bdjc", from_rows.astype(BF16), source_rows, preferred_element_type=F32
    )
    from_state = (
        (tail_pos < starts_doc[..., None])[..., None]
        & ((lengths[..., None] + slot_range)[..., None] == slot_range)
        & (z_index == 0)
    )
    conv_part = conv_part + jnp.einsum(
        "bdjs,bdsc->bdjc", from_state.astype(BF16), conv_here, preferred_element_type=F32
    )
    state_high = lax.reduce_precision(final_part, exponent_bits=8, mantissa_bits=7)
    finals = jnp.stack([state_high, final_part - state_high], axis=2)
    finals = jnp.concatenate([finals, conv_part], axis=2).reshape(-1, rec_width)
    columns = finals.shape[0]
    finals = lax.dynamic_update_slice_in_dim(
        jnp.zeros((rec_width, halves * columns), F32), finals.T, core * columns, 1
    )
    dp_index = z_index * PLANE + j_index

    states_flat = states.reshape(tokens, rec_width)
    mixed_rows = (states_flat * branch).astype(BF16)
    rec_part = dot(mixed_rows, w_back, 1, 1)
    rec_total = plane_sum(rec_part, n_streams).reshape(own_tokens, model_width)
    hidden_one = flat_in + own_live * rec_total
    normed_two, norm_two_back = jax.vjp(rms_norm, hidden_one, gains_all[1])
    own_second = normed_two.astype(BF16).reshape(n_streams, own_rows, model_width)
    second_low = plane_gather(own_second).reshape(tokens, model_width)

    down_part = second_part = 0.0
    g_narrow, g_wide = [], []
    for h in range(halves):
        both = dot(second_low, w_wide[h], 1, 0)
        activated, mix_back = jax.vjp(mix_gelu, both[:, :ff_part], both[:, ff_part:])
        act_low = activated.astype(BF16)
        down_part = down_part + dot(act_low, w_narrow[h], 1, 1)
        d_act = dot(d_down, w_narrow[h], 1, 0)
        d_both = jnp.concatenate([d.astype(BF16) for d in mix_back(d_act)], axis=1)
        second_part = second_part + dot(d_both, w_wide[h], 1, 1)
        g_narrow.append(dot(d_down, act_low, 0, 0).astype(BF16))
        g_wide.append(dot(second_low, d_both, 0, 0).astype(BF16))

    mlp_total = plane_sum(down_part, n_streams).reshape(own_tokens, model_width)
    out_flat = (hidden_one + own_live * mlp_total).astype(BF16)
    output = all_streams(out_flat.reshape(n_streams, own_rows, model_width))

    second_total = plane_sum(second_part, n_streams).reshape(own_tokens, model_width)
    d_hidden_norm, g_gain_two = norm_two_back(second_total)
    d_hidden = d_out + d_hidden_norm
    own_rec = (d_hidden * own_live).astype(BF16).reshape(n_streams, own_rows, model_width)
    d_rec = plane_gather(own_rec).reshape(tokens, model_width)
    d_rec, g_narrow, g_wide = lax.optimization_barrier((d_rec, g_narrow, g_wide))
    sum_wide, sum_narrow = both_cores(*g_wide), both_cores(*g_narrow)
    d_mixed = dot(d_rec, w_back, 1, 0)
    d_mixed, sum_wide, sum_narrow = lax.optimization_barrier((d_mixed, sum_wide, sum_narrow))
    sum_wide = sum_along_z(sum_wide)
    g_back = dot(d_rec, mixed_rows, 0, 0).astype(BF16)

    grad_state = (d_mixed * branch).reshape(n_streams, n_rows, rec_width)
    branch_low = branch_back(d_mixed * states_flat)[0].astype(BF16)
    next_keep = jnp.concatenate([retain_eff[:, 1:], jnp.ones_like(retain_eff[:, :1])], axis=1)
    later_keep, later_sum = local_scan(next_keep, grad_state, True)
    carried_grad = entering(
        retain_eff[:, 0] * later_keep[:, 0], retain_eff[:, 0] * later_sum[:, 0], True
    )
    adjoint = later_sum + later_keep * carried_grad[:, None]
    state_prev = jnp.concatenate([state_before[:, None], states[:, :-1]], axis=1)
    state_prev = jnp.where(reset_rows, carried, state_prev)
    d_retain = (adjoint * state_prev).reshape(tokens, rec_width)
    d_rate, d_entry, g_lam, d_conv_direct = gate_back(
        (d_retain, adjoint.reshape(tokens, rec_width))
    )
    rate_low = d_rate.astype(BF16)
    entry_low = d_entry.astype(BF16)
    grad_gates = jnp.concatenate(
        [
            rate_low.reshape(tokens, heads_here, HEAD_DIM),
            entry_low.reshape(tokens, heads_here, HEAD_DIM),
        ],
        axis=2,
    )
    g_gates = jnp.einsum(
        "nhk,nho->hko", conv_low, grad_gates, preferred_element_type=F32
    ).reshape(rec_width, 2 * HEAD_DIM)
    d_conv_gates = jnp.einsum(
        "nho,hko->nhk", grad_gates, gates_all, preferred_element_type=F32
    ).reshape(tokens, rec_width)
    d_conv = (d_conv_direct + d_conv_gates).reshape(n_streams, n_rows, rec_width)
    d_conv, sum_wide, sum_narrow = lax.optimization_barrier((d_conv, sum_wide, sum_narrow))
    sum_narrow = sum_along_z(sum_narrow)
    out_wide = to_owners(sum_wide)
    d_extended, g_taps, g_conv_bias = conv_back(d_conv)
    rim_grad = shifted(d_extended[:, :3].astype(BF16), -1).astype(F32)
    d_source = jnp.concatenate([d_extended[:, 3:n_rows], d_extended[:, n_rows:] + rim_grad], axis=1)
    d_projected = jnp.concatenate(
        [d_source.reshape(tokens, rec_width).astype(BF16), branch_low], axis=1
    )
    first_part = dot(d_projected, w_rec, 1, 1)
    g_rec = dot(normed_low, d_projected, 0, 0).astype(BF16)
    sum_first = both_cores(
        *(
            jnp.concatenate(
                [
                    g[:, start + h * part_width : start + (h + 1) * part_width]
                    for g, start in ((g_rec, 0), (g_rec, rec_width), (g_back, 0))
                ],
                axis=1,
            )
            for h in range(halves)
        )
    )
    g_small = jnp.concatenate(
        [
            g_taps,
            g_conv_bias[:, None],
            jnp.sum(rate_low.astype(F32), axis=0)[:, None],
            jnp.sum(entry_low.astype(F32), axis=0)[:, None],
            g_lam[:, None],
            g_gates,
            finals,
        ],
        axis=1,
    ).astype(BF16)
    sum_small = both_cores(g_small[:part_width], g_small[part_width:])
    sum_small, sum_first, sum_narrow = lax.optimization_barrier((sum_small, sum_first, sum_narrow))
    out_narrow = to_owners(sum_narrow)
    sum_first = sum_along_z(sum_first)
    out_first = to_owners(sum_first)
    g_small = sum_along_z(sum_small)
    route = [(z * PLANE + j, j * z_size + z) for z in range(z_size) for j in range(PLANE)]
    g_small = lax.ppermute(g_small, ("z", "j"), route).astype(F32)
    g_params = g_small[None, :, :8]
    g_gates = g_small[None, :, 8 : 8 + 2 * HEAD_DIM]
    finals = g_small[:, 8 + 2 * HEAD_DIM :].T.reshape(all_streams_count, 2, 5, -1)
    state_block = (finals[:, :, 0] + finals[:, :, 1])[:, :, None]
    conv_block = finals[:, :, 2:].astype(BF16)[:, :, :, None]

    first_total = plane_sum(first_part, n_streams).reshape(own_tokens, model_width)
    d_input_norm, g_gain_one = norm_one_back(first_total)
    input_grad = all_streams(
        (d_hidden + d_input_norm).astype(BF16).reshape(n_streams, own_rows, model_width)
    )
    g_gains = sum_of_all(jnp.stack([g_gain_one, g_gain_two]))
    g_gains = lax.dynamic_slice_in_dim(g_gains, dp_index * gain_width, gain_width, 1)

    def flat(blocks, start, stop):
        return jnp.concatenate([b[:, start:stop] for b in blocks], axis=1).astype(F32)

    return (
        output,
        input_grad,
        state_block,
        conv_block,
        g_gains,
        flat(out_first, 0, part_width),
        flat(out_first, part_width, 2 * part_width),
        g_params,
        g_gates,
        flat(out_first, 2 * part_width, 3 * part_width).T,
        flat(out_wide, 0, ff_part),
        flat(out_wide, ff_part, 2 * ff_part),
        flat(out_narrow, 0, ff_part).T,
    )


def solution(mesh):
    devices = mesh.devices.reshape(-1, PLANE, mesh.shape["mp"])
    planes = Mesh(devices, ("z", "j", "c"))
    dp, mp = ("z", "j"), "c"
    return jax.shard_map(
        shards,
        mesh=planes,
        in_specs=(
            P(None, dp, None),
            P(),
            P(),
            P(None, None, mp),
            P(None, None, None, mp),
            P(None, dp),
            P(dp, mp),
            P(dp, mp),
            P(mp, dp, None),
            P(mp, dp, None),
            P(mp, dp),
            P(dp, mp),
            P(dp, mp),
            P(mp, dp),
            P(None, dp, None),
        ),
        out_specs=(
            P(None, dp, None),
            P(None, dp, None),
            P(None, None, mp, dp),
            P(None, None, None, mp, dp),
            P(None, dp),
            P(dp, mp),
            P(dp, mp),
            P(mp, dp, None),
            P(mp, dp, None),
            P(mp, dp),
            P(dp, mp),
            P(dp, mp),
            P(mp, dp),
        ),
        check_vma=False,
    )
```

```python
from functools import partial

import jax
import jax.numpy as jnp
from jax import lax
from jax.experimental import pallas as pl
from jax.experimental.pallas import tpu as pltpu
from jax.sharding import Mesh
from jax.sharding import PartitionSpec as P

HEAD_DIM = 160
PLANE = 4
SEGMENTS = 8
EPSILON = 1e-06
BF16 = jnp.bfloat16
F32 = jnp.float32


def dot(left, right, left_dim, right_dim):
    return lax.dot_general(
        left, right, (((left_dim,), (right_dim,)), ((), ())), preferred_element_type=F32
    )


def to_partner(block, bit):
    return lax.ppermute(block, "j", [(i, i ^ bit) for i in range(PLANE)])


def at(block, index, axis):
    return lax.dynamic_index_in_dim(block, index, axis, keepdims=False)


def put(whole, block, index, axis):
    return lax.dynamic_update_index_in_dim(whole, block, index, axis)


def in_order(found, index):
    low, high = index % 2 == 1, index // 2 == 1
    found = [jnp.where(low, found[k ^ 1], found[k]) for k in range(PLANE)]
    return [jnp.where(high, found[k ^ 2], found[k]) for k in range(PLANE)]


def plane_gather(own):
    mine = lax.axis_index("j")
    streams, rows, width = own.shape
    half = streams // 2
    from_x = to_partner(own, 1)
    from_y = to_partner(own, 2)
    first = to_partner(from_x[:half], 2)
    second = to_partner(from_y[half:], 1)
    whole = jnp.zeros((streams, PLANE, rows, width), own.dtype)
    whole = put(whole, own, mine, 1)
    whole = put(whole, from_x, mine ^ 1, 1)
    whole = put(whole, from_y, mine ^ 2, 1)
    whole = put(whole, jnp.concatenate([first, second], axis=0), mine ^ 3, 1)
    return whole.reshape(streams, PLANE * rows, width)


def plane_sum(part, streams):
    mine = lax.axis_index("j")
    width = part.shape[-1]
    part = part.astype(BF16).reshape(streams, PLANE, -1, width)
    half = streams // 2
    far = at(part, mine ^ 3, 1)
    via_x = to_partner(far[:half], 1).astype(F32)
    via_y = to_partner(far[half:], 2).astype(F32)
    for_x = at(part, mine ^ 1, 1)
    for_y = at(part, mine ^ 2, 1)
    for_x = jnp.concatenate([for_x[:half], (for_x[half:] + via_y).astype(BF16)], axis=0)
    for_y = jnp.concatenate([(for_y[:half] + via_x).astype(BF16), for_y[half:]], axis=0)
    from_x = to_partner(for_x, 1)
    from_y = to_partner(for_y, 2)
    own = at(part, mine, 1)
    return own.astype(F32) + from_x.astype(F32) + from_y.astype(F32)


def plane_swap(blocks):
    mine = lax.axis_index("j")
    found = [at(blocks, mine, 0)]
    found += [to_partner(at(blocks, mine ^ bit, 0), bit) for bit in (1, 2, 3)]
    return in_order(found, mine)


def to_chips(weight):
    rows, columns = weight.shape
    blocks = weight.reshape(rows, PLANE, columns // PLANE)
    return jnp.moveaxis(blocks, 1, 0)


def to_core(block):
    return lax.ppermute(block, "c", [(0, 1), (1, 0)])


def along_z(block):
    own = lax.all_gather(block, "z", axis=0, tiled=True)
    return own, to_core(own)


def both_cores(own, other):
    return (own.astype(F32) + to_core(other).astype(F32)).astype(BF16)


def sum_along_z(total):
    return lax.psum_scatter(total, "z", scatter_dimension=0, tiled=True)


def to_owners(summed):
    return plane_swap(summed.reshape(PLANE, -1, summed.shape[1]))


def z_gather(block):
    size, mine = lax.axis_size("z"), lax.axis_index("z")
    whole = jnp.zeros((size, *block.shape), block.dtype)
    whole = put(whole, block, mine, 0)
    for step in range(1, size):
        got = lax.ppermute(block, "z", [(i, (i + step) % size) for i in range(size)])
        whole = put(whole, got, (mine - step) % size, 0)
    return whole


def sum_of_all(array):
    for axis, pairs in (
        ("c", [(0, 1), (1, 0)]),
        ("j", [(i, i ^ 1) for i in range(PLANE)]),
        ("j", [(i, i ^ 2) for i in range(PLANE)]),
    ):
        array = array + lax.ppermute(array, axis, pairs)
    return jnp.sum(z_gather(array), axis=0)


def with_other_core(array, dim):
    core = lax.axis_index("c")
    count = array.shape[0] // 2
    mine = lax.dynamic_slice_in_dim(array, core * count, count, 0)
    other = lax.dynamic_slice_in_dim(array, (1 - core) * count, count, 0)
    return jnp.concatenate([mine, to_core(other)], axis=dim)


def all_streams(own):
    core = lax.axis_index("c")
    other = to_core(own)
    count = own.shape[0]
    whole = jnp.zeros((2 * count, *own.shape[1:]), own.dtype)
    whole = lax.dynamic_update_slice_in_dim(whole, own, core * count, 0)
    return lax.dynamic_update_slice_in_dim(whole, other, (1 - core) * count, 0)


def shifted(block, distance):
    size = lax.axis_size("z")
    return lax.ppermute(
        block, "z", [(i - distance, i) for i in range(size) if 0 <= i - distance < size]
    )


def entering(keep, state, backward):
    size, mine = lax.axis_size("z"), lax.axis_index("z")
    pair = jnp.stack([keep, state])
    result = jnp.zeros_like(state)
    for distance in range(size - 1, 0, -1):
        got = shifted(pair, -distance if backward else distance)
        there = mine + distance < size if backward else mine >= distance
        result = jnp.where(there, got[0] * result + got[1], result)
    return result


def scan_kernel(backward, keep_ref, add_ref, product_ref, state_ref):
    streams, rows, width = keep_ref.shape
    steps = rows // SEGMENTS
    for s in range(streams):

        def step(number, carry):
            product, state = carry
            place = steps - 1 - number if backward else number
            at_once = pl.ds(place, SEGMENTS, stride=steps)
            keep = keep_ref[s, at_once, :]
            state = keep * state + add_ref[s, at_once, :]
            product = keep * product
            product_ref[s, at_once, :] = product
            state_ref[s, at_once, :] = state
            return product, state

        product, state = lax.fori_loop(
            0,
            steps,
            step,
            (jnp.ones((SEGMENTS, width), F32), jnp.zeros((SEGMENTS, width), F32)),
            unroll=8,
        )
        product_in = jnp.ones((1, width), F32)
        state_in = jnp.zeros((1, width), F32)
        order = range(SEGMENTS - 1, -1, -1) if backward else range(SEGMENTS)
        for k in order:
            here = pl.ds(k * steps, steps)
            local = product_ref[s, here, :]
            state_ref[s, here, :] = state_ref[s, here, :] + local * state_in
            product_ref[s, here, :] = local * product_in
            state_in = product[k : k + 1] * state_in + state[k : k + 1]
            product_in = product[k : k + 1] * product_in


def local_scan(keep, add, backward):
    streams, rows, width = keep.shape
    block = pl.BlockSpec((streams, rows, 128), lambda i: (0, 0, i))
    return pl.pallas_call(
        partial(scan_kernel, backward),
        grid=(width // 128,),
        in_specs=[block, block],
        out_specs=[block, block],
        out_shape=[jax.ShapeDtypeStruct(keep.shape, F32)] * 2,
        compiler_params=pltpu.CompilerParams(vmem_limit_bytes=32 * 1024 * 1024),
        cost_estimate=pl.CostEstimate(
            flops=8 * streams * rows * width,
            bytes_accessed=16 * streams * rows * width,
            transcendentals=0,
        ),
    )(keep, add)


def rms_norm(values, norm_gain):
    factor = lax.rsqrt(jnp.mean(values * values, axis=-1, keepdims=True) + EPSILON)
    return values * factor * norm_gain


def gate_math(pre_rate, pre_entry, lam_param, conv_value):
    rate_gate = jax.nn.sigmoid(pre_rate)
    entry_gate = jax.nn.sigmoid(pre_entry)
    log_decay = -8.0 * rate_gate * jax.nn.softplus(lam_param)
    retain = jnp.exp(log_decay)
    factor = jnp.sqrt(-jnp.expm1(2.0 * log_decay))
    return (retain, factor * entry_gate * conv_value)


def mix_gelu(gate_value, up_value):
    return jax.nn.gelu(gate_value) * up_value


def convolve(extended, conv_taps, conv_bias, fill_values, insides):
    n_rows = extended.shape[1] - 3
    result = conv_bias + conv_taps[:, 0] * extended[:, 3:]
    for offset in (1, 2, 3):
        window = extended[:, 3 - offset : 3 - offset + n_rows]
        result = result + conv_taps[:, offset] * jnp.where(
            insides[offset - 1], window, fill_values[offset - 1]
        )
    return result


def shards(
    inputs,
    doc_spans,
    doc_lengths,
    state_in,
    conv_in,
    norm_gains,
    w_x,
    w_g,
    rec_params,
    gate_weights,
    w_o,
    w_gate,
    w_up,
    w_down,
    cotangent,
):
    all_streams_count, own_rows, model_width = inputs.shape
    halves = lax.axis_size("c")
    z_size = lax.axis_size("z")
    z_index, j_index, core = lax.axis_index("z"), lax.axis_index("j"), lax.axis_index("c")
    n_streams = all_streams_count // halves
    n_rows = own_rows * PLANE
    tokens = n_streams * n_rows
    own_tokens = n_streams * own_rows
    weight_rows = w_x.shape[0]
    half_width = w_x.shape[1]
    part_width = half_width // PLANE
    rec_width = part_width * halves
    heads_here = rec_width // HEAD_DIM
    ff_part = w_gate.shape[1] // PLANE

    first_stream = core * n_streams

    def own_streams(array):
        return lax.dynamic_slice_in_dim(array, first_stream, n_streams, 0)

    spans = own_streams(doc_spans)
    lengths = own_streams(doc_lengths)
    own_in = own_streams(inputs)
    own_cot = own_streams(cotangent)
    small_rows = rec_params.shape[1]
    small = jnp.concatenate([rec_params[0], gate_weights[0]], axis=1)
    small_width = small.shape[1]
    gain_width = norm_gains.shape[1]
    tails = jnp.pad(norm_gains, ((0, 0), (0, small_width - gain_width)))
    small = jnp.concatenate([small, tails], axis=0)

    small = z_gather(small)
    first_blocks = jnp.concatenate([to_chips(w_x), to_chips(w_g), to_chips(w_o.T)], axis=2)
    first_blocks, small = lax.optimization_barrier((first_blocks, small))
    first_rows = jnp.concatenate(plane_swap(first_blocks), axis=0)
    first_rows, own_in, small = lax.optimization_barrier((first_rows, own_in, small))
    gain_rows = jnp.broadcast_to(
        small[:, small_rows:].reshape(1, 2 * z_size, small_width),
        (PLANE, 2 * z_size, small_width),
    )
    small_blocks = small[:, :small_rows].reshape(PLANE, -1, small_width)
    small = jnp.stack(plane_swap(jnp.concatenate([small_blocks, gain_rows], axis=1)))
    whole_in = plane_gather(own_in)
    gains_all = small[:, part_width // PLANE :, :gain_width].reshape(PLANE, z_size, 2, gain_width)
    gains_all = jnp.moveaxis(gains_all, (0, 1, 2), (2, 1, 0))
    gains_all = gains_all.reshape(2, model_width).astype(F32)
    small = small[:, : part_width // PLANE].reshape(PLANE, -1, small_rows, small_width)
    small = jnp.moveaxis(small, 0, 1).reshape(part_width, small_width)
    small = jnp.concatenate([small, to_core(small)], axis=0)
    params_all = small[:, :8].astype(F32)
    head = jnp.arange(rec_width, dtype=jnp.int32) // HEAD_DIM
    gates_all = jnp.concatenate(
        [
            jnp.where(
                head[:, None] == head[None, :],
                jnp.tile(small[:, start : start + HEAD_DIM], (1, heads_here)),
                0.0,
            ).astype(BF16)
            for start in (8, 8 + HEAD_DIM)
        ],
        axis=1,
    )

    w_first = along_z(first_rows)
    w_rec = jnp.concatenate(
        [w[:, p * part_width : (p + 1) * part_width] for p in (0, 1) for w in w_first], axis=1
    )
    w_back = jnp.concatenate([w[:, 2 * part_width :] for w in w_first], axis=1)
    later = (w_gate, w_up, w_down)
    later, whole_in = lax.optimization_barrier((later, whole_in))
    wide_blocks = jnp.concatenate([to_chips(later[0]), to_chips(later[1])], axis=2)
    wide_rows = jnp.concatenate(plane_swap(wide_blocks), axis=0)
    narrow_rows = jnp.concatenate(plane_swap(to_chips(later[2].T)), axis=0)
    own_cot, narrow_rows = lax.optimization_barrier((own_cot, narrow_rows))
    w_wide = along_z(wide_rows)
    narrow_rows, wide_own = lax.optimization_barrier((narrow_rows, w_wide[0]))
    w_wide = (wide_own, w_wide[1])
    w_narrow = along_z(narrow_rows)

    def live_at(position):
        second_start = spans[:, 0:1]
        doc_id = (position[None, :] >= second_start).astype(jnp.int32)
        doc_start = doc_id * second_start
        doc_stop = doc_start + jnp.where(doc_id == 1, lengths[:, 1:2], lengths[:, 0:1])
        live = (position[None, :] < doc_stop).astype(F32)
        return doc_id, doc_start, live

    own_first = (z_index * PLANE + j_index) * own_rows
    own_live = live_at(own_first + jnp.arange(own_rows, dtype=jnp.int32))[2]
    own_live = own_live.reshape(own_tokens, 1)
    position = z_index * n_rows + jnp.arange(n_rows, dtype=jnp.int32)
    doc_id, doc_start, _ = live_at(position)

    d_out = own_cot.reshape(own_tokens, model_width).astype(F32)
    own_down = (d_out * own_live).astype(BF16).reshape(n_streams, own_rows, model_width)
    d_down = plane_gather(own_down).reshape(tokens, model_width)

    flat_in = own_in.reshape(own_tokens, model_width).astype(F32)
    _, norm_one_back = jax.vjp(rms_norm, flat_in, gains_all[0])
    normed_low = rms_norm(
        whole_in.reshape(tokens, model_width).astype(F32), gains_all[0]
    ).astype(BF16)
    projected = dot(normed_low, w_rec, 1, 0)
    source_rows = projected[:, :rec_width].astype(BF16).reshape(n_streams, n_rows, rec_width)
    branch, branch_back = jax.vjp(jax.nn.gelu, projected[:, rec_width:])
    rim_rows = shifted(source_rows[:, n_rows - 3 :], 1)
    extended = jnp.concatenate([rim_rows, source_rows], axis=1).astype(F32)

    conv_here = with_other_core(
        lax.dynamic_slice_in_dim(conv_in, j_index * part_width, part_width, 3), 3
    )
    state_here = with_other_core(
        lax.dynamic_slice_in_dim(state_in, j_index * part_width, part_width, 2), 2
    )
    slot_range = jnp.arange(3, dtype=jnp.int32)
    doc_range = jnp.arange(2, dtype=jnp.int32)
    fill_values = []
    insides = []
    for offset in (1, 2, 3):
        earlier_pos = position[None, :] - offset
        insides.append((earlier_pos >= doc_start)[..., None])
        slot_pick = (doc_id[..., None, None] == doc_range[:, None]) & (
            (3 + earlier_pos - doc_start)[..., None, None] == slot_range
        )
        fill_values.append(
            jnp.einsum(
                "btds,bdsc->btc",
                slot_pick.astype(BF16),
                conv_here,
                preferred_element_type=F32,
            )
        )
    conv_value, conv_back = jax.vjp(
        partial(convolve, fill_values=fill_values, insides=insides),
        extended,
        params_all[:, 0:4],
        params_all[:, 4],
    )
    conv_flat = conv_value.reshape(tokens, rec_width)
    conv_low = conv_flat.astype(BF16)
    gate_mixed = dot(conv_low, gates_all, 1, 0)
    pre_rate = gate_mixed[:, :rec_width] + params_all[:, 5]
    pre_entry = gate_mixed[:, rec_width:] + params_all[:, 6]
    (retain, drive_term), gate_back = jax.vjp(
        gate_math, pre_rate, pre_entry, params_all[:, 7], conv_flat
    )
    reset_rows = (position[None, :] == doc_start)[..., None]
    carried = jnp.where((doc_id == 1)[..., None], state_here[:, None, 1], state_here[:, None, 0])
    retain_rows = retain.reshape(n_streams, n_rows, rec_width)
    retain_eff = jnp.where(reset_rows, 0.0, retain_rows)
    drive_eff = drive_term.reshape(n_streams, n_rows, rec_width) + jnp.where(
        reset_rows, retain_rows * carried, 0.0
    )
    local_keep, local_state = local_scan(retain_eff, drive_eff, False)
    state_before = entering(local_keep[:, -1], local_state[:, -1], False)
    states = local_state + local_keep * state_before[:, None]

    starts_doc = jnp.concatenate([jnp.zeros_like(spans[:, :1]), spans[:, :1]], axis=1)
    stops_doc = starts_doc + lengths
    is_last = position[None, :, None] == (stops_doc - 1)[:, None, :]
    final_part = jnp.sum(jnp.where(is_last[..., None], states[:, :, None, :], 0.0), axis=1)
    tail_pos = stops_doc[..., None] - 3 + slot_range
    from_rows = (position[None, :, None, None] == tail_pos[:, None]) & (
        tail_pos >= starts_doc[..., None]
    )[:, None]
    conv_part = jnp.einsum(
        "btdj,btc->bdjc", from_rows.astype(BF16), source_rows, preferred_element_type=F32
    )
    from_state = (
        (tail_pos < starts_doc[..., None])[..., None]
        & ((lengths[..., None] + slot_range)[..., None] == slot_range)
        & (z_index == 0)
    )
    conv_part = conv_part + jnp.einsum(
        "bdjs,bdsc->bdjc", from_state.astype(BF16), conv_here, preferred_element_type=F32
    )
    state_high = lax.reduce_precision(final_part, exponent_bits=8, mantissa_bits=7)
    finals = jnp.stack([state_high, final_part - state_high], axis=2)
    finals = jnp.concatenate([finals, conv_part], axis=2).reshape(-1, rec_width)
    columns = finals.shape[0]
    finals = lax.dynamic_update_slice_in_dim(
        jnp.zeros((rec_width, halves * columns), F32), finals.T, core * columns, 1
    )
    dp_index = z_index * PLANE + j_index

    states_flat = states.reshape(tokens, rec_width)
    mixed_rows = (states_flat * branch).astype(BF16)
    rec_part = dot(mixed_rows, w_back, 1, 1)
    rec_total = plane_sum(rec_part, n_streams).reshape(own_tokens, model_width)
    hidden_one = flat_in + own_live * rec_total
    normed_two, norm_two_back = jax.vjp(rms_norm, hidden_one, gains_all[1])
    own_second = normed_two.astype(BF16).reshape(n_streams, own_rows, model_width)
    second_low = plane_gather(own_second).reshape(tokens, model_width)

    down_part = second_part = 0.0
    g_narrow, g_wide = [], []
    for h in range(halves):
        both = dot(second_low, w_wide[h], 1, 0)
        activated, mix_back = jax.vjp(mix_gelu, both[:, :ff_part], both[:, ff_part:])
        act_low = activated.astype(BF16)
        down_part = down_part + dot(act_low, w_narrow[h], 1, 1)
        d_act = dot(d_down, w_narrow[h], 1, 0)
        d_both = jnp.concatenate([d.astype(BF16) for d in mix_back(d_act)], axis=1)
        second_part = second_part + dot(d_both, w_wide[h], 1, 1)
        g_narrow.append(dot(d_down, act_low, 0, 0).astype(BF16))
        g_wide.append(dot(second_low, d_both, 0, 0).astype(BF16))

    mlp_total = plane_sum(down_part, n_streams).reshape(own_tokens, model_width)
    out_flat = (hidden_one + own_live * mlp_total).astype(BF16)
    output = all_streams(out_flat.reshape(n_streams, own_rows, model_width))

    second_total = plane_sum(second_part, n_streams).reshape(own_tokens, model_width)
    d_hidden_norm, g_gain_two = norm_two_back(second_total)
    d_hidden = d_out + d_hidden_norm
    own_rec = (d_hidden * own_live).astype(BF16).reshape(n_streams, own_rows, model_width)
    d_rec = plane_gather(own_rec).reshape(tokens, model_width)
    d_rec, g_narrow, g_wide = lax.optimization_barrier((d_rec, g_narrow, g_wide))
    sum_wide, sum_narrow = both_cores(*g_wide), both_cores(*g_narrow)
    d_mixed = dot(d_rec, w_back, 1, 0)
    d_mixed, sum_wide, sum_narrow = lax.optimization_barrier((d_mixed, sum_wide, sum_narrow))
    sum_wide = sum_along_z(sum_wide)
    g_back = dot(d_rec, mixed_rows, 0, 0).astype(BF16)

    grad_state = (d_mixed * branch).reshape(n_streams, n_rows, rec_width)
    branch_low = branch_back(d_mixed * states_flat)[0].astype(BF16)
    next_keep = jnp.concatenate([retain_eff[:, 1:], jnp.ones_like(retain_eff[:, :1])], axis=1)
    later_keep, later_sum = local_scan(next_keep, grad_state, True)
    carried_grad = entering(
        retain_eff[:, 0] * later_keep[:, 0], retain_eff[:, 0] * later_sum[:, 0], True
    )
    adjoint = later_sum + later_keep * carried_grad[:, None]
    state_prev = jnp.concatenate([state_before[:, None], states[:, :-1]], axis=1)
    state_prev = jnp.where(reset_rows, carried, state_prev)
    d_retain = (adjoint * state_prev).reshape(tokens, rec_width)
    d_rate, d_entry, g_lam, d_conv_direct = gate_back(
        (d_retain, adjoint.reshape(tokens, rec_width))
    )
    rate_low = d_rate.astype(BF16)
    entry_low = d_entry.astype(BF16)
    grad_gates = jnp.concatenate([rate_low, entry_low], axis=1)
    g_gates = dot(conv_low, grad_gates, 0, 0)
    g_gates = jnp.concatenate(
        [
            jnp.concatenate(
                [
                    g_gates[
                        h * HEAD_DIM : (h + 1) * HEAD_DIM,
                        start + h * HEAD_DIM : start + (h + 1) * HEAD_DIM,
                    ]
                    for start in (0, rec_width)
                ],
                axis=1,
            )
            for h in range(heads_here)
        ],
        axis=0,
    )
    d_conv_gates = dot(grad_gates, gates_all, 1, 1)
    d_conv = (d_conv_direct + d_conv_gates).reshape(n_streams, n_rows, rec_width)
    d_conv, sum_wide, sum_narrow = lax.optimization_barrier((d_conv, sum_wide, sum_narrow))
    sum_narrow = sum_along_z(sum_narrow)
    out_wide = to_owners(sum_wide)
    d_extended, g_taps, g_conv_bias = conv_back(d_conv)
    rim_grad = shifted(d_extended[:, :3].astype(BF16), -1).astype(F32)
    d_source = jnp.concatenate([d_extended[:, 3:n_rows], d_extended[:, n_rows:] + rim_grad], axis=1)
    d_projected = jnp.concatenate(
        [d_source.reshape(tokens, rec_width).astype(BF16), branch_low], axis=1
    )
    first_part = dot(d_projected, w_rec, 1, 1)
    g_rec = dot(normed_low, d_projected, 0, 0).astype(BF16)
    sum_first = both_cores(
        *(
            jnp.concatenate(
                [
                    g[:, start + h * part_width : start + (h + 1) * part_width]
                    for g, start in ((g_rec, 0), (g_rec, rec_width), (g_back, 0))
                ],
                axis=1,
            )
            for h in range(halves)
        )
    )
    g_small = jnp.concatenate(
        [
            g_taps,
            g_conv_bias[:, None],
            jnp.sum(rate_low.astype(F32), axis=0)[:, None],
            jnp.sum(entry_low.astype(F32), axis=0)[:, None],
            g_lam[:, None],
            g_gates,
            finals,
        ],
        axis=1,
    ).astype(BF16)
    sum_small = both_cores(g_small[:part_width], g_small[part_width:])
    sum_small, sum_first, sum_narrow = lax.optimization_barrier((sum_small, sum_first, sum_narrow))
    out_narrow = to_owners(sum_narrow)
    sum_first = sum_along_z(sum_first)
    out_first = to_owners(sum_first)
    g_small = sum_along_z(sum_small)
    route = [(z * PLANE + j, j * z_size + z) for z in range(z_size) for j in range(PLANE)]
    g_small = lax.ppermute(g_small, ("z", "j"), route).astype(F32)
    g_params = g_small[None, :, :8]
    g_gates = g_small[None, :, 8 : 8 + 2 * HEAD_DIM]
    finals = g_small[:, 8 + 2 * HEAD_DIM :].T.reshape(all_streams_count, 2, 5, -1)
    state_block = (finals[:, :, 0] + finals[:, :, 1])[:, :, None]
    conv_block = finals[:, :, 2:].astype(BF16)[:, :, :, None]

    first_total = plane_sum(first_part, n_streams).reshape(own_tokens, model_width)
    d_input_norm, g_gain_one = norm_one_back(first_total)
    input_grad = all_streams(
        (d_hidden + d_input_norm).astype(BF16).reshape(n_streams, own_rows, model_width)
    )
    g_gains = sum_of_all(jnp.stack([g_gain_one, g_gain_two]))
    g_gains = lax.dynamic_slice_in_dim(g_gains, dp_index * gain_width, gain_width, 1)

    def flat(blocks, start, stop):
        return jnp.concatenate([b[:, start:stop] for b in blocks], axis=1).astype(F32)

    return (
        output,
        input_grad,
        state_block,
        conv_block,
        g_gains,
        flat(out_first, 0, part_width),
        flat(out_first, part_width, 2 * part_width),
        g_params,
        g_gates,
        flat(out_first, 2 * part_width, 3 * part_width).T,
        flat(out_wide, 0, ff_part),
        flat(out_wide, ff_part, 2 * ff_part),
        flat(out_narrow, 0, ff_part).T,
    )


def solution(mesh):
    devices = mesh.devices.reshape(-1, PLANE, mesh.shape["mp"])
    planes = Mesh(devices, ("z", "j", "c"))
    dp, mp = ("z", "j"), "c"
    return jax.shard_map(
        shards,
        mesh=planes,
        in_specs=(
            P(None, dp, None),
            P(),
            P(),
            P(None, None, mp),
            P(None, None, None, mp),
            P(None, dp),
            P(dp, mp),
            P(dp, mp),
            P(mp, dp, None),
            P(mp, dp, None),
            P(mp, dp),
            P(dp, mp),
            P(dp, mp),
            P(mp, dp),
            P(None, dp, None),
        ),
        out_specs=(
            P(None, dp, None),
            P(None, dp, None),
            P(None, None, mp, dp),
            P(None, None, None, mp, dp),
            P(None, dp),
            P(dp, mp),
            P(dp, mp),
            P(mp, dp, None),
            P(mp, dp, None),
            P(mp, dp),
            P(dp, mp),
            P(dp, mp),
            P(mp, dp),
        ),
        check_vma=False,
    )
```

```python
from functools import partial

import jax
import jax.numpy as jnp
from jax import lax
from jax.experimental import pallas as pl
from jax.experimental.pallas import tpu as pltpu
from jax.sharding import Mesh
from jax.sharding import PartitionSpec as P

HEAD_DIM = 160
PLANE = 4
SEGMENTS = 8
EPSILON = 1e-06
BF16 = jnp.bfloat16
F32 = jnp.float32


def dot(left, right, left_dim, right_dim):
    return lax.dot_general(
        left, right, (((left_dim,), (right_dim,)), ((), ())), preferred_element_type=F32
    )


def to_partner(block, bit):
    return lax.ppermute(block, "j", [(i, i ^ bit) for i in range(PLANE)])


def at(block, index, axis):
    return lax.dynamic_index_in_dim(block, index, axis, keepdims=False)


def put(whole, block, index, axis):
    return lax.dynamic_update_index_in_dim(whole, block, index, axis)


def in_order(found, index):
    low, high = index % 2 == 1, index // 2 == 1
    found = [jnp.where(low, found[k ^ 1], found[k]) for k in range(PLANE)]
    return [jnp.where(high, found[k ^ 2], found[k]) for k in range(PLANE)]


def plane_gather(own):
    mine = lax.axis_index("j")
    streams, rows, width = own.shape
    half = streams // 2
    from_x = to_partner(own, 1)
    from_y = to_partner(own, 2)
    first = to_partner(from_x[:half], 2)
    second = to_partner(from_y[half:], 1)
    whole = jnp.zeros((streams, PLANE, rows, width), own.dtype)
    whole = put(whole, own, mine, 1)
    whole = put(whole, from_x, mine ^ 1, 1)
    whole = put(whole, from_y, mine ^ 2, 1)
    whole = put(whole, jnp.concatenate([first, second], axis=0), mine ^ 3, 1)
    return whole.reshape(streams, PLANE * rows, width)


def plane_sum_first(part, streams):
    mine = lax.axis_index("j")
    part = part.astype(BF16).reshape(streams, PLANE, -1, part.shape[-1])
    far = at(part, mine ^ 3, 1)
    half = streams // 2
    return part, to_partner(far[:half], 1), to_partner(far[half:], 2)


def plane_sum_second(state):
    part, via_x, via_y = state
    mine = lax.axis_index("j")
    half = via_x.shape[0]
    for_x = at(part, mine ^ 1, 1)
    for_y = at(part, mine ^ 2, 1)
    for_x = jnp.concatenate(
        [for_x[:half], (for_x[half:].astype(F32) + via_y.astype(F32)).astype(BF16)], axis=0
    )
    for_y = jnp.concatenate(
        [(for_y[:half].astype(F32) + via_x.astype(F32)).astype(BF16), for_y[half:]], axis=0
    )
    from_x = to_partner(for_x, 1)
    from_y = to_partner(for_y, 2)
    own = at(part, mine, 1)
    return own.astype(F32) + from_x.astype(F32) + from_y.astype(F32)


def plane_sum(part, streams):
    return plane_sum_second(plane_sum_first(part, streams))


def plane_swap(blocks):
    mine = lax.axis_index("j")
    found = [at(blocks, mine, 0)]
    found += [to_partner(at(blocks, mine ^ bit, 0), bit) for bit in (1, 2, 3)]
    return in_order(found, mine)


def to_chips(weight):
    rows, columns = weight.shape
    blocks = weight.reshape(rows, PLANE, columns // PLANE)
    return jnp.moveaxis(blocks, 1, 0)


def to_core(block):
    return lax.ppermute(block, "c", [(0, 1), (1, 0)])


def along_z(block):
    own = lax.all_gather(block, "z", axis=0, tiled=True)
    return own, to_core(own)


def both_cores(own, other):
    return (own.astype(F32) + to_core(other).astype(F32)).astype(BF16)


def sum_along_z(total):
    return lax.psum_scatter(total, "z", scatter_dimension=0, tiled=True)


def sent_along_z(total):
    size, mine = lax.axis_size("z"), lax.axis_index("z")
    rows = total.reshape(size, -1, total.shape[1])
    result = at(rows, mine, 0).astype(F32)
    for step in range(1, size):
        route = [(i, (i + step) % size) for i in range(size)]
        result += lax.ppermute(at(rows, (mine + step) % size, 0), "z", route).astype(F32)
    return result


def to_owners(summed):
    return plane_swap(summed.reshape(PLANE, -1, summed.shape[1]))


def z_gather(block):
    size, mine = lax.axis_size("z"), lax.axis_index("z")
    whole = jnp.zeros((size, *block.shape), block.dtype)
    whole = put(whole, block, mine, 0)
    for step in range(1, size):
        got = lax.ppermute(block, "z", [(i, (i + step) % size) for i in range(size)])
        whole = put(whole, got, (mine - step) % size, 0)
    return whole


def sum_of_all(array):
    for axis, pairs in (
        ("c", [(0, 1), (1, 0)]),
        ("j", [(i, i ^ 1) for i in range(PLANE)]),
        ("j", [(i, i ^ 2) for i in range(PLANE)]),
    ):
        array = array + lax.ppermute(array, axis, pairs)
    return jnp.sum(z_gather(array), axis=0)


def with_other_core(array, dim):
    core = lax.axis_index("c")
    count = array.shape[0] // 2
    mine = lax.dynamic_slice_in_dim(array, core * count, count, 0)
    other = lax.dynamic_slice_in_dim(array, (1 - core) * count, count, 0)
    return jnp.concatenate([mine, to_core(other)], axis=dim)


def all_streams(own):
    core = lax.axis_index("c")
    other = to_core(own)
    count = own.shape[0]
    whole = jnp.zeros((2 * count, *own.shape[1:]), own.dtype)
    whole = lax.dynamic_update_slice_in_dim(whole, own, core * count, 0)
    return lax.dynamic_update_slice_in_dim(whole, other, (1 - core) * count, 0)


def shifted(block, distance):
    size = lax.axis_size("z")
    return lax.ppermute(
        block, "z", [(i - distance, i) for i in range(size) if 0 <= i - distance < size]
    )


def entering(keep, state, backward):
    size, mine = lax.axis_size("z"), lax.axis_index("z")
    pair = jnp.stack([keep, state])
    result = jnp.zeros_like(state)
    for distance in range(size - 1, 0, -1):
        got = shifted(pair, -distance if backward else distance)
        there = mine + distance < size if backward else mine >= distance
        result = jnp.where(there, got[0] * result + got[1], result)
    return result


def scan_kernel(backward, keep_ref, add_ref, product_ref, state_ref):
    streams, rows, width = keep_ref.shape
    steps = rows // SEGMENTS
    for s in range(streams):

        def step(number, carry):
            product, state = carry
            place = steps - 1 - number if backward else number
            at_once = pl.ds(place, SEGMENTS, stride=steps)
            keep = keep_ref[s, at_once, :]
            state = keep * state + add_ref[s, at_once, :]
            product = keep * product
            product_ref[s, at_once, :] = product
            state_ref[s, at_once, :] = state
            return product, state

        product, state = lax.fori_loop(
            0,
            steps,
            step,
            (jnp.ones((SEGMENTS, width), F32), jnp.zeros((SEGMENTS, width), F32)),
            unroll=8,
        )
        product_in = jnp.ones((1, width), F32)
        state_in = jnp.zeros((1, width), F32)
        order = range(SEGMENTS - 1, -1, -1) if backward else range(SEGMENTS)
        for k in order:
            here = pl.ds(k * steps, steps)
            local = product_ref[s, here, :]
            state_ref[s, here, :] = state_ref[s, here, :] + local * state_in
            product_ref[s, here, :] = local * product_in
            state_in = product[k : k + 1] * state_in + state[k : k + 1]
            product_in = product[k : k + 1] * product_in


def local_scan(keep, add, backward):
    streams, rows, width = keep.shape
    block = pl.BlockSpec((streams, rows, 128), lambda i: (0, 0, i))
    return pl.pallas_call(
        partial(scan_kernel, backward),
        grid=(width // 128,),
        in_specs=[block, block],
        out_specs=[block, block],
        out_shape=[jax.ShapeDtypeStruct(keep.shape, F32)] * 2,
        compiler_params=pltpu.CompilerParams(vmem_limit_bytes=32 * 1024 * 1024),
        cost_estimate=pl.CostEstimate(
            flops=8 * streams * rows * width,
            bytes_accessed=16 * streams * rows * width,
            transcendentals=0,
        ),
    )(keep, add)


def rms_norm(values, norm_gain):
    factor = lax.rsqrt(jnp.mean(values * values, axis=-1, keepdims=True) + EPSILON)
    return values * factor * norm_gain


def gate_math(pre_rate, pre_entry, lam_param, conv_value):
    rate_gate = jax.nn.sigmoid(pre_rate)
    entry_gate = jax.nn.sigmoid(pre_entry)
    log_decay = -8.0 * rate_gate * jax.nn.softplus(lam_param)
    retain = jnp.exp(log_decay)
    factor = jnp.sqrt(-jnp.expm1(2.0 * log_decay))
    return (retain, factor * entry_gate * conv_value)


def mix_gelu(gate_value, up_value):
    return jax.nn.gelu(gate_value) * up_value


def convolve(extended, conv_taps, conv_bias, fill_values, insides):
    n_rows = extended.shape[1] - 3
    result = conv_bias + conv_taps[:, 0] * extended[:, 3:]
    for offset in (1, 2, 3):
        window = extended[:, 3 - offset : 3 - offset + n_rows]
        result = result + conv_taps[:, offset] * jnp.where(
            insides[offset - 1], window, fill_values[offset - 1]
        )
    return result


def shards(
    inputs,
    doc_spans,
    doc_lengths,
    state_in,
    conv_in,
    norm_gains,
    w_x,
    w_g,
    rec_params,
    gate_weights,
    w_o,
    w_gate,
    w_up,
    w_down,
    cotangent,
):
    all_streams_count, own_rows, model_width = inputs.shape
    halves = lax.axis_size("c")
    z_size = lax.axis_size("z")
    z_index, j_index, core = lax.axis_index("z"), lax.axis_index("j"), lax.axis_index("c")
    n_streams = all_streams_count // halves
    n_rows = own_rows * PLANE
    tokens = n_streams * n_rows
    own_tokens = n_streams * own_rows
    weight_rows = w_x.shape[0]
    half_width = w_x.shape[1]
    part_width = half_width // PLANE
    rec_width = part_width * halves
    heads_here = rec_width // HEAD_DIM
    ff_part = w_gate.shape[1] // PLANE

    first_stream = core * n_streams

    def own_streams(array):
        return lax.dynamic_slice_in_dim(array, first_stream, n_streams, 0)

    spans = own_streams(doc_spans)
    lengths = own_streams(doc_lengths)
    own_in = own_streams(inputs)
    own_cot = own_streams(cotangent)
    small_rows = rec_params.shape[1]
    small = jnp.concatenate([rec_params[0], gate_weights[0]], axis=1)
    small_width = small.shape[1]
    gain_width = norm_gains.shape[1]
    tails = jnp.pad(norm_gains, ((0, 0), (0, small_width - gain_width)))
    small = jnp.concatenate([small, tails], axis=0)

    first_blocks = jnp.concatenate([to_chips(w_x), to_chips(w_g), to_chips(w_o.T)], axis=2)
    first_rows = jnp.concatenate(plane_swap(first_blocks), axis=0)
    small = z_gather(small)
    later = (w_gate, w_up, w_down)
    first_rows, own_in, small, later = lax.optimization_barrier((first_rows, own_in, small, later))
    gain_rows = jnp.broadcast_to(
        small[:, small_rows:].reshape(1, 2 * z_size, small_width),
        (PLANE, 2 * z_size, small_width),
    )
    small_blocks = small[:, :small_rows].reshape(PLANE, -1, small_width)
    small = jnp.stack(plane_swap(jnp.concatenate([small_blocks, gain_rows], axis=1)))
    whole_in = plane_gather(own_in)
    gains_all = small[:, part_width // PLANE :, :gain_width].reshape(PLANE, z_size, 2, gain_width)
    gains_all = jnp.moveaxis(gains_all, (0, 1, 2), (2, 1, 0))
    gains_all = gains_all.reshape(2, model_width).astype(F32)
    small = small[:, : part_width // PLANE].reshape(PLANE, -1, small_rows, small_width)
    small = jnp.moveaxis(small, 0, 1).reshape(part_width, small_width)
    small = jnp.concatenate([small, to_core(small)], axis=0)
    params_all = small[:, :8].astype(F32)
    head = jnp.arange(rec_width, dtype=jnp.int32) // HEAD_DIM
    gates_all = jnp.concatenate(
        [
            jnp.where(
                head[:, None] == head[None, :],
                jnp.tile(small[:, start : start + HEAD_DIM], (1, heads_here)),
                0.0,
            ).astype(BF16)
            for start in (8, 8 + HEAD_DIM)
        ],
        axis=1,
    )

    wide_blocks = jnp.concatenate([to_chips(later[0]), to_chips(later[1])], axis=2)
    wide_rows = jnp.concatenate(plane_swap(wide_blocks), axis=0)
    narrow_rows = jnp.concatenate(plane_swap(to_chips(later[2].T)), axis=0)
    own_cot, narrow_rows = lax.optimization_barrier((own_cot, narrow_rows))

    def live_at(position):
        second_start = spans[:, 0:1]
        doc_id = (position[None, :] >= second_start).astype(jnp.int32)
        doc_start = doc_id * second_start
        doc_stop = doc_start + jnp.where(doc_id == 1, lengths[:, 1:2], lengths[:, 0:1])
        live = (position[None, :] < doc_stop).astype(F32)
        return doc_id, doc_start, live

    own_first = (z_index * PLANE + j_index) * own_rows
    own_live = live_at(own_first + jnp.arange(own_rows, dtype=jnp.int32))[2]
    own_live = own_live.reshape(own_tokens, 1)
    position = z_index * n_rows + jnp.arange(n_rows, dtype=jnp.int32)
    doc_id, doc_start, _ = live_at(position)

    d_out = own_cot.reshape(own_tokens, model_width).astype(F32)
    own_down = (d_out * own_live).astype(BF16).reshape(n_streams, own_rows, model_width)
    d_down = plane_gather(own_down).reshape(tokens, model_width)

    flat_in = own_in.reshape(own_tokens, model_width).astype(F32)
    _, norm_one_back = jax.vjp(rms_norm, flat_in, gains_all[0])
    normed_low = rms_norm(
        whole_in.reshape(tokens, model_width).astype(F32), gains_all[0]
    ).astype(BF16)
    first_own, normed_low, wide_rows = lax.optimization_barrier(
        (lax.all_gather(first_rows, "z", axis=0, tiled=True), normed_low, wide_rows)
    )
    wide_own = lax.all_gather(wide_rows, "z", axis=0, tiled=True)
    w_first = (first_own, to_core(first_own))
    w_rec = jnp.concatenate(
        [w[:, p * part_width : (p + 1) * part_width] for p in (0, 1) for w in w_first], axis=1
    )
    w_back = jnp.concatenate([w[:, 2 * part_width :] for w in w_first], axis=1)
    projected = dot(normed_low, w_rec, 1, 0)
    source_rows = projected[:, :rec_width].astype(BF16).reshape(n_streams, n_rows, rec_width)
    branch, branch_back = jax.vjp(jax.nn.gelu, projected[:, rec_width:])
    rim_rows = shifted(source_rows[:, n_rows - 3 :], 1)
    extended = jnp.concatenate([rim_rows, source_rows], axis=1).astype(F32)

    conv_here = with_other_core(
        lax.dynamic_slice_in_dim(conv_in, j_index * part_width, part_width, 3), 3
    )
    state_here = with_other_core(
        lax.dynamic_slice_in_dim(state_in, j_index * part_width, part_width, 2), 2
    )
    slot_range = jnp.arange(3, dtype=jnp.int32)
    doc_range = jnp.arange(2, dtype=jnp.int32)
    fill_values = []
    insides = []
    for offset in (1, 2, 3):
        earlier_pos = position[None, :] - offset
        insides.append((earlier_pos >= doc_start)[..., None])
        slot_pick = (doc_id[..., None, None] == doc_range[:, None]) & (
            (3 + earlier_pos - doc_start)[..., None, None] == slot_range
        )
        fill_values.append(
            jnp.einsum(
                "btds,bdsc->btc",
                slot_pick.astype(BF16),
                conv_here,
                preferred_element_type=F32,
            )
        )
    conv_value, conv_back = jax.vjp(
        partial(convolve, fill_values=fill_values, insides=insides),
        extended,
        params_all[:, 0:4],
        params_all[:, 4],
    )
    conv_flat = conv_value.reshape(tokens, rec_width)
    conv_low = conv_flat.astype(BF16)
    gate_mixed = dot(conv_low, gates_all, 1, 0)
    pre_rate = gate_mixed[:, :rec_width] + params_all[:, 5]
    pre_entry = gate_mixed[:, rec_width:] + params_all[:, 6]
    (retain, drive_term), gate_back = jax.vjp(
        gate_math, pre_rate, pre_entry, params_all[:, 7], conv_flat
    )
    reset_rows = (position[None, :] == doc_start)[..., None]
    carried = jnp.where((doc_id == 1)[..., None], state_here[:, None, 1], state_here[:, None, 0])
    retain_rows = retain.reshape(n_streams, n_rows, rec_width)
    retain_eff = jnp.where(reset_rows, 0.0, retain_rows)
    drive_eff = drive_term.reshape(n_streams, n_rows, rec_width) + jnp.where(
        reset_rows, retain_rows * carried, 0.0
    )
    local_keep, local_state = local_scan(retain_eff, drive_eff, False)
    state_before = entering(local_keep[:, -1], local_state[:, -1], False)
    states = local_state + local_keep * state_before[:, None]

    starts_doc = jnp.concatenate([jnp.zeros_like(spans[:, :1]), spans[:, :1]], axis=1)
    stops_doc = starts_doc + lengths
    is_last = position[None, :, None] == (stops_doc - 1)[:, None, :]
    final_part = jnp.sum(jnp.where(is_last[..., None], states[:, :, None, :], 0.0), axis=1)
    tail_pos = stops_doc[..., None] - 3 + slot_range
    from_rows = (position[None, :, None, None] == tail_pos[:, None]) & (
        tail_pos >= starts_doc[..., None]
    )[:, None]
    conv_part = jnp.einsum(
        "btdj,btc->bdjc", from_rows.astype(BF16), source_rows, preferred_element_type=F32
    )
    from_state = (
        (tail_pos < starts_doc[..., None])[..., None]
        & ((lengths[..., None] + slot_range)[..., None] == slot_range)
        & (z_index == 0)
    )
    conv_part = conv_part + jnp.einsum(
        "bdjs,bdsc->bdjc", from_state.astype(BF16), conv_here, preferred_element_type=F32
    )
    state_high = lax.reduce_precision(final_part, exponent_bits=8, mantissa_bits=7)
    finals = jnp.stack([state_high, final_part - state_high], axis=2)
    finals = jnp.concatenate([finals, conv_part], axis=2).reshape(-1, rec_width)
    columns = finals.shape[0]
    finals = lax.dynamic_update_slice_in_dim(
        jnp.zeros((rec_width, halves * columns), F32), finals.T, core * columns, 1
    )
    dp_index = z_index * PLANE + j_index

    states_flat = states.reshape(tokens, rec_width)
    mixed_rows = (states_flat * branch).astype(BF16)
    rec_part = dot(mixed_rows, w_back, 1, 1)
    rec_total, wide_own, narrow_rows = lax.optimization_barrier(
        (plane_sum(rec_part, n_streams), wide_own, narrow_rows)
    )
    rec_total = rec_total.reshape(own_tokens, model_width)
    w_wide = (wide_own, to_core(wide_own))
    w_narrow = along_z(narrow_rows)
    hidden_one = flat_in + own_live * rec_total
    normed_two, norm_two_back = jax.vjp(rms_norm, hidden_one, gains_all[1])
    own_second = normed_two.astype(BF16).reshape(n_streams, own_rows, model_width)
    second_low = plane_gather(own_second).reshape(tokens, model_width)

    second_part = 0.0
    hidden, g_narrow, g_wide = [], [], []
    for h in range(halves):
        both = dot(second_low, w_wide[h], 1, 0)
        activated, mix_back = jax.vjp(mix_gelu, both[:, :ff_part], both[:, ff_part:])
        act_low = activated.astype(BF16)
        hidden.append((act_low, mix_back))
        g_narrow.append(dot(d_down, act_low, 0, 0).astype(BF16))
    sum_narrow = both_cores(*g_narrow)
    for h, (act_low, mix_back) in enumerate(hidden):
        d_act = dot(d_down, w_narrow[h], 1, 0)
        d_both = jnp.concatenate([d.astype(BF16) for d in mix_back(d_act)], axis=1)
        second_part = second_part + dot(d_both, w_wide[h], 1, 1)
        g_wide.append(dot(second_low, d_both, 0, 0).astype(BF16))
    second_part, sum_narrow = lax.optimization_barrier((second_part, sum_narrow))
    sum_narrow = sum_along_z(sum_narrow)

    second_total = plane_sum(second_part, n_streams).reshape(own_tokens, model_width)
    d_hidden_norm, g_gain_two = norm_two_back(second_total)
    d_hidden = d_out + d_hidden_norm
    own_rec = (d_hidden * own_live).astype(BF16).reshape(n_streams, own_rows, model_width)
    d_rec = plane_gather(own_rec).reshape(tokens, model_width)
    d_rec, g_wide, sum_narrow = lax.optimization_barrier((d_rec, g_wide, sum_narrow))
    sum_wide = both_cores(*g_wide)
    d_mixed = dot(d_rec, w_back, 1, 0)
    acts = [act_low for act_low, _ in hidden]
    d_mixed, sum_wide, sum_narrow, acts = lax.optimization_barrier(
        (d_mixed, sum_wide, sum_narrow, acts)
    )
    down_part = sum(dot(act_low, w, 1, 1) for act_low, w in zip(acts, w_narrow))
    mlp_sum = plane_sum_first(down_part, n_streams)
    sum_wide = sum_along_z(sum_wide)
    g_back = dot(d_rec, mixed_rows, 0, 0).astype(BF16)

    grad_state = (d_mixed * branch).reshape(n_streams, n_rows, rec_width)
    branch_low = branch_back(d_mixed * states_flat)[0].astype(BF16)
    next_keep = jnp.concatenate([retain_eff[:, 1:], jnp.ones_like(retain_eff[:, :1])], axis=1)
    later_keep, later_sum = local_scan(next_keep, grad_state, True)
    later_sum, mlp_sum = lax.optimization_barrier((later_sum, mlp_sum))
    mlp_sum = plane_sum_second(mlp_sum)
    out_narrow = to_owners(sum_narrow)
    carried_grad = entering(
        retain_eff[:, 0] * later_keep[:, 0], retain_eff[:, 0] * later_sum[:, 0], True
    )
    adjoint = later_sum + later_keep * carried_grad[:, None]
    state_prev = jnp.concatenate([state_before[:, None], states[:, :-1]], axis=1)
    state_prev = jnp.where(reset_rows, carried, state_prev)
    d_retain = (adjoint * state_prev).reshape(tokens, rec_width)
    d_rate, d_entry, g_lam, d_conv_direct = gate_back(
        (d_retain, adjoint.reshape(tokens, rec_width))
    )
    rate_low = d_rate.astype(BF16)
    entry_low = d_entry.astype(BF16)
    grad_gates = jnp.concatenate([rate_low, entry_low], axis=1)
    g_gates = dot(conv_low, grad_gates, 0, 0)
    g_gates = jnp.concatenate(
        [
            jnp.concatenate(
                [
                    g_gates[
                        h * HEAD_DIM : (h + 1) * HEAD_DIM,
                        start + h * HEAD_DIM : start + (h + 1) * HEAD_DIM,
                    ]
                    for start in (0, rec_width)
                ],
                axis=1,
            )
            for h in range(heads_here)
        ],
        axis=0,
    )
    grad_gates, mlp_total, out_narrow = lax.optimization_barrier((grad_gates, mlp_sum, out_narrow))
    mlp_total = mlp_total.reshape(own_tokens, model_width)
    out_flat = (hidden_one + own_live * mlp_total).astype(BF16)
    output = all_streams(out_flat.reshape(n_streams, own_rows, model_width))

    d_conv_gates = dot(grad_gates, gates_all, 1, 1)
    d_conv = (d_conv_direct + d_conv_gates).reshape(n_streams, n_rows, rec_width)
    d_extended, g_taps, g_conv_bias = conv_back(d_conv)
    rim_grad = shifted(d_extended[:, :3].astype(BF16), -1).astype(F32)
    d_source = jnp.concatenate([d_extended[:, 3:n_rows], d_extended[:, n_rows:] + rim_grad], axis=1)
    d_projected = jnp.concatenate(
        [d_source.reshape(tokens, rec_width).astype(BF16), branch_low], axis=1
    )
    first_part = dot(d_projected, w_rec, 1, 1)
    g_rec = dot(normed_low, d_projected, 0, 0).astype(BF16)
    sum_first = both_cores(
        *(
            jnp.concatenate(
                [
                    g[:, start + h * part_width : start + (h + 1) * part_width]
                    for g, start in ((g_rec, 0), (g_rec, rec_width), (g_back, 0))
                ],
                axis=1,
            )
            for h in range(halves)
        )
    )
    g_small = jnp.concatenate(
        [
            g_taps,
            g_conv_bias[:, None],
            jnp.sum(rate_low.astype(F32), axis=0)[:, None],
            jnp.sum(entry_low.astype(F32), axis=0)[:, None],
            g_lam[:, None],
            g_gates,
            finals,
        ],
        axis=1,
    ).astype(BF16)
    sum_small = both_cores(g_small[:part_width], g_small[part_width:])
    first_part, sum_first, sum_wide = lax.optimization_barrier((first_part, sum_first, sum_wide))
    out_wide = to_owners(sum_wide)
    sum_first = sum_along_z(sum_first)
    out_first = to_owners(sum_first)
    g_small = sent_along_z(sum_small)
    route = [(z * PLANE + j, j * z_size + z) for z in range(z_size) for j in range(PLANE)]
    g_small = lax.ppermute(g_small.astype(BF16), ("z", "j"), route).astype(F32)
    g_params = g_small[None, :, :8]
    g_gates = g_small[None, :, 8 : 8 + 2 * HEAD_DIM]
    finals = g_small[:, 8 + 2 * HEAD_DIM :].T.reshape(all_streams_count, 2, 5, -1)
    state_block = (finals[:, :, 0] + finals[:, :, 1])[:, :, None]
    conv_block = finals[:, :, 2:].astype(BF16)[:, :, :, None]

    first_total = plane_sum(first_part, n_streams).reshape(own_tokens, model_width)
    d_input_norm, g_gain_one = norm_one_back(first_total)
    input_grad = all_streams(
        (d_hidden + d_input_norm).astype(BF16).reshape(n_streams, own_rows, model_width)
    )
    g_gains = sum_of_all(jnp.stack([g_gain_one, g_gain_two]))
    g_gains = lax.dynamic_slice_in_dim(g_gains, dp_index * gain_width, gain_width, 1)

    def flat(blocks, start, stop):
        return jnp.concatenate([b[:, start:stop] for b in blocks], axis=1).astype(F32)

    return (
        output,
        input_grad,
        state_block,
        conv_block,
        g_gains,
        flat(out_first, 0, part_width),
        flat(out_first, part_width, 2 * part_width),
        g_params,
        g_gates,
        flat(out_first, 2 * part_width, 3 * part_width).T,
        flat(out_wide, 0, ff_part),
        flat(out_wide, ff_part, 2 * ff_part),
        flat(out_narrow, 0, ff_part).T,
    )


def solution(mesh):
    devices = mesh.devices.reshape(-1, PLANE, mesh.shape["mp"])
    planes = Mesh(devices, ("z", "j", "c"))
    dp, mp = ("z", "j"), "c"
    return jax.shard_map(
        shards,
        mesh=planes,
        in_specs=(
            P(None, dp, None),
            P(),
            P(),
            P(None, None, mp),
            P(None, None, None, mp),
            P(None, dp),
            P(dp, mp),
            P(dp, mp),
            P(mp, dp, None),
            P(mp, dp, None),
            P(mp, dp),
            P(dp, mp),
            P(dp, mp),
            P(mp, dp),
            P(None, dp, None),
        ),
        out_specs=(
            P(None, dp, None),
            P(None, dp, None),
            P(None, None, mp, dp),
            P(None, None, None, mp, dp),
            P(None, dp),
            P(dp, mp),
            P(dp, mp),
            P(mp, dp, None),
            P(mp, dp, None),
            P(mp, dp),
            P(dp, mp),
            P(dp, mp),
            P(mp, dp),
        ),
        check_vma=False,
    )
```

```python
from functools import partial

import jax
import jax.numpy as jnp
from jax import lax
from jax.experimental import pallas as pl
from jax.experimental.pallas import tpu as pltpu
from jax.sharding import Mesh
from jax.sharding import PartitionSpec as P

HEAD_DIM = 160
PLANE = 4
SEGMENTS = 8
EPSILON = 1e-06
BF16 = jnp.bfloat16
F32 = jnp.float32


def dot(left, right, left_dim, right_dim):
    return lax.dot_general(
        left, right, (((left_dim,), (right_dim,)), ((), ())), preferred_element_type=F32
    )


def to_partner(block, bit):
    return lax.ppermute(block, "j", [(i, i ^ bit) for i in range(PLANE)])


def at(block, index, axis):
    return lax.dynamic_index_in_dim(block, index, axis, keepdims=False)


def put(whole, block, index, axis):
    return lax.dynamic_update_index_in_dim(whole, block, index, axis)


def in_order(found, index):
    low, high = index % 2 == 1, index // 2 == 1
    found = [jnp.where(low, found[k ^ 1], found[k]) for k in range(PLANE)]
    return [jnp.where(high, found[k ^ 2], found[k]) for k in range(PLANE)]


def plane_gather_first(own):
    return own, to_partner(own, 1), to_partner(own, 2)


def plane_gather_second(state):
    own, from_x, from_y = state
    mine = lax.axis_index("j")
    streams, rows, width = own.shape
    half = streams // 2
    first = to_partner(from_x[:half], 2)
    second = to_partner(from_y[half:], 1)
    whole = jnp.zeros((streams, PLANE, rows, width), own.dtype)
    whole = put(whole, own, mine, 1)
    whole = put(whole, from_x, mine ^ 1, 1)
    whole = put(whole, from_y, mine ^ 2, 1)
    whole = put(whole, jnp.concatenate([first, second], axis=0), mine ^ 3, 1)
    return whole.reshape(streams, PLANE * rows, width)


def plane_gather(own):
    return plane_gather_second(plane_gather_first(own))


def plane_sum_first(part, streams):
    mine = lax.axis_index("j")
    part = part.astype(BF16).reshape(streams, PLANE, -1, part.shape[-1])
    far = at(part, mine ^ 3, 1)
    half = streams // 2
    return part, to_partner(far[:half], 1), to_partner(far[half:], 2)


def plane_sum_second(state):
    part, via_x, via_y = state
    mine = lax.axis_index("j")
    half = via_x.shape[0]
    for_x = at(part, mine ^ 1, 1)
    for_y = at(part, mine ^ 2, 1)
    for_x = jnp.concatenate(
        [for_x[:half], (for_x[half:].astype(F32) + via_y.astype(F32)).astype(BF16)], axis=0
    )
    for_y = jnp.concatenate(
        [(for_y[:half].astype(F32) + via_x.astype(F32)).astype(BF16), for_y[half:]], axis=0
    )
    from_x = to_partner(for_x, 1)
    from_y = to_partner(for_y, 2)
    own = at(part, mine, 1)
    return own.astype(F32) + from_x.astype(F32) + from_y.astype(F32)


def plane_sum(part, streams):
    return plane_sum_second(plane_sum_first(part, streams))


def plane_swap(blocks):
    mine = lax.axis_index("j")
    found = [at(blocks, mine, 0)]
    found += [to_partner(at(blocks, mine ^ bit, 0), bit) for bit in (1, 2, 3)]
    return in_order(found, mine)


def to_chips(weight):
    rows, columns = weight.shape
    blocks = weight.reshape(rows, PLANE, columns // PLANE)
    return jnp.moveaxis(blocks, 1, 0)


def to_core(block):
    return lax.ppermute(block, "c", [(0, 1), (1, 0)])


def along_z(block):
    own = lax.all_gather(block, "z", axis=0, tiled=True)
    return own, to_core(own)


def both_cores(own, other):
    return (own.astype(F32) + to_core(other).astype(F32)).astype(BF16)


def sum_along_z(total):
    return lax.psum_scatter(total, "z", scatter_dimension=0, tiled=True)


def sent_along_z(total):
    size, mine = lax.axis_size("z"), lax.axis_index("z")
    rows = total.reshape(size, -1, total.shape[1])
    result = at(rows, mine, 0).astype(F32)
    for step in range(1, size):
        route = [(i, (i + step) % size) for i in range(size)]
        result += lax.ppermute(at(rows, (mine + step) % size, 0), "z", route).astype(F32)
    return result


def to_owners(summed):
    return plane_swap(summed.reshape(PLANE, -1, summed.shape[1]))


def z_gather(block):
    size, mine = lax.axis_size("z"), lax.axis_index("z")
    whole = jnp.zeros((size, *block.shape), block.dtype)
    whole = put(whole, block, mine, 0)
    for step in range(1, size):
        got = lax.ppermute(block, "z", [(i, (i + step) % size) for i in range(size)])
        whole = put(whole, got, (mine - step) % size, 0)
    return whole


def sum_of_chip_plane(array):
    for axis, pairs in (
        ("c", [(0, 1), (1, 0)]),
        ("j", [(i, i ^ 1) for i in range(PLANE)]),
        ("j", [(i, i ^ 2) for i in range(PLANE)]),
    ):
        array = array + lax.ppermute(array, axis, pairs)
    return array


def with_other_core(array, dim):
    core = lax.axis_index("c")
    count = array.shape[0] // 2
    mine = lax.dynamic_slice_in_dim(array, core * count, count, 0)
    other = lax.dynamic_slice_in_dim(array, (1 - core) * count, count, 0)
    return jnp.concatenate([mine, to_core(other)], axis=dim)


def all_streams(own):
    core = lax.axis_index("c")
    other = to_core(own)
    count = own.shape[0]
    whole = jnp.zeros((2 * count, *own.shape[1:]), own.dtype)
    whole = lax.dynamic_update_slice_in_dim(whole, own, core * count, 0)
    return lax.dynamic_update_slice_in_dim(whole, other, (1 - core) * count, 0)


def shifted(block, distance):
    size = lax.axis_size("z")
    return lax.ppermute(
        block, "z", [(i - distance, i) for i in range(size) if 0 <= i - distance < size]
    )


def entering(keep, state, backward):
    size, mine = lax.axis_size("z"), lax.axis_index("z")
    pair = jnp.stack([keep, state])
    result = jnp.zeros_like(state)
    for distance in range(size - 1, 0, -1):
        got = shifted(pair, -distance if backward else distance)
        there = mine + distance < size if backward else mine >= distance
        result = jnp.where(there, got[0] * result + got[1], result)
    return result


def scan_kernel(backward, keep_ref, add_ref, product_ref, state_ref):
    streams, rows, width = keep_ref.shape
    steps = rows // SEGMENTS
    for s in range(streams):

        def step(number, carry):
            product, state = carry
            place = steps - 1 - number if backward else number
            at_once = pl.ds(place, SEGMENTS, stride=steps)
            keep = keep_ref[s, at_once, :]
            state = keep * state + add_ref[s, at_once, :]
            product = keep * product
            product_ref[s, at_once, :] = product
            state_ref[s, at_once, :] = state
            return product, state

        product, state = lax.fori_loop(
            0,
            steps,
            step,
            (jnp.ones((SEGMENTS, width), F32), jnp.zeros((SEGMENTS, width), F32)),
            unroll=8,
        )
        product_in = jnp.ones((1, width), F32)
        state_in = jnp.zeros((1, width), F32)
        order = range(SEGMENTS - 1, -1, -1) if backward else range(SEGMENTS)
        for k in order:
            here = pl.ds(k * steps, steps)
            local = product_ref[s, here, :]
            state_ref[s, here, :] = state_ref[s, here, :] + local * state_in
            product_ref[s, here, :] = local * product_in
            state_in = product[k : k + 1] * state_in + state[k : k + 1]
            product_in = product[k : k + 1] * product_in


def local_scan(keep, add, backward):
    streams, rows, width = keep.shape
    block = pl.BlockSpec((streams, rows, 128), lambda i: (0, 0, i))
    return pl.pallas_call(
        partial(scan_kernel, backward),
        grid=(width // 128,),
        in_specs=[block, block],
        out_specs=[block, block],
        out_shape=[jax.ShapeDtypeStruct(keep.shape, F32)] * 2,
        compiler_params=pltpu.CompilerParams(vmem_limit_bytes=32 * 1024 * 1024),
        cost_estimate=pl.CostEstimate(
            flops=8 * streams * rows * width,
            bytes_accessed=16 * streams * rows * width,
            transcendentals=0,
        ),
    )(keep, add)


def rms_norm(values, norm_gain):
    factor = lax.rsqrt(jnp.mean(values * values, axis=-1, keepdims=True) + EPSILON)
    return values * factor * norm_gain


def gate_math(pre_rate, pre_entry, lam_param, conv_value):
    rate_gate = jax.nn.sigmoid(pre_rate)
    entry_gate = jax.nn.sigmoid(pre_entry)
    log_decay = -8.0 * rate_gate * jax.nn.softplus(lam_param)
    retain = jnp.exp(log_decay)
    factor = jnp.sqrt(-jnp.expm1(2.0 * log_decay))
    return (retain, factor * entry_gate * conv_value)


def mlp_kernel(
    in_ref, down_ref, gate_w, up_w, narrow_w, act_ref, both_ref, second_ref, out_ref, *totals
):
    half, tile = pl.program_id(1), pl.program_id(2)
    first = (half == 0) & (tile == 0)
    last = (half == pl.num_programs(1) - 1) & (tile == pl.num_programs(2) - 1)
    second_total, out_total = totals
    wide = gate_w.shape[2]
    hidden = wide * pl.num_programs(2)

    def times(left, right, left_dim, right_dim):
        return dot(left, right, left_dim, right_dim)

    rows = in_ref[0]
    gate = times(rows, gate_w[0], 1, 0)
    up = times(rows, up_w[0], 1, 0)
    d_act = times(down_ref[0], narrow_w[0], 1, 0)
    scale = 0.7978845608028654
    square = gate * gate
    bent = jnp.tanh(scale * (gate + 0.044715 * square * gate))
    gelu = 0.5 * gate * (1.0 + bent)
    slope = 0.5 * (1.0 + bent) + (0.5 * scale) * gate * (1.0 - bent * bent) * (
        1.0 + 0.134145 * square
    )
    act = (gelu * up).astype(BF16)
    d_gate = (d_act * up * slope).astype(BF16)
    d_up = (d_act * gelu).astype(BF16)
    act_ref[0] = act
    place = pl.multiple_of(tile * wide, wide)
    both_ref[0, :, pl.ds(place, wide)] = d_gate
    both_ref[0, :, pl.ds(pl.multiple_of(hidden + place, wide), wide)] = d_up
    second = times(d_gate, gate_w[0], 1, 1) + times(d_up, up_w[0], 1, 1)
    out = times(act, narrow_w[0], 1, 1)

    @pl.when(first)
    def _():
        second_total[...] = second
        out_total[...] = out

    @pl.when(jnp.logical_not(first))
    def _():
        second_total[...] += second
        out_total[...] += out

    @pl.when(last)
    def _():
        second_ref[0] = second_total[...].astype(BF16)
        out_ref[0] = out_total[...].astype(BF16)


def mlp(second_low, d_down, weights, tiles):
    streams, rows, width = second_low.shape
    halves, _, columns = weights.shape
    hidden = columns // 3
    wide = hidden // tiles
    token_block = pl.BlockSpec((1, rows, width), lambda s, h, t: (s, 0, 0))
    weight_blocks = [
        pl.BlockSpec((1, width, wide), lambda s, h, t, k=k: (h, 0, k * tiles + t)) for k in range(3)
    ]
    return pl.pallas_call(
        mlp_kernel,
        grid=(streams, halves, tiles),
        in_specs=[token_block, token_block, *weight_blocks],
        out_specs=[
            pl.BlockSpec((1, rows, wide), lambda s, h, t: (h, s, t)),
            pl.BlockSpec((1, rows, 2 * hidden), lambda s, h, t: (h, s, 0)),
            token_block,
            token_block,
        ],
        out_shape=[
            jax.ShapeDtypeStruct((halves, streams * rows, hidden), BF16),
            jax.ShapeDtypeStruct((halves, streams * rows, 2 * hidden), BF16),
            jax.ShapeDtypeStruct(second_low.shape, BF16),
            jax.ShapeDtypeStruct(second_low.shape, BF16),
        ],
        scratch_shapes=[pltpu.VMEM((rows, width), F32), pltpu.VMEM((rows, width), F32)],
        compiler_params=pltpu.CompilerParams(
            vmem_limit_bytes=60 * 1024 * 1024,
            dimension_semantics=("arbitrary", "arbitrary", "arbitrary"),
        ),
        cost_estimate=pl.CostEstimate(
            flops=12 * streams * rows * width * hidden * halves,
            bytes_accessed=40 * 1024 * 1024,
            transcendentals=streams * rows * hidden * halves,
        ),
    )(second_low, d_down, weights, weights, weights)


def convolve(extended, conv_taps, conv_bias, fill_values, insides):
    n_rows = extended.shape[1] - 3
    result = conv_bias + conv_taps[:, 0] * extended[:, 3:]
    for offset in (1, 2, 3):
        window = extended[:, 3 - offset : 3 - offset + n_rows]
        result = result + conv_taps[:, offset] * jnp.where(
            insides[offset - 1], window, fill_values[offset - 1]
        )
    return result


def shards(
    inputs,
    doc_spans,
    doc_lengths,
    state_in,
    conv_in,
    norm_gains,
    w_x,
    w_g,
    rec_params,
    gate_weights,
    w_o,
    w_gate,
    w_up,
    w_down,
    cotangent,
):
    all_streams_count, own_rows, model_width = inputs.shape
    halves = lax.axis_size("c")
    z_size = lax.axis_size("z")
    z_index, j_index, core = lax.axis_index("z"), lax.axis_index("j"), lax.axis_index("c")
    n_streams = all_streams_count // halves
    n_rows = own_rows * PLANE
    tokens = n_streams * n_rows
    own_tokens = n_streams * own_rows
    weight_rows = w_x.shape[0]
    half_width = w_x.shape[1]
    part_width = half_width // PLANE
    rec_width = part_width * halves
    heads_here = rec_width // HEAD_DIM
    ff_part = w_gate.shape[1] // PLANE

    first_stream = core * n_streams

    def own_streams(array):
        return lax.dynamic_slice_in_dim(array, first_stream, n_streams, 0)

    spans = own_streams(doc_spans)
    lengths = own_streams(doc_lengths)
    own_in = own_streams(inputs)
    own_cot = own_streams(cotangent)
    small_rows = rec_params.shape[1]
    small = jnp.concatenate([rec_params[0], gate_weights[0]], axis=1)
    small_width = small.shape[1]
    gain_width = norm_gains.shape[1]
    tails = jnp.pad(norm_gains, ((0, 0), (0, small_width - gain_width)))
    small = jnp.concatenate([small, tails], axis=0)

    first_blocks = jnp.concatenate([to_chips(w_x), to_chips(w_g), to_chips(w_o.T)], axis=2)
    first_rows = jnp.concatenate(plane_swap(first_blocks), axis=0)
    small = z_gather(small)
    later = (w_gate, w_up, w_down)
    first_rows, own_in, small, later = lax.optimization_barrier((first_rows, own_in, small, later))
    gain_rows = jnp.broadcast_to(
        small[:, small_rows:].reshape(1, 2 * z_size, small_width),
        (PLANE, 2 * z_size, small_width),
    )
    small_blocks = small[:, :small_rows].reshape(PLANE, -1, small_width)
    small = jnp.stack(plane_swap(jnp.concatenate([small_blocks, gain_rows], axis=1)))
    in_state, later = lax.optimization_barrier((plane_gather_first(own_in), later))
    whole_in = plane_gather_second(in_state)
    gains_all = small[:, part_width // PLANE :, :gain_width].reshape(PLANE, z_size, 2, gain_width)
    gains_all = jnp.moveaxis(gains_all, (0, 1, 2), (2, 1, 0))
    gains_all = gains_all.reshape(2, model_width).astype(F32)
    small = small[:, : part_width // PLANE].reshape(PLANE, -1, small_rows, small_width)
    small = jnp.moveaxis(small, 0, 1).reshape(part_width, small_width)
    small = jnp.concatenate([small, to_core(small)], axis=0)
    params_all = small[:, :8].astype(F32)
    head = jnp.arange(rec_width, dtype=jnp.int32) // HEAD_DIM
    gates_all = jnp.concatenate(
        [
            jnp.where(
                head[:, None] == head[None, :],
                jnp.tile(small[:, start : start + HEAD_DIM], (1, heads_here)),
                0.0,
            ).astype(BF16)
            for start in (8, 8 + HEAD_DIM)
        ],
        axis=1,
    )

    later_blocks = jnp.concatenate(
        [to_chips(later[0]), to_chips(later[1]), to_chips(later[2].T)], axis=2
    )
    later_rows = jnp.concatenate(plane_swap(later_blocks), axis=0)
    own_cot, later_rows = lax.optimization_barrier((own_cot, later_rows))

    def live_at(position):
        second_start = spans[:, 0:1]
        doc_id = (position[None, :] >= second_start).astype(jnp.int32)
        doc_start = doc_id * second_start
        doc_stop = doc_start + jnp.where(doc_id == 1, lengths[:, 1:2], lengths[:, 0:1])
        live = (position[None, :] < doc_stop).astype(F32)
        return doc_id, doc_start, live

    own_first = (z_index * PLANE + j_index) * own_rows
    own_live = live_at(own_first + jnp.arange(own_rows, dtype=jnp.int32))[2]
    own_live = own_live.reshape(own_tokens, 1)
    position = z_index * n_rows + jnp.arange(n_rows, dtype=jnp.int32)
    doc_id, doc_start, _ = live_at(position)

    d_out = own_cot.reshape(own_tokens, model_width).astype(F32)
    own_down = (d_out * own_live).astype(BF16).reshape(n_streams, own_rows, model_width)
    d_down = plane_gather(own_down)

    flat_in = own_in.reshape(own_tokens, model_width).astype(F32)
    _, norm_one_back = jax.vjp(rms_norm, flat_in, gains_all[0])
    normed_low = rms_norm(
        whole_in.reshape(tokens, model_width).astype(F32), gains_all[0]
    ).astype(BF16)
    first_own, normed_low, later_rows = lax.optimization_barrier(
        (lax.all_gather(first_rows, "z", axis=0, tiled=True), normed_low, later_rows)
    )
    w_later = lax.all_gather(later_rows, ("c", "z"), axis=0)
    w_first = (first_own, to_core(first_own))
    w_rec = jnp.concatenate(
        [w[:, p * part_width : (p + 1) * part_width] for p in (0, 1) for w in w_first], axis=1
    )
    w_back = jnp.concatenate([w[:, 2 * part_width :] for w in w_first], axis=1)
    projected = dot(normed_low, w_rec, 1, 0)
    source_rows = projected[:, :rec_width].astype(BF16).reshape(n_streams, n_rows, rec_width)
    branch, branch_back = jax.vjp(jax.nn.gelu, projected[:, rec_width:])
    rim_rows = shifted(source_rows[:, n_rows - 3 :], 1)
    extended = jnp.concatenate([rim_rows, source_rows], axis=1).astype(F32)

    conv_here = with_other_core(
        lax.dynamic_slice_in_dim(conv_in, j_index * part_width, part_width, 3), 3
    )
    state_here = with_other_core(
        lax.dynamic_slice_in_dim(state_in, j_index * part_width, part_width, 2), 2
    )
    slot_range = jnp.arange(3, dtype=jnp.int32)
    doc_range = jnp.arange(2, dtype=jnp.int32)
    fill_values = []
    insides = []
    for offset in (1, 2, 3):
        earlier_pos = position[None, :] - offset
        insides.append((earlier_pos >= doc_start)[..., None])
        slot_pick = (doc_id[..., None, None] == doc_range[:, None]) & (
            (3 + earlier_pos - doc_start)[..., None, None] == slot_range
        )
        fill_values.append(
            jnp.einsum(
                "btds,bdsc->btc",
                slot_pick.astype(BF16),
                conv_here,
                preferred_element_type=F32,
            )
        )
    conv_value, conv_back = jax.vjp(
        partial(convolve, fill_values=fill_values, insides=insides),
        extended,
        params_all[:, 0:4],
        params_all[:, 4],
    )
    conv_flat = conv_value.reshape(tokens, rec_width)
    conv_low = conv_flat.astype(BF16)
    gate_mixed = dot(conv_low, gates_all, 1, 0)
    pre_rate = gate_mixed[:, :rec_width] + params_all[:, 5]
    pre_entry = gate_mixed[:, rec_width:] + params_all[:, 6]
    (retain, drive_term), gate_back = jax.vjp(
        gate_math, pre_rate, pre_entry, params_all[:, 7], conv_flat
    )
    reset_rows = (position[None, :] == doc_start)[..., None]
    carried = jnp.where((doc_id == 1)[..., None], state_here[:, None, 1], state_here[:, None, 0])
    retain_rows = retain.reshape(n_streams, n_rows, rec_width)
    retain_eff = jnp.where(reset_rows, 0.0, retain_rows)
    drive_eff = drive_term.reshape(n_streams, n_rows, rec_width) + jnp.where(
        reset_rows, retain_rows * carried, 0.0
    )
    local_keep, local_state = local_scan(retain_eff, drive_eff, False)
    state_before = entering(local_keep[:, -1], local_state[:, -1], False)
    states = local_state + local_keep * state_before[:, None]

    starts_doc = jnp.concatenate([jnp.zeros_like(spans[:, :1]), spans[:, :1]], axis=1)
    stops_doc = starts_doc + lengths
    is_last = position[None, :, None] == (stops_doc - 1)[:, None, :]
    final_part = jnp.sum(jnp.where(is_last[..., None], states[:, :, None, :], 0.0), axis=1)
    tail_pos = stops_doc[..., None] - 3 + slot_range
    from_rows = (position[None, :, None, None] == tail_pos[:, None]) & (
        tail_pos >= starts_doc[..., None]
    )[:, None]
    conv_part = jnp.einsum(
        "btdj,btc->bdjc", from_rows.astype(BF16), source_rows, preferred_element_type=F32
    )
    from_state = (
        (tail_pos < starts_doc[..., None])[..., None]
        & ((lengths[..., None] + slot_range)[..., None] == slot_range)
        & (z_index == 0)
    )
    conv_part = conv_part + jnp.einsum(
        "bdjs,bdsc->bdjc", from_state.astype(BF16), conv_here, preferred_element_type=F32
    )
    state_high = lax.reduce_precision(final_part, exponent_bits=8, mantissa_bits=7)
    finals = jnp.stack([state_high, final_part - state_high], axis=2)
    finals = jnp.concatenate([finals, conv_part], axis=2).reshape(-1, rec_width)
    columns = finals.shape[0]
    finals = lax.dynamic_update_slice_in_dim(
        jnp.zeros((rec_width, halves * columns), F32), finals.T, core * columns, 1
    )
    dp_index = z_index * PLANE + j_index

    states_flat = states.reshape(tokens, rec_width)
    mixed_rows = (states_flat * branch).astype(BF16)
    rec_part = dot(mixed_rows, w_back, 1, 1)
    rec_total = plane_sum(rec_part, n_streams).reshape(own_tokens, model_width)
    hidden_one = flat_in + own_live * rec_total
    normed_two, norm_two_back = jax.vjp(rms_norm, hidden_one, gains_all[1])
    own_second = normed_two.astype(BF16).reshape(n_streams, own_rows, model_width)
    second_state, w_later = lax.optimization_barrier((plane_gather_first(own_second), w_later))
    second_low = plane_gather_second(second_state)
    w_later = w_later.reshape(halves, model_width, 3 * ff_part)
    acts, d_both, second_part, down_part = mlp(second_low, d_down, w_later, 1)
    second_low = second_low.reshape(tokens, model_width)
    d_down = d_down.reshape(tokens, model_width)

    def mine_and_other(array):
        return at(array, core, 0), at(array, 1 - core, 0)

    g_narrow = [dot(d_down, act, 0, 0).astype(BF16) for act in mine_and_other(acts)]
    g_wide = [dot(second_low, d, 0, 0).astype(BF16) for d in mine_and_other(d_both)]
    sum_narrow = sum_along_z(both_cores(*g_narrow))

    second_total = plane_sum(second_part, n_streams).reshape(own_tokens, model_width)
    d_hidden_norm, g_gain_two = norm_two_back(second_total)
    d_hidden = d_out + d_hidden_norm
    own_rec = (d_hidden * own_live).astype(BF16).reshape(n_streams, own_rows, model_width)
    d_rec = plane_gather(own_rec).reshape(tokens, model_width)
    d_rec, sum_wide, sum_narrow = lax.optimization_barrier(
        (d_rec, both_cores(*g_wide), sum_narrow)
    )
    sum_wide = sum_along_z(sum_wide)
    d_mixed = dot(d_rec, w_back, 1, 0)
    d_mixed, down_part = lax.optimization_barrier((d_mixed, down_part))
    mlp_sum = plane_sum_first(down_part, n_streams)
    g_back = dot(d_rec, mixed_rows, 0, 0).astype(BF16)

    grad_state = (d_mixed * branch).reshape(n_streams, n_rows, rec_width)
    branch_low = branch_back(d_mixed * states_flat)[0].astype(BF16)
    next_keep = jnp.concatenate([retain_eff[:, 1:], jnp.ones_like(retain_eff[:, :1])], axis=1)
    later_keep, later_sum = local_scan(next_keep, grad_state, True)
    carried_grad = entering(
        retain_eff[:, 0] * later_keep[:, 0], retain_eff[:, 0] * later_sum[:, 0], True
    )
    carried_grad, mlp_sum = lax.optimization_barrier((carried_grad, mlp_sum))
    mlp_sum = plane_sum_second(mlp_sum)
    out_narrow = to_owners(sum_narrow)
    adjoint = later_sum + later_keep * carried_grad[:, None]
    state_prev = jnp.concatenate([state_before[:, None], states[:, :-1]], axis=1)
    state_prev = jnp.where(reset_rows, carried, state_prev)
    d_retain = (adjoint * state_prev).reshape(tokens, rec_width)
    d_rate, d_entry, g_lam, d_conv_direct = gate_back(
        (d_retain, adjoint.reshape(tokens, rec_width))
    )
    rate_low = d_rate.astype(BF16)
    entry_low = d_entry.astype(BF16)
    grad_gates = jnp.concatenate([rate_low, entry_low], axis=1)
    d_conv_gates = dot(grad_gates, gates_all, 1, 1)
    d_conv = (d_conv_direct + d_conv_gates).reshape(n_streams, n_rows, rec_width)
    d_extended, g_taps, g_conv_bias = conv_back(d_conv)
    rim_grad = shifted(d_extended[:, :3].astype(BF16), -1).astype(F32)
    d_source = jnp.concatenate([d_extended[:, 3:n_rows], d_extended[:, n_rows:] + rim_grad], axis=1)
    d_projected = jnp.concatenate(
        [d_source.reshape(tokens, rec_width).astype(BF16), branch_low], axis=1
    )
    d_projected, sum_wide, mlp_total, out_narrow = lax.optimization_barrier(
        (d_projected, sum_wide, mlp_sum, out_narrow)
    )
    mlp_total = mlp_total.reshape(own_tokens, model_width)
    out_flat = (hidden_one + own_live * mlp_total).astype(BF16)
    output = all_streams(out_flat.reshape(n_streams, own_rows, model_width))

    g_rec = dot(normed_low, d_projected, 0, 0).astype(BF16)
    mine, other = (
        jnp.concatenate(
            [
                g[:, start + h * part_width : start + (h + 1) * part_width]
                for g, start in ((g_rec, 0), (g_rec, rec_width), (g_back, 0))
            ],
            axis=1,
        )
        for h in range(halves)
    )
    sum_first = both_cores(mine, other)
    sum_first, d_projected, grad_gates = lax.optimization_barrier(
        (sum_first, d_projected, grad_gates)
    )
    sum_first = sum_along_z(sum_first)
    first_part = dot(d_projected, w_rec, 1, 1)
    whole_flat = whole_in.reshape(tokens, model_width).astype(F32)
    whole_factor = lax.rsqrt(jnp.mean(whole_flat * whole_flat, axis=-1, keepdims=True) + EPSILON)
    g_gain_one = jnp.sum(first_part * whole_flat * whole_factor, axis=0)
    g_gains = sum_of_chip_plane(jnp.stack([g_gain_one, g_gain_two]))
    g_gates = dot(conv_low, grad_gates, 0, 0)
    g_gates = jnp.concatenate(
        [
            jnp.concatenate(
                [
                    g_gates[
                        h * HEAD_DIM : (h + 1) * HEAD_DIM,
                        start + h * HEAD_DIM : start + (h + 1) * HEAD_DIM,
                    ]
                    for start in (0, rec_width)
                ],
                axis=1,
            )
            for h in range(heads_here)
        ],
        axis=0,
    )
    g_small = jnp.concatenate(
        [
            g_taps,
            g_conv_bias[:, None],
            jnp.sum(rate_low.astype(F32), axis=0)[:, None],
            jnp.sum(entry_low.astype(F32), axis=0)[:, None],
            g_lam[:, None],
            g_gates,
            finals,
        ],
        axis=1,
    ).astype(BF16)
    sum_small = both_cores(g_small[:part_width], g_small[part_width:])
    sum_first, sum_small, g_gains = lax.optimization_barrier((sum_first, sum_small, g_gains))
    g_gains = jnp.sum(z_gather(g_gains), axis=0)
    out_first = to_owners(sum_first)
    g_small = sent_along_z(sum_small)
    route = [(z * PLANE + j, j * z_size + z) for z in range(z_size) for j in range(PLANE)]
    g_small = lax.ppermute(g_small.astype(BF16), ("z", "j"), route).astype(F32)
    g_params = g_small[None, :, :8]
    g_gates = g_small[None, :, 8 : 8 + 2 * HEAD_DIM]
    finals = g_small[:, 8 + 2 * HEAD_DIM :].T.reshape(all_streams_count, 2, 5, -1)
    state_block = (finals[:, :, 0] + finals[:, :, 1])[:, :, None]
    conv_block = finals[:, :, 2:].astype(BF16)[:, :, :, None]

    first_total, sum_wide = lax.optimization_barrier((plane_sum(first_part, n_streams), sum_wide))
    first_total = first_total.reshape(own_tokens, model_width)
    out_wide = to_owners(sum_wide)
    d_input_norm = norm_one_back(first_total)[0]
    input_grad = all_streams(
        (d_hidden + d_input_norm).astype(BF16).reshape(n_streams, own_rows, model_width)
    )
    g_gains = lax.dynamic_slice_in_dim(g_gains, dp_index * gain_width, gain_width, 1)

    def flat(blocks, start, stop):
        return jnp.concatenate([b[:, start:stop] for b in blocks], axis=1).astype(F32)

    return (
        output,
        input_grad,
        state_block,
        conv_block,
        g_gains,
        flat(out_first, 0, part_width),
        flat(out_first, part_width, 2 * part_width),
        g_params,
        g_gates,
        flat(out_first, 2 * part_width, 3 * part_width).T,
        flat(out_wide, 0, ff_part),
        flat(out_wide, ff_part, 2 * ff_part),
        flat(out_narrow, 0, ff_part).T,
    )


def solution(mesh):
    devices = mesh.devices.reshape(-1, PLANE, mesh.shape["mp"])
    planes = Mesh(devices, ("z", "j", "c"))
    dp, mp = ("z", "j"), "c"
    return jax.shard_map(
        shards,
        mesh=planes,
        in_specs=(
            P(None, dp, None),
            P(),
            P(),
            P(None, None, mp),
            P(None, None, None, mp),
            P(None, dp),
            P(dp, mp),
            P(dp, mp),
            P(mp, dp, None),
            P(mp, dp, None),
            P(mp, dp),
            P(dp, mp),
            P(dp, mp),
            P(mp, dp),
            P(None, dp, None),
        ),
        out_specs=(
            P(None, dp, None),
            P(None, dp, None),
            P(None, None, mp, dp),
            P(None, None, None, mp, dp),
            P(None, dp),
            P(dp, mp),
            P(dp, mp),
            P(mp, dp, None),
            P(mp, dp, None),
            P(mp, dp),
            P(dp, mp),
            P(dp, mp),
            P(mp, dp),
        ),
        check_vma=False,
    )
```

```python
from functools import partial

import jax
import jax.numpy as jnp
from jax import lax
from jax.experimental import pallas as pl
from jax.experimental.pallas import tpu as pltpu
from jax.sharding import Mesh
from jax.sharding import PartitionSpec as P

HEAD_DIM = 160
PLANE = 4
SEGMENTS = 8
EPSILON = 1e-06
BF16 = jnp.bfloat16
F32 = jnp.float32


def dot(left, right, left_dim, right_dim):
    return lax.dot_general(
        left, right, (((left_dim,), (right_dim,)), ((), ())), preferred_element_type=F32
    )


def to_partner(block, bit):
    return lax.ppermute(block, "j", [(i, i ^ bit) for i in range(PLANE)])


def at(block, index, axis):
    return lax.dynamic_index_in_dim(block, index, axis, keepdims=False)


def put(whole, block, index, axis):
    return lax.dynamic_update_index_in_dim(whole, block, index, axis)


def in_order(found, index):
    low, high = index % 2 == 1, index // 2 == 1
    found = [jnp.where(low, found[k ^ 1], found[k]) for k in range(PLANE)]
    return [jnp.where(high, found[k ^ 2], found[k]) for k in range(PLANE)]


def plane_gather_first(own):
    return own, to_partner(own, 1), to_partner(own, 2)


def plane_gather_second(state):
    own, from_x, from_y = state
    mine = lax.axis_index("j")
    streams, rows, width = own.shape
    half = streams // 2
    first = to_partner(from_x[:half], 2)
    second = to_partner(from_y[half:], 1)
    whole = jnp.zeros((streams, PLANE, rows, width), own.dtype)
    whole = put(whole, own, mine, 1)
    whole = put(whole, from_x, mine ^ 1, 1)
    whole = put(whole, from_y, mine ^ 2, 1)
    whole = put(whole, jnp.concatenate([first, second], axis=0), mine ^ 3, 1)
    return whole.reshape(streams, PLANE * rows, width)


def plane_gather(own):
    return plane_gather_second(plane_gather_first(own))


def plane_sum_first(part, streams):
    mine = lax.axis_index("j")
    part = part.astype(BF16).reshape(streams, PLANE, -1, part.shape[-1])
    far = at(part, mine ^ 3, 1)
    half = streams // 2
    return part, to_partner(far[:half], 1), to_partner(far[half:], 2)


def plane_sum_second(state):
    part, via_x, via_y = state
    mine = lax.axis_index("j")
    half = via_x.shape[0]
    for_x = at(part, mine ^ 1, 1)
    for_y = at(part, mine ^ 2, 1)
    for_x = jnp.concatenate(
        [for_x[:half], (for_x[half:].astype(F32) + via_y.astype(F32)).astype(BF16)], axis=0
    )
    for_y = jnp.concatenate(
        [(for_y[:half].astype(F32) + via_x.astype(F32)).astype(BF16), for_y[half:]], axis=0
    )
    from_x = to_partner(for_x, 1)
    from_y = to_partner(for_y, 2)
    own = at(part, mine, 1)
    return own.astype(F32) + from_x.astype(F32) + from_y.astype(F32)


def plane_sum(part, streams):
    return plane_sum_second(plane_sum_first(part, streams))


def plane_swap(blocks):
    mine = lax.axis_index("j")
    found = [at(blocks, mine, 0)]
    found += [to_partner(at(blocks, mine ^ bit, 0), bit) for bit in (1, 2, 3)]
    return in_order(found, mine)


def to_chips(weight):
    rows, columns = weight.shape
    blocks = weight.reshape(rows, PLANE, columns // PLANE)
    return jnp.moveaxis(blocks, 1, 0)


def to_core(block):
    return lax.ppermute(block, "c", [(0, 1), (1, 0)])


def along_z(block):
    own = lax.all_gather(block, "z", axis=0, tiled=True)
    return own, to_core(own)


def both_cores(own, other):
    return (own.astype(F32) + to_core(other).astype(F32)).astype(BF16)


def sum_along_z(total):
    return lax.psum_scatter(total, "z", scatter_dimension=0, tiled=True)


def sent_along_z(total):
    size, mine = lax.axis_size("z"), lax.axis_index("z")
    rows = total.reshape(size, -1, total.shape[1])
    result = at(rows, mine, 0).astype(F32)
    for step in range(1, size):
        route = [(i, (i + step) % size) for i in range(size)]
        result += lax.ppermute(at(rows, (mine + step) % size, 0), "z", route).astype(F32)
    return result


def to_owners(summed):
    return plane_swap(summed.reshape(PLANE, -1, summed.shape[1]))


def z_gather(block):
    size, mine = lax.axis_size("z"), lax.axis_index("z")
    whole = jnp.zeros((size, *block.shape), block.dtype)
    whole = put(whole, block, mine, 0)
    for step in range(1, size):
        got = lax.ppermute(block, "z", [(i, (i + step) % size) for i in range(size)])
        whole = put(whole, got, (mine - step) % size, 0)
    return whole


def sum_of_chip_plane(array):
    for axis, pairs in (
        ("c", [(0, 1), (1, 0)]),
        ("j", [(i, i ^ 1) for i in range(PLANE)]),
        ("j", [(i, i ^ 2) for i in range(PLANE)]),
    ):
        array = array + lax.ppermute(array, axis, pairs)
    return array


def with_other_core(array, dim):
    core = lax.axis_index("c")
    count = array.shape[0] // 2
    mine = lax.dynamic_slice_in_dim(array, core * count, count, 0)
    other = lax.dynamic_slice_in_dim(array, (1 - core) * count, count, 0)
    return jnp.concatenate([mine, to_core(other)], axis=dim)


def all_streams(own):
    core = lax.axis_index("c")
    other = to_core(own)
    count = own.shape[0]
    whole = jnp.zeros((2 * count, *own.shape[1:]), own.dtype)
    whole = lax.dynamic_update_slice_in_dim(whole, own, core * count, 0)
    return lax.dynamic_update_slice_in_dim(whole, other, (1 - core) * count, 0)


def shifted(block, distance):
    size = lax.axis_size("z")
    return lax.ppermute(
        block, "z", [(i - distance, i) for i in range(size) if 0 <= i - distance < size]
    )


def entering(keep, state, backward):
    size, mine = lax.axis_size("z"), lax.axis_index("z")
    pair = jnp.stack([keep, state])
    result = jnp.zeros_like(state)
    for distance in range(size - 1, 0, -1):
        got = shifted(pair, -distance if backward else distance)
        there = mine + distance < size if backward else mine >= distance
        result = jnp.where(there, got[0] * result + got[1], result)
    return result


def scan_kernel(backward, keep_ref, add_ref, product_ref, state_ref):
    streams, rows, width = keep_ref.shape
    steps = rows // SEGMENTS
    for s in range(streams):

        def step(number, carry):
            product, state = carry
            place = steps - 1 - number if backward else number
            at_once = pl.ds(place, SEGMENTS, stride=steps)
            keep = keep_ref[s, at_once, :]
            state = keep * state + add_ref[s, at_once, :]
            product = keep * product
            product_ref[s, at_once, :] = product
            state_ref[s, at_once, :] = state
            return product, state

        product, state = lax.fori_loop(
            0,
            steps,
            step,
            (jnp.ones((SEGMENTS, width), F32), jnp.zeros((SEGMENTS, width), F32)),
            unroll=8,
        )
        product_in = jnp.ones((1, width), F32)
        state_in = jnp.zeros((1, width), F32)
        order = range(SEGMENTS - 1, -1, -1) if backward else range(SEGMENTS)
        for k in order:
            here = pl.ds(k * steps, steps)
            local = product_ref[s, here, :]
            state_ref[s, here, :] = state_ref[s, here, :] + local * state_in
            product_ref[s, here, :] = local * product_in
            state_in = product[k : k + 1] * state_in + state[k : k + 1]
            product_in = product[k : k + 1] * product_in


def local_scan(keep, add, backward):
    streams, rows, width = keep.shape
    block = pl.BlockSpec((streams, rows, 128), lambda i: (0, 0, i))
    return pl.pallas_call(
        partial(scan_kernel, backward),
        grid=(width // 128,),
        in_specs=[block, block],
        out_specs=[block, block],
        out_shape=[jax.ShapeDtypeStruct(keep.shape, F32)] * 2,
        compiler_params=pltpu.CompilerParams(vmem_limit_bytes=32 * 1024 * 1024),
        cost_estimate=pl.CostEstimate(
            flops=8 * streams * rows * width,
            bytes_accessed=16 * streams * rows * width,
            transcendentals=0,
        ),
    )(keep, add)


def rms_norm(values, norm_gain):
    factor = lax.rsqrt(jnp.mean(values * values, axis=-1, keepdims=True) + EPSILON)
    return values * factor * norm_gain


def gate_math(pre_rate, pre_entry, lam_param, conv_value):
    rate_gate = jax.nn.sigmoid(pre_rate)
    entry_gate = jax.nn.sigmoid(pre_entry)
    log_decay = -8.0 * rate_gate * jax.nn.softplus(lam_param)
    retain = jnp.exp(log_decay)
    factor = jnp.sqrt(-jnp.expm1(2.0 * log_decay))
    return (retain, factor * entry_gate * conv_value)


def mlp_kernel(
    in_ref, down_ref, gate_w, up_w, narrow_w, act_ref, both_ref, second_ref, out_ref, *totals
):
    half, tile = pl.program_id(1), pl.program_id(2)
    first = (half == 0) & (tile == 0)
    last = (half == pl.num_programs(1) - 1) & (tile == pl.num_programs(2) - 1)
    second_total, out_total = totals
    wide = gate_w.shape[2]
    hidden = wide * pl.num_programs(2)

    def times(left, right, left_dim, right_dim):
        return dot(left, right, left_dim, right_dim)

    rows = in_ref[0]
    gate = times(rows, gate_w[0], 1, 0)
    up = times(rows, up_w[0], 1, 0)
    d_act = times(down_ref[0], narrow_w[0], 1, 0)
    scale = 0.7978845608028654
    square = gate * gate
    bent = jnp.tanh(scale * (gate + 0.044715 * square * gate))
    gelu = 0.5 * gate * (1.0 + bent)
    slope = 0.5 * (1.0 + bent) + (0.5 * scale) * gate * (1.0 - bent * bent) * (
        1.0 + 0.134145 * square
    )
    act = (gelu * up).astype(BF16)
    d_gate = (d_act * up * slope).astype(BF16)
    d_up = (d_act * gelu).astype(BF16)
    act_ref[0] = act
    place = pl.multiple_of(tile * wide, wide)
    both_ref[0, :, pl.ds(place, wide)] = d_gate
    both_ref[0, :, pl.ds(pl.multiple_of(hidden + place, wide), wide)] = d_up
    second = times(d_gate, gate_w[0], 1, 1) + times(d_up, up_w[0], 1, 1)
    out = times(act, narrow_w[0], 1, 1)

    @pl.when(first)
    def _():
        second_total[...] = second
        out_total[...] = out

    @pl.when(jnp.logical_not(first))
    def _():
        second_total[...] += second
        out_total[...] += out

    @pl.when(last)
    def _():
        second_ref[0] = second_total[...].astype(BF16)
        out_ref[0] = out_total[...].astype(BF16)


def mlp(second_low, d_down, weights, tiles):
    streams, rows, width = second_low.shape
    halves, _, columns = weights.shape
    hidden = columns // 3
    wide = hidden // tiles
    token_block = pl.BlockSpec((1, rows, width), lambda s, h, t: (s, 0, 0))
    weight_blocks = [
        pl.BlockSpec((1, width, wide), lambda s, h, t, k=k: (h, 0, k * tiles + t)) for k in range(3)
    ]
    return pl.pallas_call(
        mlp_kernel,
        grid=(streams, halves, tiles),
        in_specs=[token_block, token_block, *weight_blocks],
        out_specs=[
            pl.BlockSpec((1, rows, wide), lambda s, h, t: (h, s, t)),
            pl.BlockSpec((1, rows, 2 * hidden), lambda s, h, t: (h, s, 0)),
            token_block,
            token_block,
        ],
        out_shape=[
            jax.ShapeDtypeStruct((halves, streams * rows, hidden), BF16),
            jax.ShapeDtypeStruct((halves, streams * rows, 2 * hidden), BF16),
            jax.ShapeDtypeStruct(second_low.shape, BF16),
            jax.ShapeDtypeStruct(second_low.shape, BF16),
        ],
        scratch_shapes=[pltpu.VMEM((rows, width), F32), pltpu.VMEM((rows, width), F32)],
        compiler_params=pltpu.CompilerParams(
            vmem_limit_bytes=60 * 1024 * 1024,
            dimension_semantics=("arbitrary", "arbitrary", "arbitrary"),
        ),
        cost_estimate=pl.CostEstimate(
            flops=12 * streams * rows * width * hidden * halves,
            bytes_accessed=40 * 1024 * 1024,
            transcendentals=streams * rows * hidden * halves,
        ),
    )(second_low, d_down, weights, weights, weights)


def convolve(extended, conv_taps, conv_bias, fill_values, insides):
    n_rows = extended.shape[1] - 3
    result = conv_bias + conv_taps[:, 0] * extended[:, 3:]
    for offset in (1, 2, 3):
        window = extended[:, 3 - offset : 3 - offset + n_rows]
        result = result + conv_taps[:, offset] * jnp.where(
            insides[offset - 1], window, fill_values[offset - 1]
        )
    return result


def shards(
    inputs,
    doc_spans,
    doc_lengths,
    state_in,
    conv_in,
    norm_gains,
    w_x,
    w_g,
    rec_params,
    gate_weights,
    w_o,
    w_gate,
    w_up,
    w_down,
    cotangent,
):
    all_streams_count, own_rows, model_width = inputs.shape
    halves = lax.axis_size("c")
    z_size = lax.axis_size("z")
    z_index, j_index, core = lax.axis_index("z"), lax.axis_index("j"), lax.axis_index("c")
    n_streams = all_streams_count // halves
    n_rows = own_rows * PLANE
    tokens = n_streams * n_rows
    own_tokens = n_streams * own_rows
    weight_rows = w_x.shape[0]
    half_width = w_x.shape[1]
    part_width = half_width // PLANE
    rec_width = part_width * halves
    heads_here = rec_width // HEAD_DIM
    ff_part = w_gate.shape[1] // PLANE

    first_stream = core * n_streams

    def own_streams(array):
        return lax.dynamic_slice_in_dim(array, first_stream, n_streams, 0)

    spans = own_streams(doc_spans)
    lengths = own_streams(doc_lengths)
    own_in = own_streams(inputs)
    own_cot = own_streams(cotangent)
    small_rows = rec_params.shape[1]
    small = jnp.concatenate([rec_params[0], gate_weights[0]], axis=1)
    small_width = small.shape[1]
    gain_width = norm_gains.shape[1]
    tails = jnp.pad(norm_gains, ((0, 0), (0, small_width - gain_width)))
    small = jnp.concatenate([small, tails], axis=0)

    first_blocks = jnp.concatenate([to_chips(w_x), to_chips(w_g), to_chips(w_o.T)], axis=2)
    first_rows = jnp.concatenate(plane_swap(first_blocks), axis=0)
    small = z_gather(small)
    later = (w_gate, w_up, w_down)
    first_rows, own_in, small, later = lax.optimization_barrier((first_rows, own_in, small, later))
    gain_rows = jnp.broadcast_to(
        small[:, small_rows:].reshape(1, 2 * z_size, small_width),
        (PLANE, 2 * z_size, small_width),
    )
    small_blocks = small[:, :small_rows].reshape(PLANE, -1, small_width)
    small = jnp.stack(plane_swap(jnp.concatenate([small_blocks, gain_rows], axis=1)))
    in_state, later = lax.optimization_barrier((plane_gather_first(own_in), later))
    whole_in = plane_gather_second(in_state)
    gains_all = small[:, part_width // PLANE :, :gain_width].reshape(PLANE, z_size, 2, gain_width)
    gains_all = jnp.moveaxis(gains_all, (0, 1, 2), (2, 1, 0))
    gains_all = gains_all.reshape(2, model_width).astype(F32)
    small = small[:, : part_width // PLANE].reshape(PLANE, -1, small_rows, small_width)
    small = jnp.moveaxis(small, 0, 1).reshape(part_width, small_width)
    small = jnp.concatenate([small, to_core(small)], axis=0)
    params_all = small[:, :8].astype(F32)
    head = jnp.arange(rec_width, dtype=jnp.int32) // HEAD_DIM
    gates_all = jnp.concatenate(
        [
            jnp.where(
                head[:, None] == head[None, :],
                jnp.tile(small[:, start : start + HEAD_DIM], (1, heads_here)),
                0.0,
            ).astype(BF16)
            for start in (8, 8 + HEAD_DIM)
        ],
        axis=1,
    )

    later_blocks = jnp.concatenate(
        [to_chips(later[0]), to_chips(later[1]), to_chips(later[2].T)], axis=2
    )
    later_rows = jnp.concatenate(plane_swap(later_blocks), axis=0)
    own_cot, later_rows = lax.optimization_barrier((own_cot, later_rows))

    def live_at(position):
        second_start = spans[:, 0:1]
        doc_id = (position[None, :] >= second_start).astype(jnp.int32)
        doc_start = doc_id * second_start
        doc_stop = doc_start + jnp.where(doc_id == 1, lengths[:, 1:2], lengths[:, 0:1])
        live = (position[None, :] < doc_stop).astype(F32)
        return doc_id, doc_start, live

    own_first = (z_index * PLANE + j_index) * own_rows
    own_live = live_at(own_first + jnp.arange(own_rows, dtype=jnp.int32))[2]
    own_live = own_live.reshape(own_tokens, 1)
    position = z_index * n_rows + jnp.arange(n_rows, dtype=jnp.int32)
    doc_id, doc_start, _ = live_at(position)

    d_out = own_cot.reshape(own_tokens, model_width).astype(F32)
    own_down = (d_out * own_live).astype(BF16).reshape(n_streams, own_rows, model_width)
    down_state = plane_gather_first(own_down)

    flat_in = own_in.reshape(own_tokens, model_width).astype(F32)
    _, norm_one_back = jax.vjp(rms_norm, flat_in, gains_all[0])
    normed_low = rms_norm(
        whole_in.reshape(tokens, model_width).astype(F32), gains_all[0]
    ).astype(BF16)
    first_own, normed_low, later_rows = lax.optimization_barrier(
        (lax.all_gather(first_rows, "z", axis=0, tiled=True), normed_low, later_rows)
    )
    w_later = lax.all_gather(later_rows, ("c", "z"), axis=0)
    w_first = (first_own, to_core(first_own))
    w_rec = jnp.concatenate(
        [w[:, p * part_width : (p + 1) * part_width] for p in (0, 1) for w in w_first], axis=1
    )
    w_back = jnp.concatenate([w[:, 2 * part_width :] for w in w_first], axis=1)
    w_rec, down_state = lax.optimization_barrier((w_rec, down_state))
    projected = dot(normed_low, w_rec, 1, 0)
    source_rows = projected[:, :rec_width].astype(BF16).reshape(n_streams, n_rows, rec_width)
    branch, branch_back = jax.vjp(jax.nn.gelu, projected[:, rec_width:])
    rim_rows = shifted(source_rows[:, n_rows - 3 :], 1)
    extended = jnp.concatenate([rim_rows, source_rows], axis=1).astype(F32)

    conv_here = with_other_core(
        lax.dynamic_slice_in_dim(conv_in, j_index * part_width, part_width, 3), 3
    )
    state_here = with_other_core(
        lax.dynamic_slice_in_dim(state_in, j_index * part_width, part_width, 2), 2
    )
    slot_range = jnp.arange(3, dtype=jnp.int32)
    doc_range = jnp.arange(2, dtype=jnp.int32)
    fill_values = []
    insides = []
    for offset in (1, 2, 3):
        earlier_pos = position[None, :] - offset
        insides.append((earlier_pos >= doc_start)[..., None])
        slot_pick = (doc_id[..., None, None] == doc_range[:, None]) & (
            (3 + earlier_pos - doc_start)[..., None, None] == slot_range
        )
        fill_values.append(
            jnp.einsum(
                "btds,bdsc->btc",
                slot_pick.astype(BF16),
                conv_here,
                preferred_element_type=F32,
            )
        )
    conv_value, conv_back = jax.vjp(
        partial(convolve, fill_values=fill_values, insides=insides),
        extended,
        params_all[:, 0:4],
        params_all[:, 4],
    )
    conv_flat = conv_value.reshape(tokens, rec_width)
    conv_low = conv_flat.astype(BF16)
    gate_mixed = dot(conv_low, gates_all, 1, 0)
    pre_rate = gate_mixed[:, :rec_width] + params_all[:, 5]
    pre_entry = gate_mixed[:, rec_width:] + params_all[:, 6]
    (retain, drive_term), gate_back = jax.vjp(
        gate_math, pre_rate, pre_entry, params_all[:, 7], conv_flat
    )
    reset_rows = (position[None, :] == doc_start)[..., None]
    carried = jnp.where((doc_id == 1)[..., None], state_here[:, None, 1], state_here[:, None, 0])
    retain_rows = retain.reshape(n_streams, n_rows, rec_width)
    retain_eff = jnp.where(reset_rows, 0.0, retain_rows)
    drive_eff = drive_term.reshape(n_streams, n_rows, rec_width) + jnp.where(
        reset_rows, retain_rows * carried, 0.0
    )
    local_keep, local_state = local_scan(retain_eff, drive_eff, False)
    state_before = entering(local_keep[:, -1], local_state[:, -1], False)
    states = local_state + local_keep * state_before[:, None]

    starts_doc = jnp.concatenate([jnp.zeros_like(spans[:, :1]), spans[:, :1]], axis=1)
    stops_doc = starts_doc + lengths
    is_last = position[None, :, None] == (stops_doc - 1)[:, None, :]
    final_part = jnp.sum(jnp.where(is_last[..., None], states[:, :, None, :], 0.0), axis=1)
    tail_pos = stops_doc[..., None] - 3 + slot_range
    from_rows = (position[None, :, None, None] == tail_pos[:, None]) & (
        tail_pos >= starts_doc[..., None]
    )[:, None]
    conv_part = jnp.einsum(
        "btdj,btc->bdjc", from_rows.astype(BF16), source_rows, preferred_element_type=F32
    )
    from_state = (
        (tail_pos < starts_doc[..., None])[..., None]
        & ((lengths[..., None] + slot_range)[..., None] == slot_range)
        & (z_index == 0)
    )
    conv_part = conv_part + jnp.einsum(
        "bdjs,bdsc->bdjc", from_state.astype(BF16), conv_here, preferred_element_type=F32
    )
    state_high = lax.reduce_precision(final_part, exponent_bits=8, mantissa_bits=7)
    finals = jnp.stack([state_high, final_part - state_high], axis=2)
    finals = jnp.concatenate([finals, conv_part], axis=2).reshape(-1, rec_width)
    columns = finals.shape[0]
    finals = lax.dynamic_update_slice_in_dim(
        jnp.zeros((rec_width, halves * columns), F32), finals.T, core * columns, 1
    )
    dp_index = z_index * PLANE + j_index

    states_flat = states.reshape(tokens, rec_width)
    mixed_rows = (states_flat * branch).astype(BF16)
    mixed_rows, d_down = lax.optimization_barrier((mixed_rows, plane_gather_second(down_state)))
    rec_part = dot(mixed_rows, w_back, 1, 1)
    rec_total = plane_sum(rec_part, n_streams).reshape(own_tokens, model_width)
    hidden_one = flat_in + own_live * rec_total
    normed_two, norm_two_back = jax.vjp(rms_norm, hidden_one, gains_all[1])
    own_second = normed_two.astype(BF16).reshape(n_streams, own_rows, model_width)
    second_low, w_later = lax.optimization_barrier((plane_gather(own_second), w_later))
    w_later = w_later.reshape(halves, model_width, 3 * ff_part)
    acts, d_both, second_part, down_part = mlp(second_low, d_down, w_later, 1)
    second_low = second_low.reshape(tokens, model_width)
    d_down = d_down.reshape(tokens, model_width)

    def mine_and_other(array):
        return at(array, core, 0), at(array, 1 - core, 0)

    g_narrow = [dot(d_down, act, 0, 0).astype(BF16) for act in mine_and_other(acts)]
    g_wide = [dot(second_low, d, 0, 0).astype(BF16) for d in mine_and_other(d_both)]
    sum_narrow = sum_along_z(both_cores(*g_narrow))

    second_total = plane_sum(second_part, n_streams).reshape(own_tokens, model_width)
    d_hidden_norm, g_gain_two = norm_two_back(second_total)
    d_hidden = d_out + d_hidden_norm
    own_rec = (d_hidden * own_live).astype(BF16).reshape(n_streams, own_rows, model_width)
    d_rec = plane_gather(own_rec).reshape(tokens, model_width)
    d_rec, sum_wide, sum_narrow = lax.optimization_barrier(
        (d_rec, both_cores(*g_wide), sum_narrow)
    )
    sum_wide = sum_along_z(sum_wide)
    d_mixed = dot(d_rec, w_back, 1, 0)
    d_mixed, down_part = lax.optimization_barrier((d_mixed, down_part))
    mlp_sum = plane_sum_first(down_part, n_streams)
    g_back = dot(d_rec, mixed_rows, 0, 0).astype(BF16)

    grad_state = (d_mixed * branch).reshape(n_streams, n_rows, rec_width)
    branch_low = branch_back(d_mixed * states_flat)[0].astype(BF16)
    next_keep = jnp.concatenate([retain_eff[:, 1:], jnp.ones_like(retain_eff[:, :1])], axis=1)
    later_keep, later_sum = local_scan(next_keep, grad_state, True)
    carried_grad = entering(
        retain_eff[:, 0] * later_keep[:, 0], retain_eff[:, 0] * later_sum[:, 0], True
    )
    carried_grad, mlp_sum = lax.optimization_barrier((carried_grad, mlp_sum))
    mlp_sum = plane_sum_second(mlp_sum)
    out_narrow = to_owners(sum_narrow)
    adjoint = later_sum + later_keep * carried_grad[:, None]
    state_prev = jnp.concatenate([state_before[:, None], states[:, :-1]], axis=1)
    state_prev = jnp.where(reset_rows, carried, state_prev)
    d_retain = (adjoint * state_prev).reshape(tokens, rec_width)
    d_rate, d_entry, g_lam, d_conv_direct = gate_back(
        (d_retain, adjoint.reshape(tokens, rec_width))
    )
    rate_low = d_rate.astype(BF16)
    entry_low = d_entry.astype(BF16)
    grad_gates = jnp.concatenate([rate_low, entry_low], axis=1)
    d_conv_gates = dot(grad_gates, gates_all, 1, 1)
    d_conv = (d_conv_direct + d_conv_gates).reshape(n_streams, n_rows, rec_width)
    d_extended, g_taps, g_conv_bias = conv_back(d_conv)
    rim_grad = shifted(d_extended[:, :3].astype(BF16), -1).astype(F32)
    d_source = jnp.concatenate([d_extended[:, 3:n_rows], d_extended[:, n_rows:] + rim_grad], axis=1)
    d_projected = jnp.concatenate(
        [d_source.reshape(tokens, rec_width).astype(BF16), branch_low], axis=1
    )
    d_projected, sum_wide, mlp_total, out_narrow = lax.optimization_barrier(
        (d_projected, sum_wide, mlp_sum, out_narrow)
    )
    mlp_total = mlp_total.reshape(own_tokens, model_width)
    out_flat = (hidden_one + own_live * mlp_total).astype(BF16)
    output = all_streams(out_flat.reshape(n_streams, own_rows, model_width))

    g_rec = dot(normed_low, d_projected, 0, 0).astype(BF16)
    mine, other = (
        jnp.concatenate(
            [
                g[:, start + h * part_width : start + (h + 1) * part_width]
                for g, start in ((g_rec, 0), (g_rec, rec_width), (g_back, 0))
            ],
            axis=1,
        )
        for h in range(halves)
    )
    sum_first = both_cores(mine, other)
    sum_first, d_projected, grad_gates = lax.optimization_barrier(
        (sum_first, d_projected, grad_gates)
    )
    sum_first = sum_along_z(sum_first)
    first_part = dot(d_projected, w_rec, 1, 1)
    whole_flat = whole_in.reshape(tokens, model_width).astype(F32)
    whole_factor = lax.rsqrt(jnp.mean(whole_flat * whole_flat, axis=-1, keepdims=True) + EPSILON)
    g_gain_one = jnp.sum(first_part * whole_flat * whole_factor, axis=0)
    g_gains = sum_of_chip_plane(jnp.stack([g_gain_one, g_gain_two]))
    g_gates = dot(conv_low, grad_gates, 0, 0)
    g_gates = jnp.concatenate(
        [
            jnp.concatenate(
                [
                    g_gates[
                        h * HEAD_DIM : (h + 1) * HEAD_DIM,
                        start + h * HEAD_DIM : start + (h + 1) * HEAD_DIM,
                    ]
                    for start in (0, rec_width)
                ],
                axis=1,
            )
            for h in range(heads_here)
        ],
        axis=0,
    )
    g_small = jnp.concatenate(
        [
            g_taps,
            g_conv_bias[:, None],
            jnp.sum(rate_low.astype(F32), axis=0)[:, None],
            jnp.sum(entry_low.astype(F32), axis=0)[:, None],
            g_lam[:, None],
            g_gates,
            finals,
        ],
        axis=1,
    ).astype(BF16)
    sum_small = both_cores(g_small[:part_width], g_small[part_width:])
    sum_first, sum_small, g_gains = lax.optimization_barrier((sum_first, sum_small, g_gains))
    g_gains = jnp.sum(z_gather(g_gains), axis=0)
    out_first = to_owners(sum_first)
    g_small = sent_along_z(sum_small)
    route = [(z * PLANE + j, j * z_size + z) for z in range(z_size) for j in range(PLANE)]
    g_small = lax.ppermute(g_small.astype(BF16), ("z", "j"), route).astype(F32)
    g_params = g_small[None, :, :8]
    g_gates = g_small[None, :, 8 : 8 + 2 * HEAD_DIM]
    finals = g_small[:, 8 + 2 * HEAD_DIM :].T.reshape(all_streams_count, 2, 5, -1)
    state_block = (finals[:, :, 0] + finals[:, :, 1])[:, :, None]
    conv_block = finals[:, :, 2:].astype(BF16)[:, :, :, None]

    first_total, sum_wide = lax.optimization_barrier((plane_sum(first_part, n_streams), sum_wide))
    first_total = first_total.reshape(own_tokens, model_width)
    out_wide = to_owners(sum_wide)
    d_input_norm = norm_one_back(first_total)[0]
    input_grad = all_streams(
        (d_hidden + d_input_norm).astype(BF16).reshape(n_streams, own_rows, model_width)
    )
    g_gains = lax.dynamic_slice_in_dim(g_gains, dp_index * gain_width, gain_width, 1)

    def flat(blocks, start, stop):
        return jnp.concatenate([b[:, start:stop] for b in blocks], axis=1).astype(F32)

    return (
        output,
        input_grad,
        state_block,
        conv_block,
        g_gains,
        flat(out_first, 0, part_width),
        flat(out_first, part_width, 2 * part_width),
        g_params,
        g_gates,
        flat(out_first, 2 * part_width, 3 * part_width).T,
        flat(out_wide, 0, ff_part),
        flat(out_wide, ff_part, 2 * ff_part),
        flat(out_narrow, 0, ff_part).T,
    )


def solution(mesh):
    devices = mesh.devices.reshape(-1, PLANE, mesh.shape["mp"])
    planes = Mesh(devices, ("z", "j", "c"))
    dp, mp = ("z", "j"), "c"
    return jax.shard_map(
        shards,
        mesh=planes,
        in_specs=(
            P(None, dp, None),
            P(),
            P(),
            P(None, None, mp),
            P(None, None, None, mp),
            P(None, dp),
            P(dp, mp),
            P(dp, mp),
            P(mp, dp, None),
            P(mp, dp, None),
            P(mp, dp),
            P(dp, mp),
            P(dp, mp),
            P(mp, dp),
            P(None, dp, None),
        ),
        out_specs=(
            P(None, dp, None),
            P(None, dp, None),
            P(None, None, mp, dp),
            P(None, None, None, mp, dp),
            P(None, dp),
            P(dp, mp),
            P(dp, mp),
            P(mp, dp, None),
            P(mp, dp, None),
            P(mp, dp),
            P(dp, mp),
            P(dp, mp),
            P(mp, dp),
        ),
        check_vma=False,
    )
```

```python
from functools import partial

import jax
import jax.numpy as jnp
from jax import lax
from jax.experimental import pallas as pl
from jax.experimental.pallas import tpu as pltpu
from jax.sharding import Mesh
from jax.sharding import PartitionSpec as P

HEAD_DIM = 160
PLANE = 4
SEGMENTS = 8
EPSILON = 1e-06
BF16 = jnp.bfloat16
F32 = jnp.float32


def dot(left, right, left_dim, right_dim):
    return lax.dot_general(
        left, right, (((left_dim,), (right_dim,)), ((), ())), preferred_element_type=F32
    )


def to_partner(block, bit):
    return lax.ppermute(block, "j", [(i, i ^ bit) for i in range(PLANE)])


def at(block, index, axis):
    return lax.dynamic_index_in_dim(block, index, axis, keepdims=False)


def put(whole, block, index, axis):
    return lax.dynamic_update_index_in_dim(whole, block, index, axis)


def in_order(found, index):
    low, high = index % 2 == 1, index // 2 == 1
    found = [jnp.where(low, found[k ^ 1], found[k]) for k in range(PLANE)]
    return [jnp.where(high, found[k ^ 2], found[k]) for k in range(PLANE)]


def plane_gather_first(own):
    return own, to_partner(own, 1), to_partner(own, 2)


def plane_gather_second(state):
    own, from_x, from_y = state
    mine = lax.axis_index("j")
    streams, rows, width = own.shape
    half = streams // 2
    first = to_partner(from_x[:half], 2)
    second = to_partner(from_y[half:], 1)
    whole = jnp.zeros((streams, PLANE, rows, width), own.dtype)
    whole = put(whole, own, mine, 1)
    whole = put(whole, from_x, mine ^ 1, 1)
    whole = put(whole, from_y, mine ^ 2, 1)
    whole = put(whole, jnp.concatenate([first, second], axis=0), mine ^ 3, 1)
    return whole.reshape(streams, PLANE * rows, width)


def plane_gather(own):
    return plane_gather_second(plane_gather_first(own))


def plane_sum_first(part, streams):
    mine = lax.axis_index("j")
    part = part.astype(BF16).reshape(streams, PLANE, -1, part.shape[-1])
    far = at(part, mine ^ 3, 1)
    half = streams // 2
    return part, to_partner(far[:half], 1), to_partner(far[half:], 2)


def plane_sum_second(state):
    part, via_x, via_y = state
    mine = lax.axis_index("j")
    half = via_x.shape[0]
    for_x = at(part, mine ^ 1, 1)
    for_y = at(part, mine ^ 2, 1)
    for_x = jnp.concatenate(
        [for_x[:half], (for_x[half:].astype(F32) + via_y.astype(F32)).astype(BF16)], axis=0
    )
    for_y = jnp.concatenate(
        [(for_y[:half].astype(F32) + via_x.astype(F32)).astype(BF16), for_y[half:]], axis=0
    )
    from_x = to_partner(for_x, 1)
    from_y = to_partner(for_y, 2)
    own = at(part, mine, 1)
    return own.astype(F32) + from_x.astype(F32) + from_y.astype(F32)


def plane_sum(part, streams):
    return plane_sum_second(plane_sum_first(part, streams))


def plane_swap(blocks):
    mine = lax.axis_index("j")
    found = [at(blocks, mine, 0)]
    found += [to_partner(at(blocks, mine ^ bit, 0), bit) for bit in (1, 2, 3)]
    return in_order(found, mine)


def to_chips(weight):
    rows, columns = weight.shape
    blocks = weight.reshape(rows, PLANE, columns // PLANE)
    return jnp.moveaxis(blocks, 1, 0)


def to_core(block):
    return lax.ppermute(block, "c", [(0, 1), (1, 0)])


def along_z(block):
    own = lax.all_gather(block, "z", axis=0, tiled=True)
    return own, to_core(own)


def both_cores(own, other):
    return (own.astype(F32) + to_core(other).astype(F32)).astype(BF16)


def sum_along_z(total):
    return lax.psum_scatter(total, "z", scatter_dimension=0, tiled=True)


def sent_along_z(total):
    size, mine = lax.axis_size("z"), lax.axis_index("z")
    rows = total.reshape(size, -1, total.shape[1])
    result = at(rows, mine, 0).astype(F32)
    for step in range(1, size):
        route = [(i, (i + step) % size) for i in range(size)]
        result += lax.ppermute(at(rows, (mine + step) % size, 0), "z", route).astype(F32)
    return result


def to_owners(summed):
    return plane_swap(summed.reshape(PLANE, -1, summed.shape[1]))


def z_gather(block):
    size, mine = lax.axis_size("z"), lax.axis_index("z")
    whole = jnp.zeros((size, *block.shape), block.dtype)
    whole = put(whole, block, mine, 0)
    for step in range(1, size):
        got = lax.ppermute(block, "z", [(i, (i + step) % size) for i in range(size)])
        whole = put(whole, got, (mine - step) % size, 0)
    return whole


def sum_of_chip_plane(array):
    for axis, pairs in (
        ("c", [(0, 1), (1, 0)]),
        ("j", [(i, i ^ 1) for i in range(PLANE)]),
        ("j", [(i, i ^ 2) for i in range(PLANE)]),
    ):
        array = array + lax.ppermute(array, axis, pairs)
    return array


def with_other_core(array, dim):
    core = lax.axis_index("c")
    count = array.shape[0] // 2
    mine = lax.dynamic_slice_in_dim(array, core * count, count, 0)
    other = lax.dynamic_slice_in_dim(array, (1 - core) * count, count, 0)
    return jnp.concatenate([mine, to_core(other)], axis=dim)


def all_streams(own):
    core = lax.axis_index("c")
    other = to_core(own)
    count = own.shape[0]
    whole = jnp.zeros((2 * count, *own.shape[1:]), own.dtype)
    whole = lax.dynamic_update_slice_in_dim(whole, own, core * count, 0)
    return lax.dynamic_update_slice_in_dim(whole, other, (1 - core) * count, 0)


def shifted(block, distance):
    size = lax.axis_size("z")
    return lax.ppermute(
        block, "z", [(i - distance, i) for i in range(size) if 0 <= i - distance < size]
    )


def entering(keep, state, backward):
    size, mine = lax.axis_size("z"), lax.axis_index("z")
    pair = jnp.stack([keep, state])
    result = jnp.zeros_like(state)
    for distance in range(size - 1, 0, -1):
        got = shifted(pair, -distance if backward else distance)
        there = mine + distance < size if backward else mine >= distance
        result = jnp.where(there, got[0] * result + got[1], result)
    return result


def scan_kernel(backward, keep_ref, add_ref, product_ref, state_ref):
    streams, rows, width = keep_ref.shape
    steps = rows // SEGMENTS
    for s in range(streams):

        def step(number, carry):
            product, state = carry
            place = steps - 1 - number if backward else number
            at_once = pl.ds(place, SEGMENTS, stride=steps)
            keep = keep_ref[s, at_once, :]
            state = keep * state + add_ref[s, at_once, :]
            product = keep * product
            product_ref[s, at_once, :] = product
            state_ref[s, at_once, :] = state
            return product, state

        product, state = lax.fori_loop(
            0,
            steps,
            step,
            (jnp.ones((SEGMENTS, width), F32), jnp.zeros((SEGMENTS, width), F32)),
            unroll=8,
        )
        product_in = jnp.ones((1, width), F32)
        state_in = jnp.zeros((1, width), F32)
        order = range(SEGMENTS - 1, -1, -1) if backward else range(SEGMENTS)
        for k in order:
            here = pl.ds(k * steps, steps)
            local = product_ref[s, here, :]
            state_ref[s, here, :] = state_ref[s, here, :] + local * state_in
            product_ref[s, here, :] = local * product_in
            state_in = product[k : k + 1] * state_in + state[k : k + 1]
            product_in = product[k : k + 1] * product_in


def local_scan(keep, add, backward):
    streams, rows, width = keep.shape
    block = pl.BlockSpec((streams, rows, 128), lambda i: (0, 0, i))
    return pl.pallas_call(
        partial(scan_kernel, backward),
        grid=(width // 128,),
        in_specs=[block, block],
        out_specs=[block, block],
        out_shape=[jax.ShapeDtypeStruct(keep.shape, F32)] * 2,
        compiler_params=pltpu.CompilerParams(vmem_limit_bytes=32 * 1024 * 1024),
        cost_estimate=pl.CostEstimate(
            flops=8 * streams * rows * width,
            bytes_accessed=16 * streams * rows * width,
            transcendentals=0,
        ),
    )(keep, add)


def rms_norm(values, norm_gain):
    factor = lax.rsqrt(jnp.mean(values * values, axis=-1, keepdims=True) + EPSILON)
    return values * factor * norm_gain


def gate_math(pre_rate, pre_entry, lam_param, conv_value):
    rate_gate = jax.nn.sigmoid(pre_rate)
    entry_gate = jax.nn.sigmoid(pre_entry)
    log_decay = -8.0 * rate_gate * jax.nn.softplus(lam_param)
    retain = jnp.exp(log_decay)
    factor = jnp.sqrt(-jnp.expm1(2.0 * log_decay))
    return (retain, factor * entry_gate * conv_value)


def mlp_kernel(
    in_ref, down_ref, gate_w, up_w, narrow_w, act_ref, both_ref, second_ref, out_ref, *totals
):
    half, tile = pl.program_id(1), pl.program_id(2)
    first = (half == 0) & (tile == 0)
    last = (half == pl.num_programs(1) - 1) & (tile == pl.num_programs(2) - 1)
    second_total, out_total = totals
    wide = gate_w.shape[2]
    hidden = wide * pl.num_programs(2)

    def times(left, right, left_dim, right_dim):
        return dot(left, right, left_dim, right_dim)

    rows = in_ref[0]
    gate = times(rows, gate_w[0], 1, 0)
    up = times(rows, up_w[0], 1, 0)
    d_act = times(down_ref[0], narrow_w[0], 1, 0)
    scale = 0.7978845608028654
    square = gate * gate
    bent = jnp.tanh(scale * (gate + 0.044715 * square * gate))
    gelu = 0.5 * gate * (1.0 + bent)
    slope = 0.5 * (1.0 + bent) + (0.5 * scale) * gate * (1.0 - bent * bent) * (
        1.0 + 0.134145 * square
    )
    act = (gelu * up).astype(BF16)
    d_gate = (d_act * up * slope).astype(BF16)
    d_up = (d_act * gelu).astype(BF16)
    act_ref[0] = act
    place = pl.multiple_of(tile * wide, wide)
    both_ref[0, :, pl.ds(place, wide)] = d_gate
    both_ref[0, :, pl.ds(pl.multiple_of(hidden + place, wide), wide)] = d_up
    second = times(d_gate, gate_w[0], 1, 1) + times(d_up, up_w[0], 1, 1)
    out = times(act, narrow_w[0], 1, 1)

    @pl.when(first)
    def _():
        second_total[...] = second
        out_total[...] = out

    @pl.when(jnp.logical_not(first))
    def _():
        second_total[...] += second
        out_total[...] += out

    @pl.when(last)
    def _():
        second_ref[0] = second_total[...].astype(BF16)
        out_ref[0] = out_total[...].astype(BF16)


def mlp(second_low, d_down, weights, tiles):
    streams, rows, width = second_low.shape
    halves, _, columns = weights.shape
    hidden = columns // 3
    wide = hidden // tiles
    token_block = pl.BlockSpec((1, rows, width), lambda s, h, t: (s, 0, 0))
    weight_blocks = [
        pl.BlockSpec((1, width, wide), lambda s, h, t, k=k: (h, 0, k * tiles + t)) for k in range(3)
    ]
    return pl.pallas_call(
        mlp_kernel,
        grid=(streams, halves, tiles),
        in_specs=[token_block, token_block, *weight_blocks],
        out_specs=[
            pl.BlockSpec((1, rows, wide), lambda s, h, t: (h, s, t)),
            pl.BlockSpec((1, rows, 2 * hidden), lambda s, h, t: (h, s, 0)),
            token_block,
            token_block,
        ],
        out_shape=[
            jax.ShapeDtypeStruct((halves, streams * rows, hidden), BF16),
            jax.ShapeDtypeStruct((halves, streams * rows, 2 * hidden), BF16),
            jax.ShapeDtypeStruct(second_low.shape, BF16),
            jax.ShapeDtypeStruct(second_low.shape, BF16),
        ],
        scratch_shapes=[pltpu.VMEM((rows, width), F32), pltpu.VMEM((rows, width), F32)],
        compiler_params=pltpu.CompilerParams(
            vmem_limit_bytes=60 * 1024 * 1024,
            dimension_semantics=("arbitrary", "arbitrary", "arbitrary"),
        ),
        cost_estimate=pl.CostEstimate(
            flops=12 * streams * rows * width * hidden * halves,
            bytes_accessed=40 * 1024 * 1024,
            transcendentals=streams * rows * hidden * halves,
        ),
    )(second_low, d_down, weights, weights, weights)


def convolve(extended, conv_taps, conv_bias, fill_values, insides):
    n_rows = extended.shape[1] - 3
    result = conv_bias + conv_taps[:, 0] * extended[:, 3:]
    for offset in (1, 2, 3):
        window = extended[:, 3 - offset : 3 - offset + n_rows]
        result = result + conv_taps[:, offset] * jnp.where(
            insides[offset - 1], window, fill_values[offset - 1]
        )
    return result


def shards(
    inputs,
    doc_spans,
    doc_lengths,
    state_in,
    conv_in,
    norm_gains,
    w_x,
    w_g,
    rec_params,
    gate_weights,
    w_o,
    w_gate,
    w_up,
    w_down,
    cotangent,
):
    all_streams_count, own_rows, model_width = inputs.shape
    halves = lax.axis_size("c")
    z_size = lax.axis_size("z")
    z_index, j_index, core = lax.axis_index("z"), lax.axis_index("j"), lax.axis_index("c")
    n_streams = all_streams_count // halves
    n_rows = own_rows * PLANE
    tokens = n_streams * n_rows
    own_tokens = n_streams * own_rows
    weight_rows = w_x.shape[0]
    half_width = w_x.shape[1]
    part_width = half_width // PLANE
    rec_width = part_width * halves
    heads_here = rec_width // HEAD_DIM
    ff_part = w_gate.shape[1] // PLANE

    first_stream = core * n_streams

    def own_streams(array):
        return lax.dynamic_slice_in_dim(array, first_stream, n_streams, 0)

    spans = own_streams(doc_spans)
    lengths = own_streams(doc_lengths)
    own_in = own_streams(inputs)
    own_cot = own_streams(cotangent)
    small_rows = rec_params.shape[1]
    small = jnp.concatenate([rec_params[0], gate_weights[0]], axis=1)
    small_width = small.shape[1]
    gain_width = norm_gains.shape[1]
    tails = jnp.pad(norm_gains, ((0, 0), (0, small_width - gain_width)))
    small = jnp.concatenate([small, tails], axis=0)

    first_blocks = jnp.concatenate([to_chips(w_x), to_chips(w_g), to_chips(w_o.T)], axis=2)
    first_rows = jnp.concatenate(plane_swap(first_blocks), axis=0)
    small = z_gather(small)
    later = (w_gate, w_up, w_down)
    first_rows, own_in, small, later = lax.optimization_barrier((first_rows, own_in, small, later))
    gain_rows = jnp.broadcast_to(
        small[:, small_rows:].reshape(1, 2 * z_size, small_width),
        (PLANE, 2 * z_size, small_width),
    )
    small_blocks = small[:, :small_rows].reshape(PLANE, -1, small_width)
    small = jnp.stack(plane_swap(jnp.concatenate([small_blocks, gain_rows], axis=1)))
    in_state, later = lax.optimization_barrier((plane_gather_first(own_in), later))
    whole_in = plane_gather_second(in_state)
    gains_all = small[:, part_width // PLANE :, :gain_width].reshape(PLANE, z_size, 2, gain_width)
    gains_all = jnp.moveaxis(gains_all, (0, 1, 2), (2, 1, 0))
    gains_all = gains_all.reshape(2, model_width).astype(F32)
    small = small[:, : part_width // PLANE].reshape(PLANE, -1, small_rows, small_width)
    small = jnp.moveaxis(small, 0, 1).reshape(part_width, small_width)
    small = jnp.concatenate([small, to_core(small)], axis=0)
    params_all = small[:, :8].astype(F32)
    head = jnp.arange(rec_width, dtype=jnp.int32) // HEAD_DIM
    gates_all = jnp.concatenate(
        [
            jnp.where(
                head[:, None] == head[None, :],
                jnp.tile(small[:, start : start + HEAD_DIM], (1, heads_here)),
                0.0,
            ).astype(BF16)
            for start in (8, 8 + HEAD_DIM)
        ],
        axis=1,
    )

    later_blocks = jnp.concatenate(
        [to_chips(later[0]), to_chips(later[1]), to_chips(later[2].T)], axis=2
    )
    later_rows = jnp.concatenate(plane_swap(later_blocks), axis=0)
    own_cot, later_rows = lax.optimization_barrier((own_cot, later_rows))

    def live_at(position):
        second_start = spans[:, 0:1]
        doc_id = (position[None, :] >= second_start).astype(jnp.int32)
        doc_start = doc_id * second_start
        doc_stop = doc_start + jnp.where(doc_id == 1, lengths[:, 1:2], lengths[:, 0:1])
        live = (position[None, :] < doc_stop).astype(F32)
        return doc_id, doc_start, live

    own_first = (z_index * PLANE + j_index) * own_rows
    own_live = live_at(own_first + jnp.arange(own_rows, dtype=jnp.int32))[2]
    own_live = own_live.reshape(own_tokens, 1)
    position = z_index * n_rows + jnp.arange(n_rows, dtype=jnp.int32)
    doc_id, doc_start, _ = live_at(position)

    d_out = own_cot.reshape(own_tokens, model_width).astype(F32)
    own_down = (d_out * own_live).astype(BF16).reshape(n_streams, own_rows, model_width)
    down_state = plane_gather_first(own_down)

    flat_in = own_in.reshape(own_tokens, model_width).astype(F32)
    _, norm_one_back = jax.vjp(rms_norm, flat_in, gains_all[0])
    normed_low = rms_norm(
        whole_in.reshape(tokens, model_width).astype(F32), gains_all[0]
    ).astype(BF16)
    first_own, normed_low, later_rows = lax.optimization_barrier(
        (lax.all_gather(first_rows, "z", axis=0, tiled=True), normed_low, later_rows)
    )
    w_later = lax.all_gather(later_rows, ("c", "z"), axis=0)
    first_other, down_state = lax.optimization_barrier((to_core(first_own), down_state))
    w_first = (first_own, first_other)
    w_rec = jnp.concatenate(
        [w[:, p * part_width : (p + 1) * part_width] for p in (0, 1) for w in w_first], axis=1
    )
    w_back = jnp.concatenate([w[:, 2 * part_width :] for w in w_first], axis=1)
    projected = dot(normed_low, w_rec, 1, 0)
    source_rows = projected[:, :rec_width].astype(BF16).reshape(n_streams, n_rows, rec_width)
    branch, branch_back = jax.vjp(jax.nn.gelu, projected[:, rec_width:])
    rim_rows = shifted(source_rows[:, n_rows - 3 :], 1)
    extended = jnp.concatenate([rim_rows, source_rows], axis=1).astype(F32)

    conv_here = with_other_core(
        lax.dynamic_slice_in_dim(conv_in, j_index * part_width, part_width, 3), 3
    )
    state_here = with_other_core(
        lax.dynamic_slice_in_dim(state_in, j_index * part_width, part_width, 2), 2
    )
    slot_range = jnp.arange(3, dtype=jnp.int32)
    doc_range = jnp.arange(2, dtype=jnp.int32)
    fill_values = []
    insides = []
    for offset in (1, 2, 3):
        earlier_pos = position[None, :] - offset
        insides.append((earlier_pos >= doc_start)[..., None])
        slot_pick = (doc_id[..., None, None] == doc_range[:, None]) & (
            (3 + earlier_pos - doc_start)[..., None, None] == slot_range
        )
        fill_values.append(
            jnp.einsum(
                "btds,bdsc->btc",
                slot_pick.astype(BF16),
                conv_here,
                preferred_element_type=F32,
            )
        )
    conv_value, conv_back = jax.vjp(
        partial(convolve, fill_values=fill_values, insides=insides),
        extended,
        params_all[:, 0:4],
        params_all[:, 4],
    )
    conv_flat = conv_value.reshape(tokens, rec_width)
    conv_low = conv_flat.astype(BF16)
    gate_mixed = dot(conv_low, gates_all, 1, 0)
    pre_rate = gate_mixed[:, :rec_width] + params_all[:, 5]
    pre_entry = gate_mixed[:, rec_width:] + params_all[:, 6]
    (retain, drive_term), gate_back = jax.vjp(
        gate_math, pre_rate, pre_entry, params_all[:, 7], conv_flat
    )
    reset_rows = (position[None, :] == doc_start)[..., None]
    carried = jnp.where((doc_id == 1)[..., None], state_here[:, None, 1], state_here[:, None, 0])
    retain_rows = retain.reshape(n_streams, n_rows, rec_width)
    retain_eff = jnp.where(reset_rows, 0.0, retain_rows)
    drive_eff = drive_term.reshape(n_streams, n_rows, rec_width) + jnp.where(
        reset_rows, retain_rows * carried, 0.0
    )
    local_keep, local_state = local_scan(retain_eff, drive_eff, False)
    state_before = entering(local_keep[:, -1], local_state[:, -1], False)
    states = local_state + local_keep * state_before[:, None]

    starts_doc = jnp.concatenate([jnp.zeros_like(spans[:, :1]), spans[:, :1]], axis=1)
    stops_doc = starts_doc + lengths
    is_last = position[None, :, None] == (stops_doc - 1)[:, None, :]
    final_part = jnp.sum(jnp.where(is_last[..., None], states[:, :, None, :], 0.0), axis=1)
    tail_pos = stops_doc[..., None] - 3 + slot_range
    from_rows = (position[None, :, None, None] == tail_pos[:, None]) & (
        tail_pos >= starts_doc[..., None]
    )[:, None]
    conv_part = jnp.einsum(
        "btdj,btc->bdjc", from_rows.astype(BF16), source_rows, preferred_element_type=F32
    )
    from_state = (
        (tail_pos < starts_doc[..., None])[..., None]
        & ((lengths[..., None] + slot_range)[..., None] == slot_range)
        & (z_index == 0)
    )
    conv_part = conv_part + jnp.einsum(
        "bdjs,bdsc->bdjc", from_state.astype(BF16), conv_here, preferred_element_type=F32
    )
    state_high = lax.reduce_precision(final_part, exponent_bits=8, mantissa_bits=7)
    finals = jnp.stack([state_high, final_part - state_high], axis=2)
    finals = jnp.concatenate([finals, conv_part], axis=2).reshape(-1, rec_width)
    columns = finals.shape[0]
    finals = lax.dynamic_update_slice_in_dim(
        jnp.zeros((rec_width, halves * columns), F32), finals.T, core * columns, 1
    )
    dp_index = z_index * PLANE + j_index

    states_flat = states.reshape(tokens, rec_width)
    mixed_rows = (states_flat * branch).astype(BF16)
    mixed_rows, d_down = lax.optimization_barrier((mixed_rows, plane_gather_second(down_state)))
    rec_part = dot(mixed_rows, w_back, 1, 1)
    rec_total = plane_sum(rec_part, n_streams).reshape(own_tokens, model_width)
    hidden_one = flat_in + own_live * rec_total
    normed_two, norm_two_back = jax.vjp(rms_norm, hidden_one, gains_all[1])
    own_second = normed_two.astype(BF16).reshape(n_streams, own_rows, model_width)
    second_low, w_later = lax.optimization_barrier((plane_gather(own_second), w_later))
    w_later = w_later.reshape(halves, model_width, 3 * ff_part)
    acts, d_both, second_part, down_part = mlp(second_low, d_down, w_later, 1)
    second_low = second_low.reshape(tokens, model_width)
    d_down = d_down.reshape(tokens, model_width)

    def mine_and_other(array):
        return at(array, core, 0), at(array, 1 - core, 0)

    g_narrow = [dot(d_down, act, 0, 0).astype(BF16) for act in mine_and_other(acts)]
    g_wide = [dot(second_low, d, 0, 0).astype(BF16) for d in mine_and_other(d_both)]
    sum_narrow = sum_along_z(both_cores(*g_narrow))

    second_total = plane_sum(second_part, n_streams).reshape(own_tokens, model_width)
    d_hidden_norm, g_gain_two = norm_two_back(second_total)
    d_hidden = d_out + d_hidden_norm
    own_rec = (d_hidden * own_live).astype(BF16).reshape(n_streams, own_rows, model_width)
    d_rec = plane_gather(own_rec).reshape(tokens, model_width)
    d_rec, sum_wide, sum_narrow = lax.optimization_barrier(
        (d_rec, both_cores(*g_wide), sum_narrow)
    )
    sum_wide = sum_along_z(sum_wide)
    d_mixed = dot(d_rec, w_back, 1, 0)
    d_mixed, down_part = lax.optimization_barrier((d_mixed, down_part))
    mlp_sum = plane_sum_first(down_part, n_streams)
    g_back = dot(d_rec, mixed_rows, 0, 0).astype(BF16)

    grad_state = (d_mixed * branch).reshape(n_streams, n_rows, rec_width)
    branch_low = branch_back(d_mixed * states_flat)[0].astype(BF16)
    next_keep = jnp.concatenate([retain_eff[:, 1:], jnp.ones_like(retain_eff[:, :1])], axis=1)
    later_keep, later_sum = local_scan(next_keep, grad_state, True)
    carried_grad = entering(
        retain_eff[:, 0] * later_keep[:, 0], retain_eff[:, 0] * later_sum[:, 0], True
    )
    carried_grad, mlp_sum = lax.optimization_barrier((carried_grad, mlp_sum))
    mlp_sum = plane_sum_second(mlp_sum)
    out_narrow = to_owners(sum_narrow)
    adjoint = later_sum + later_keep * carried_grad[:, None]
    state_prev = jnp.concatenate([state_before[:, None], states[:, :-1]], axis=1)
    state_prev = jnp.where(reset_rows, carried, state_prev)
    d_retain = (adjoint * state_prev).reshape(tokens, rec_width)
    d_rate, d_entry, g_lam, d_conv_direct = gate_back(
        (d_retain, adjoint.reshape(tokens, rec_width))
    )
    rate_low = d_rate.astype(BF16)
    entry_low = d_entry.astype(BF16)
    grad_gates = jnp.concatenate([rate_low, entry_low], axis=1)
    d_conv_gates = dot(grad_gates, gates_all, 1, 1)
    d_conv = (d_conv_direct + d_conv_gates).reshape(n_streams, n_rows, rec_width)
    d_extended, g_taps, g_conv_bias = conv_back(d_conv)
    rim_grad = shifted(d_extended[:, :3].astype(BF16), -1).astype(F32)
    d_source = jnp.concatenate([d_extended[:, 3:n_rows], d_extended[:, n_rows:] + rim_grad], axis=1)
    d_projected = jnp.concatenate(
        [d_source.reshape(tokens, rec_width).astype(BF16), branch_low], axis=1
    )
    d_projected, sum_wide, mlp_total, out_narrow = lax.optimization_barrier(
        (d_projected, sum_wide, mlp_sum, out_narrow)
    )
    mlp_total = mlp_total.reshape(own_tokens, model_width)
    out_flat = (hidden_one + own_live * mlp_total).astype(BF16)
    output = all_streams(out_flat.reshape(n_streams, own_rows, model_width))

    g_rec = dot(normed_low, d_projected, 0, 0).astype(BF16)
    mine, other = (
        jnp.concatenate(
            [
                g[:, start + h * part_width : start + (h + 1) * part_width]
                for g, start in ((g_rec, 0), (g_rec, rec_width), (g_back, 0))
            ],
            axis=1,
        )
        for h in range(halves)
    )
    sum_first = both_cores(mine, other)
    sum_first, d_projected, grad_gates = lax.optimization_barrier(
        (sum_first, d_projected, grad_gates)
    )
    sum_first = sum_along_z(sum_first)
    first_part = dot(d_projected, w_rec, 1, 1)
    whole_flat = whole_in.reshape(tokens, model_width).astype(F32)
    whole_factor = lax.rsqrt(jnp.mean(whole_flat * whole_flat, axis=-1, keepdims=True) + EPSILON)
    g_gain_one = jnp.sum(first_part * whole_flat * whole_factor, axis=0)
    g_gains = sum_of_chip_plane(jnp.stack([g_gain_one, g_gain_two]))
    g_gates = dot(conv_low, grad_gates, 0, 0)
    g_gates = jnp.concatenate(
        [
            jnp.concatenate(
                [
                    g_gates[
                        h * HEAD_DIM : (h + 1) * HEAD_DIM,
                        start + h * HEAD_DIM : start + (h + 1) * HEAD_DIM,
                    ]
                    for start in (0, rec_width)
                ],
                axis=1,
            )
            for h in range(heads_here)
        ],
        axis=0,
    )
    g_small = jnp.concatenate(
        [
            g_taps,
            g_conv_bias[:, None],
            jnp.sum(rate_low.astype(F32), axis=0)[:, None],
            jnp.sum(entry_low.astype(F32), axis=0)[:, None],
            g_lam[:, None],
            g_gates,
            finals,
        ],
        axis=1,
    ).astype(BF16)
    sum_small = both_cores(g_small[:part_width], g_small[part_width:])
    sum_first, sum_small, g_gains = lax.optimization_barrier((sum_first, sum_small, g_gains))
    g_gains = jnp.sum(z_gather(g_gains), axis=0)
    out_first = to_owners(sum_first)
    g_small = sent_along_z(sum_small)
    route = [(z * PLANE + j, j * z_size + z) for z in range(z_size) for j in range(PLANE)]
    g_small = lax.ppermute(g_small.astype(BF16), ("z", "j"), route).astype(F32)
    g_params = g_small[None, :, :8]
    g_gates = g_small[None, :, 8 : 8 + 2 * HEAD_DIM]
    finals = g_small[:, 8 + 2 * HEAD_DIM :].T.reshape(all_streams_count, 2, 5, -1)
    state_block = (finals[:, :, 0] + finals[:, :, 1])[:, :, None]
    conv_block = finals[:, :, 2:].astype(BF16)[:, :, :, None]

    first_total, sum_wide = lax.optimization_barrier((plane_sum(first_part, n_streams), sum_wide))
    first_total = first_total.reshape(own_tokens, model_width)
    out_wide = to_owners(sum_wide)
    d_input_norm = norm_one_back(first_total)[0]
    input_grad = all_streams(
        (d_hidden + d_input_norm).astype(BF16).reshape(n_streams, own_rows, model_width)
    )
    g_gains = lax.dynamic_slice_in_dim(g_gains, dp_index * gain_width, gain_width, 1)

    def flat(blocks, start, stop):
        return jnp.concatenate([b[:, start:stop] for b in blocks], axis=1).astype(F32)

    return (
        output,
        input_grad,
        state_block,
        conv_block,
        g_gains,
        flat(out_first, 0, part_width),
        flat(out_first, part_width, 2 * part_width),
        g_params,
        g_gates,
        flat(out_first, 2 * part_width, 3 * part_width).T,
        flat(out_wide, 0, ff_part),
        flat(out_wide, ff_part, 2 * ff_part),
        flat(out_narrow, 0, ff_part).T,
    )


def solution(mesh):
    devices = mesh.devices.reshape(-1, PLANE, mesh.shape["mp"])
    planes = Mesh(devices, ("z", "j", "c"))
    dp, mp = ("z", "j"), "c"
    return jax.shard_map(
        shards,
        mesh=planes,
        in_specs=(
            P(None, dp, None),
            P(),
            P(),
            P(None, None, mp),
            P(None, None, None, mp),
            P(None, dp),
            P(dp, mp),
            P(dp, mp),
            P(mp, dp, None),
            P(mp, dp, None),
            P(mp, dp),
            P(dp, mp),
            P(dp, mp),
            P(mp, dp),
            P(None, dp, None),
        ),
        out_specs=(
            P(None, dp, None),
            P(None, dp, None),
            P(None, None, mp, dp),
            P(None, None, None, mp, dp),
            P(None, dp),
            P(dp, mp),
            P(dp, mp),
            P(mp, dp, None),
            P(mp, dp, None),
            P(mp, dp),
            P(dp, mp),
            P(dp, mp),
            P(mp, dp),
        ),
        check_vma=False,
    )
```
